256 devices in a mesh: group: 2 (over x_lo), row: 8 (over z), col: 16 (over x_hi, y, core).
Axes of the slice: x: 4 (x_hi: 2, x_lo: 2; x = x_hi * 2 + x_lo), y: 4, z: 8, core: 2. Of those that a mesh axis runs over, the one named last changes fastest.
Arguments:
- pair: bfloat16 [512, 512, 128], P(('group', 'row'), 'col'), may hold values from -6 to 6
- pair_mask: int32 [512, 512], P(('group', 'row'), 'col'), may hold values from 0 to 1, as said below
- tri_proj: bfloat16 [2, 128, 512], replicated, may hold values from -0.5 to 0.5
- tri_gate: bfloat16 [2, 128, 128], replicated, may hold values from -0.5 to 0.5
- triangle_output_weight: bfloat16 [2, 128, 128], replicated, may hold values from -0.5 to 0.5
- tri_gains: float32 [2, 2, 128], replicated, may hold values from 0.1 to 1.9
- pair_bias_gain: float32 [128], replicated, may hold values from 0.1 to 1.9
- bias_weight: bfloat16 [128, 16], replicated, as said below
- tokens: bfloat16 [64, 512, 768], P(('group', 'row')), may hold values from -6 to 6
- att_gain: float32 [768], replicated, may hold values from 0.3 to 3
- att_proj: bfloat16 [4, 768, 768], P(None, None, 'col'), may hold values from -0.21875 to 0.21875
- att_out: bfloat16 [768, 768], replicated, may hold values from -0.21875 to 0.21875
- tr_gain: float32 [768], replicated, may hold values from 0.1 to 1.9
- tr_up: bfloat16 [768, 3072], replicated, may hold values from -0.21875 to 0.21875
- tr_down: bfloat16 [1536, 768], replicated, may hold values from -0.15625 to 0.15625
Outputs:
- pair_out: float32 [512, 512, 128], P(('group', 'row'), 'col')
- tokens_out: float32 [64, 512, 768], P(('group', 'row'), 'col')
The draws below stay inside these ranges and needn't reach their ends.
Inputs may be any that keep to these rules, and one draw needn't show every extreme that they name: `bias_weight`: a projection of order one to some tens. `pair_mask`: tokens form chains of consecutive tokens; pairs within a chain are mostly valid, pairs across chains rarely.
All inputs are finite; a program needn't handle non-finite values.
Results may differ from the reference program's by a relative error of at most 0.035.
The reference program's roundings to bfloat16 on the way count: a program that leaves them out, or rounds other values in their place, can miss the bound.
Values may be sent and summed in bfloat16 or wider, within the bound.
A program may use at most 128 MiB of HBM per device.

```python
import math
import jax
import jax.numpy as jnp
from jax import lax

C = 128
D = 768
HEADS = 16
FFN = 1536
N = 512
SAMPLES = 64


def draw_bias_weight(key, part):
    key = jax.random.fold_in(key, 7)
    base = jax.random.normal(jax.random.fold_in(key, 1), (C, HEADS), jnp.float32)
    return (base * 3.0 / jnp.sqrt(jnp.float32(C))).astype(jnp.bfloat16)


def draw_pair_mask(key, part):
    key = jax.random.fold_in(key, 11)
    span = N // 16
    offset = jax.random.randint(jax.random.fold_in(key, 1), (), 0, span)
    chain_ids = (jnp.arange(N, dtype=jnp.int32) + offset) // span
    same = chain_ids[:, None] == chain_ids[None, :]
    rolled = jax.random.randint(jax.random.fold_in(key, 2), (N, N), 0, 32)
    return jnp.where(same, rolled < 28, rolled < 1).astype(jnp.int32)


def block_scale(own_key, dims, cuts, smallest, high):
    level, own = 1.0, jax.random.fold_in(own_key, 6)
    for axis_at, blocks in cuts:
        draws = jnp.exp(jax.random.uniform(jax.random.fold_in(own, axis_at), (blocks,), jnp.float32, smallest / len(cuts), high / len(cuts)))
        level = level * jnp.repeat(draws, dims[axis_at] // blocks).reshape([-1 if axis == axis_at else 1 for axis in range(len(dims))])
    return level


def noise(rng, extent, scale, most, pieces=(), kind=jnp.bfloat16):
    factor_of = block_scale(rng, extent, pieces, -0.22, 0.18) if pieces else 1.0
    values = jax.random.normal(rng, extent, jnp.float32) * scale * factor_of
    return jnp.minimum(jnp.maximum(values, -most), most).astype(kind)


def setup_inputs(seed: int = 0) -> dict:
    splits = jax.random.split(jax.random.key(seed), 16)
    pair = noise(splits[0], (N, N, C), 1.0, 6.0, ((0, 16), (1, 16)))
    pair_mask = draw_pair_mask(jax.random.fold_in(splits[15], 71), 0)
    tri_proj = noise(splits[2], (2, C, 4 * C), C ** -0.5, 0.5)
    tri_gate = noise(splits[3], (2, C, C), C ** -0.5, 0.5)
    triangle_output_weight = noise(splits[4], (2, C, C), C ** -0.5, 0.5)
    tri_gains = jnp.clip(1.0 + 0.18 * jax.random.normal(splits[5], (2, 2, C), jnp.float32), 0.1, 1.9)
    pair_bias_gain = jnp.clip(1.0 + 0.18 * jax.random.normal(splits[6], (C,), jnp.float32), 0.1, 1.9)
    bias_weight = draw_bias_weight(jax.random.fold_in(splits[15], 71), 0)
    tokens = noise(splits[8], (SAMPLES, N, D), 1.0, 6.0, ((0, 16),))
    att_gain = jnp.clip(jnp.exp(jax.random.uniform(splits[9], (D,), jnp.float32, math.log(0.3), math.log(3.0))), 0.3, 3.0)
    att_proj = noise(splits[10], (4, D, D), D ** -0.5, 0.21875, ((2, 16),))
    att_out = noise(splits[11], (D, D), D ** -0.5, 0.21875)
    tr_gain = jnp.clip(1.0 + 0.18 * jax.random.normal(splits[12], (D,), jnp.float32), 0.1, 1.9)
    tr_up = noise(splits[13], (D, 2 * FFN), D ** -0.5, 0.21875)
    tr_down = noise(splits[14], (FFN, D), FFN ** -0.5, 0.15625)
    return dict(pair=pair, pair_mask=pair_mask, tri_proj=tri_proj, tri_gate=tri_gate, triangle_output_weight=triangle_output_weight, tri_gains=tri_gains, pair_bias_gain=pair_bias_gain, bias_weight=bias_weight, tokens=tokens, att_gain=att_gain, att_proj=att_proj, att_out=att_out, tr_gain=tr_gain, tr_up=tr_up, tr_down=tr_down)


EPS = 1e-05

def normalize(value, gain):
    mean = lax.optimization_barrier(jnp.mean(value, axis=-1, keepdims=True))
    mean_removed = value - mean
    variance = lax.optimization_barrier(jnp.mean(mean_removed * mean_removed, axis=-1, keepdims=True))
    return mean_removed * lax.rsqrt(variance + EPS) * gain

def edges(state, mask, proj_weight, gate_weight, gain_in):
    normed = normalize(state.astype(jnp.float32), gain_in).astype(jnp.bfloat16)
    proj = jnp.dot(normed, proj_weight, preferred_element_type=jnp.float32)
    width = proj.shape[-1] // 4
    keep = mask.astype(jnp.float32)[..., None]
    left = (keep * jax.nn.sigmoid(proj[..., :width]) * proj[..., width:2 * width]).astype(jnp.bfloat16)
    right = (keep * jax.nn.sigmoid(proj[..., 2 * width:3 * width]) * proj[..., 3 * width:]).astype(jnp.bfloat16)
    gate = jax.nn.sigmoid(jnp.dot(normed, gate_weight, preferred_element_type=jnp.float32))
    return (left, right, gate)

def finish(state, summed, gate, out_weight, gain_mid):
    normed = normalize(summed, gain_mid).astype(jnp.bfloat16)
    update = jnp.dot(normed, out_weight, preferred_element_type=jnp.float32)
    return state.astype(jnp.float32) + gate * update

def reference(pair, pair_mask, tri_proj, tri_gate, triangle_output_weight, tri_gains, pair_bias_gain, bias_weight, tokens, att_gain, att_proj, att_out, tr_gain, tr_up, tr_down):
    left, right, gate = edges(pair, pair_mask, tri_proj[0], tri_gate[0], tri_gains[0, 0])
    summed = jnp.einsum('ikc,jkc->ijc', left.astype(jnp.float32), right.astype(jnp.float32))
    state = finish(pair, summed, gate, triangle_output_weight[0], tri_gains[0, 1])
    left, right, gate = edges(state, pair_mask, tri_proj[1], tri_gate[1], tri_gains[1, 0])
    summed = jnp.einsum('kic,kjc->ijc', left.astype(jnp.float32), right.astype(jnp.float32))
    pair_out = finish(state, summed, gate, triangle_output_weight[1], tri_gains[1, 1])
    normed = normalize(pair_out, pair_bias_gain).astype(jnp.bfloat16)
    bias = jnp.dot(normed, bias_weight, preferred_element_type=jnp.float32).astype(jnp.bfloat16)
    head_bias = jnp.transpose(bias, (2, 0, 1)).astype(jnp.float32)
    heads = head_bias.shape[0]
    head_size = D // heads

    def one_sample(sample):
        count = sample.shape[0]
        xn = normalize(sample.astype(jnp.float32), att_gain).astype(jnp.bfloat16)
        query = jnp.dot(xn, att_proj[0], preferred_element_type=jnp.float32).astype(jnp.bfloat16)
        keyed = jnp.dot(xn, att_proj[1], preferred_element_type=jnp.float32).astype(jnp.bfloat16)
        value = jnp.dot(xn, att_proj[2], preferred_element_type=jnp.float32).astype(jnp.bfloat16)
        gating = jnp.dot(xn, att_proj[3], preferred_element_type=jnp.float32)
        query = query.astype(jnp.float32).reshape(count, heads, head_size)
        keyed = keyed.astype(jnp.float32).reshape(count, heads, head_size)
        value = value.astype(jnp.float32).reshape(count, heads, head_size)
        scores = jnp.einsum('qhe,khe->hqk', query, keyed) / jnp.sqrt(jnp.float32(head_size)) + head_bias
        weights = jax.nn.softmax(scores, axis=-1).astype(jnp.bfloat16)
        attended = jnp.einsum('hqk,khe->qhe', weights.astype(jnp.float32), value).reshape(count, D)
        attended = (attended * jax.nn.sigmoid(gating)).astype(jnp.bfloat16)
        first = sample.astype(jnp.float32) + jnp.dot(attended, att_out, preferred_element_type=jnp.float32)
        xn2 = normalize(first, tr_gain).astype(jnp.bfloat16)
        upped = jnp.dot(xn2, tr_up, preferred_element_type=jnp.float32)
        hidden = (jax.nn.silu(upped[:, :FFN]) * upped[:, FFN:]).astype(jnp.bfloat16)
        return first + jnp.dot(hidden, tr_down, preferred_element_type=jnp.float32)
    tokens_out = lax.map(one_sample, tokens)
    return (pair_out, tokens_out)
```

```python
import jax
import jax.numpy as jnp
from jax import lax
from jax.experimental import pallas as pl
from jax.experimental.pallas import tpu as pltpu
from jax.sharding import PartitionSpec as P

EPS = 1e-05
MESH = pl.DeviceIdType.MESH
F32 = jnp.float32
BF16 = jnp.bfloat16
NT = (((1,), (1,)), ((), ()))
TN = (((0,), (0,)), ((), ()))


def normalize(value, gain):
    mean = jnp.mean(value, axis=-1, keepdims=True)
    mean_removed = value - mean
    variance = jnp.mean(mean_removed * mean_removed, axis=-1, keepdims=True)
    return mean_removed * lax.rsqrt(variance + EPS) * gain


def mm(a, b, dims=(((1,), (0,)), ((), ()))):
    return lax.dot_general(a, b, dims, preferred_element_type=F32)


def swap_map(lane, inner):
    a, b, k = lane >> 7, (lane >> 5) & 3, lane & 31
    if inner:
        k = ((k & 3) << 3) + (k >> 2)
    return (b << 7) + (a << 5) + k


def swap_matrix(inner, transposed=False):
    row = lax.broadcasted_iota(jnp.int32, (512, 512), 0)
    col = lax.broadcasted_iota(jnp.int32, (512, 512), 1)
    if transposed:
        hit = row == swap_map(col, inner)
    else:
        hit = swap_map(row, inner) == col
    return jnp.where(hit, 1.0, 0.0).astype(BF16)


def remote(src, dst, send, recv, device):
    return pltpu.make_async_remote_copy(
        src_ref=src,
        dst_ref=dst,
        send_sem=send,
        recv_sem=recv,
        device_id=device,
        device_id_type=MESH,
    )


class Exchange:
    def __init__(self, n, me, device, src, dst, send, recv):
        self.n, self.me, self.device = n, me, device
        self.src, self.dst, self.send, self.recv = src, dst, send, recv

    def copy(self, d):
        peer = lax.rem(self.me + d, self.n)
        return remote(
            self.src(peer), self.dst(self.me), self.send.at[d], self.recv.at[d], self.device(peer)
        )

    def own(self):
        return pltpu.make_async_copy(self.src(self.me), self.dst(self.me), self.recv.at[0])

    def start(self):
        def body(d, carry):
            self.copy(d).start()
            return carry

        lax.fori_loop(1, self.n, body, 0)
        self.own().start()

    def wait(self):
        self.own().wait()

        def body(d, carry):
            self.copy(d).wait()
            return carry

        lax.fori_loop(1, self.n, body, 0)


def pair_kernel(
    pair_ref,
    mask_ref,
    wp_ref,
    wg_ref,
    wo_ref,
    gin_ref,
    gmid_ref,
    bgain_ref,
    bw_ref,
    out_ref,
    bias_ref,
    z_s,
    gate_s,
    flat_s,
    nrm_s,
    send_a,
    recv_a,
    send_b,
    recv_b,
    x_left,
    x_right,
    send_bt,
    recv_bt,
    send_at,
    recv_at,
    heads_s,
    recv_h,
    rows_s,
    ssem,
    rsem,
):
    group, row, col = (lax.axis_index(name) for name in ("group", "row", "col"))
    big = group * 8 + row
    quad = col // 2
    core = lax.rem(col, 2)

    def on_col(peer):
        return {"col": peer}

    def on_quad(peer):
        return {"col": peer * 2 + core}

    def on_rows(peer):
        return {"group": peer // 8, "row": lax.rem(peer, 8)}

    barrier = pltpu.get_barrier_semaphore()

    def greet_col(d, carry):
        pl.semaphore_signal(
            barrier, inc=1, device_id=on_col(lax.rem(col + d, 16)), device_id_type=MESH
        )
        return carry

    def greet_rows(d, carry):
        pl.semaphore_signal(
            barrier, inc=1, device_id=on_rows(lax.rem(big + d, 16)), device_id_type=MESH
        )
        return carry

    lax.fori_loop(1, 16, greet_col, 0)
    lax.fori_loop(1, 16, greet_rows, 0)

    swap_in = swap_matrix(True)
    swap_out = swap_matrix(True, transposed=True)

    def edges(m, state):
        for it in range(8):
            zn = normalize(state(it), gin_ref[m]).astype(BF16)
            gate_s[pl.ds(it * 128, 128), :] = jax.nn.sigmoid(mm(zn, wg_ref[m]))
            proj = mm(wp_ref[m], zn, NT)
            keep = mask_ref[it : it + 1, :]
            left = keep * jax.nn.sigmoid(proj[0:128]) * proj[128:256]
            right = keep * jax.nn.sigmoid(proj[256:384]) * proj[384:512]
            flat_s[pl.ds(it, 128, stride=16), :] = left
            flat_s[pl.ds(8 + it, 128, stride=16), :] = right
        for s in range(8):
            send_a[m, s] = flat_s[pl.ds(s * 256, 256), :].astype(BF16)

    def triangle(m):
        go_a = Exchange(
            8,
            quad,
            on_quad,
            lambda p: send_a.at[m, p],
            lambda p: recv_a.at[m, p],
            ssem.at[5 * m],
            rsem.at[5 * m],
        )
        go_a.start()
        go_a.wait()
        for hi in range(2):
            lanes = jnp.concatenate([recv_a[m, hi * 4 + lo] for lo in range(4)], axis=1)
            moved = mm(lanes, swap_in)
            parts = [moved[:, lo * 128 : (lo + 1) * 128].reshape(32, 8, 128) for lo in range(4)]
            send_b[m, :, :, hi * 128 : (hi + 1) * 128] = jnp.concatenate(parts, axis=1).astype(BF16)
        go_b = Exchange(
            16,
            big,
            on_rows,
            lambda p: send_b.at[m, pl.ds(p * 2, 2)],
            lambda p: recv_b.at[m, p // 2, lax.rem(p, 2)],
            ssem.at[5 * m + 1],
            rsem.at[5 * m + 1],
        )
        go_b.start()
        go_b.wait()
        partner = on_col(quad * 2 + 1 - core)
        cross = remote(
            recv_b.at[m, :, :, 0],
            x_left.at[m],
            ssem.at[5 * m + 2, 0],
            rsem.at[5 * m + 2, 0],
            partner,
        )
        cross.start()
        if m == 0:
            cross_right = remote(
                recv_b.at[m, :, 1 - core, 1],
                x_right,
                ssem.at[5 * m + 2, 1],
                rsem.at[5 * m + 2, 1],
                partner,
            )
            cross_right.start()
            left = recv_b[m, :, :, 0].reshape(512, 256)
            right = recv_b[m, :, core, 1].reshape(256, 256)
            total = mm(left, right, NT)
            cross.wait()
            cross_right.wait()
            total += mm(x_left[m].reshape(512, 256), x_right[...].reshape(256, 256), NT)
            send_bt[m] = total.reshape(8, 2, 32, 256).astype(BF16)
        else:
            right = recv_b[m, :, :, 1].reshape(512, 256)
            own = mm(recv_b[m, :, :, 0].reshape(512, 256), right, TN)
            send_bt[m, :, core] = own.reshape(8, 32, 256).astype(BF16)
            cross.wait()
            other = mm(x_left[m].reshape(512, 256), right, TN)
            send_bt[m, :, 1 - core] = other.reshape(8, 32, 256).astype(BF16)
        back_b = Exchange(
            16,
            big,
            on_rows,
            lambda p: send_bt.at[m, p // 2, lax.rem(p, 2)],
            lambda p: recv_bt.at[m, p],
            ssem.at[5 * m + 3],
            rsem.at[5 * m + 3],
        )
        back_b.start()
        back_b.wait()
        for hi in range(2):
            block = recv_bt[m, :, :, hi * 128 : (hi + 1) * 128].astype(F32)
            lanes = jnp.concatenate(
                [block[:, lo * 8 : (lo + 1) * 8, :].reshape(128, 128) for lo in range(4)], axis=1
            ).astype(BF16)
            moved = mm(lanes, swap_out).astype(BF16)
            for lo in range(4):
                send_at[m, hi * 4 + lo] = moved[:, lo * 128 : (lo + 1) * 128]
        back_a = Exchange(
            8,
            quad,
            on_quad,
            lambda p: send_at.at[m, p],
            lambda p: recv_at.at[m, p],
            ssem.at[5 * m + 4],
            rsem.at[5 * m + 4],
        )
        back_a.start()
        back_a.wait()
        summed = recv_at[m].astype(F32).reshape(128, 8, 128)
        mean = jnp.sum(summed, axis=0, keepdims=True) * (1.0 / 128)
        mean_removed = summed - mean
        variance = jnp.sum(mean_removed * mean_removed, axis=0, keepdims=True) * (1.0 / 128)
        nrm_s[...] = (mean_removed * lax.rsqrt(variance + EPS)).reshape(1024, 128)

    def update(m, it):
        normed = (nrm_s[pl.ds(it, 128, stride=8), :] * gmid_ref[m]).astype(BF16)
        return gate_s[pl.ds(it * 128, 128), :] * mm(normed, wo_ref[m], TN)

    def first_state(it):
        return pair_ref[pl.ds(it * 128, 128), :].astype(F32)

    def second_state(it):
        z = first_state(it) + update(0, it)
        z_s[pl.ds(it * 128, 128), :] = z
        return z

    edges(0, first_state)
    pl.semaphore_wait(barrier, 30)
    triangle(0)
    edges(1, second_state)
    triangle(1)
    for it in range(8):
        z = z_s[pl.ds(it * 128, 128), :] + update(1, it)
        out_ref[pl.ds(it * 128, 128), :] = z
        zn = normalize(z, bgain_ref[...]).astype(BF16)
        bias = mm(bw_ref[...], zn, NT).astype(BF16).astype(F32)
        heads_s[pl.ds(it, 16, stride=8), :] = bias
    to_head = Exchange(
        16,
        col,
        on_col,
        lambda p: heads_s.at[pl.ds(p * 8, 8)],
        lambda p: recv_h.at[p],
        ssem.at[10],
        rsem.at[10],
    )
    to_head.start()
    to_head.wait()
    lanes = jnp.concatenate(
        [
            jnp.concatenate([recv_h[hi * 4 + lo] for lo in range(4)], axis=1)
            for hi in range(4)
        ],
        axis=0,
    ).astype(BF16)
    moved = mm(lanes, swap_matrix(False))
    for hi in range(4):
        for lo in range(4):
            rows_s[pl.ds(hi * 32 + lo, 8, stride=4), :] = moved[
                hi * 8 : (hi + 1) * 8, lo * 128 : (lo + 1) * 128
            ]
    bias_ref[big] = jnp.concatenate(
        [rows_s[hi * 32 : (hi + 1) * 32, :] for hi in range(4)], axis=1
    ).astype(BF16)
    spread = Exchange(
        16,
        big,
        on_rows,
        lambda p: bias_ref.at[big],
        lambda p: bias_ref.at[p],
        ssem.at[11],
        rsem.at[11],
    )

    def spread_start(d, carry):
        spread.copy(d).start()
        return carry

    def spread_wait(d, carry):
        spread.copy(d).wait()
        return carry

    lax.fori_loop(1, 16, spread_start, 0)
    lax.fori_loop(1, 16, spread_wait, 0)


def pair_part(
    pair, pair_mask, tri_proj, tri_gate, triangle_output_weight, tri_gains, pair_bias_gain, bias_weight
):
    vmem = pl.BlockSpec(memory_space=pltpu.VMEM)
    pair_out, head_bias = pl.pallas_call(
        pair_kernel,
        out_shape=(
            jax.ShapeDtypeStruct((1024, 128), F32),
            jax.ShapeDtypeStruct((16, 32, 512), BF16),
        ),
        in_specs=[vmem] * 9,
        out_specs=(vmem, vmem),
        scratch_shapes=[
            pltpu.VMEM((1024, 128), F32),
            pltpu.VMEM((1024, 128), F32),
            pltpu.VMEM((2048, 128), F32),
            pltpu.VMEM((1024, 128), F32),
            pltpu.VMEM((2, 8, 256, 128), BF16),
            pltpu.VMEM((2, 8, 256, 128), BF16),
            pltpu.VMEM((2, 32, 32, 256), BF16),
            pltpu.VMEM((2, 8, 2, 2, 32, 256), BF16),
            pltpu.VMEM((2, 8, 2, 32, 256), BF16),
            pltpu.VMEM((8, 32, 256), BF16),
            pltpu.VMEM((2, 8, 2, 32, 256), BF16),
            pltpu.VMEM((2, 16, 32, 256), BF16),
            pltpu.VMEM((2, 8, 128, 128), BF16),
            pltpu.VMEM((2, 8, 128, 128), BF16),
            pltpu.VMEM((128, 128), F32),
            pltpu.VMEM((16, 8, 128), F32),
            pltpu.VMEM((128, 128), F32),
            pltpu.SemaphoreType.DMA((12, 16)),
            pltpu.SemaphoreType.DMA((12, 16)),
        ],
        compiler_params=pltpu.CompilerParams(
            collective_id=0, has_side_effects=True, vmem_limit_bytes=40 * 1024 * 1024
        ),
        cost_estimate=pl.CostEstimate(
            flops=1_500_000_000, bytes_accessed=3_000_000, transcendentals=1_500_000
        ),
    )(
        pair.reshape(1024, 128),
        pair_mask.reshape(8, 128).astype(F32),
        jnp.swapaxes(tri_proj, 1, 2),
        tri_gate,
        triangle_output_weight,
        tri_gains[:, 0:1, :],
        jnp.broadcast_to(tri_gains[:, 1, :, None], (2, 128, 128)),
        pair_bias_gain.reshape(1, 128),
        jnp.swapaxes(bias_weight, 0, 1),
    )
    return pair_out.reshape(32, 32, 128), head_bias.reshape(512, 512)


def on_device(
    pair,
    pair_mask,
    tri_proj,
    tri_gate,
    triangle_output_weight,
    tri_gains,
    pair_bias_gain,
    bias_weight,
    tokens,
    att_gain,
    att_proj,
    att_out,
    tr_gain,
    tr_up,
    tr_down,
):
    pair_out, head_bias = pair_part(
        pair,
        pair_mask,
        tri_proj,
        tri_gate,
        triangle_output_weight,
        tri_gains,
        pair_bias_gain,
        bias_weight,
    )
    samples, length, width = tokens.shape
    head_size = att_proj.shape[2]
    xn = normalize(tokens.astype(F32), att_gain).astype(BF16)
    projected = jnp.einsum("snd,fde->fsne", xn, att_proj, preferred_element_type=F32)
    query, keyed, value = (projected[i].astype(BF16) for i in range(3))
    scores = jnp.einsum("sqe,ske->sqk", query, keyed, preferred_element_type=F32)
    scores = scores / jnp.sqrt(F32(head_size)) + head_bias.astype(F32)[None]
    weights = jax.nn.softmax(scores, axis=-1).astype(BF16)
    attended = jnp.einsum("sqk,ske->sqe", weights, value, preferred_element_type=F32)
    attended = (attended * jax.nn.sigmoid(projected[3])).astype(BF16)
    attended = lax.all_to_all(attended, "col", split_axis=1, concat_axis=2, tiled=True)
    share = length // lax.axis_size("col")
    own_tokens = lax.dynamic_slice_in_dim(tokens, lax.axis_index("col") * share, share, 1)
    mixed = jnp.dot(attended, att_out, preferred_element_type=F32)
    first = own_tokens.astype(F32) + mixed
    xn2 = normalize(first, tr_gain).astype(BF16)
    upped = jnp.dot(xn2, tr_up, preferred_element_type=F32)
    hidden_width = tr_down.shape[0]
    hidden = (jax.nn.silu(upped[..., :hidden_width]) * upped[..., hidden_width:]).astype(BF16)
    tokens_out = first + jnp.dot(hidden, tr_down, preferred_element_type=F32)
    return (pair_out, tokens_out)


def solution(mesh):
    placed = (
        P(("group", "row"), "col", None),
        P(("group", "row"), "col"),
        P(),
        P(),
        P(),
        P(),
        P(),
        P(),
        P(("group", "row"), None, None),
        P(),
        P(None, None, "col"),
        P(),
        P(),
        P(),
        P(),
    )
    return jax.shard_map(
        on_device,
        mesh=mesh,
        in_specs=placed,
        out_specs=(P(("group", "row"), "col", None), P(("group", "row"), "col", None)),
        check_vma=False,
    )
```

```python
import jax
import jax.numpy as jnp
from jax import lax
from jax.experimental import pallas as pl
from jax.experimental.pallas import tpu as pltpu
from jax.sharding import PartitionSpec as P

EPS = 1e-05
MESH = pl.DeviceIdType.MESH
F32 = jnp.float32
BF16 = jnp.bfloat16
NT = (((1,), (1,)), ((), ()))
TN = (((0,), (0,)), ((), ()))


def normalize(value, gain):
    mean = jnp.mean(value, axis=-1, keepdims=True)
    mean_removed = value - mean
    variance = jnp.mean(mean_removed * mean_removed, axis=-1, keepdims=True)
    return mean_removed * lax.rsqrt(variance + EPS) * gain


def mm(a, b, dims=(((1,), (0,)), ((), ()))):
    return lax.dot_general(a, b, dims, preferred_element_type=F32)


def swap_map(lane, inner):
    a, b, k = lane >> 7, (lane >> 5) & 3, lane & 31
    if inner:
        k = ((k & 3) << 3) + (k >> 2)
    return (b << 7) + (a << 5) + k


def swap_matrix(inner, transposed=False):
    row = lax.broadcasted_iota(jnp.int32, (512, 512), 0)
    col = lax.broadcasted_iota(jnp.int32, (512, 512), 1)
    if transposed:
        hit = row == swap_map(col, inner)
    else:
        hit = swap_map(row, inner) == col
    return jnp.where(hit, 1.0, 0.0).astype(BF16)


def remote(src, dst, send, recv, device):
    return pltpu.make_async_remote_copy(
        src_ref=src,
        dst_ref=dst,
        send_sem=send,
        recv_sem=recv,
        device_id=device,
        device_id_type=MESH,
    )


class Exchange:
    def __init__(self, n, me, device, src, dst, send, recv):
        self.n, self.me, self.device = n, me, device
        self.src, self.dst, self.send, self.recv = src, dst, send, recv

    def copy(self, d):
        peer = lax.rem(self.me + d, self.n)
        return remote(
            self.src(peer), self.dst(self.me), self.send.at[d], self.recv.at[d], self.device(peer)
        )

    def own(self):
        return pltpu.make_async_copy(self.src(self.me), self.dst(self.me), self.recv.at[0])

    def start(self):
        def body(d, carry):
            self.copy(d).start()
            return carry

        lax.fori_loop(1, self.n, body, 0)
        self.own().start()

    def wait(self):
        self.own().wait()

        def body(d, carry):
            self.copy(d).wait()
            return carry

        lax.fori_loop(1, self.n, body, 0)


NAMES = (
    "pair",
    "mask",
    "wp",
    "wg",
    "wo",
    "gains",
    "bgain",
    "bw",
    "tokens",
    "again",
    "watt",
    "wout",
    "tgain",
    "wup",
    "wdown",
)


def block_kernel(*refs):
    inputs = dict(zip(NAMES, refs[:15]))
    out_ref, tok_ref = refs[15:17]
    held = dict(zip(NAMES, refs[17:32]))
    (
        z_s,
        gate_s,
        flat_s,
        nrm_s,
        send_a,
        recv_a,
        send_b,
        recv_b,
        x_left,
        x_right,
        send_bt,
        recv_bt,
        send_at,
        recv_at,
        heads_s,
        recv_h,
        rows_s,
        bias_s,
        xn_s,
        qkv_s,
        sig_s,
        scores_s,
        ot_s,
        send_o,
        recv_o,
        ssem,
        rsem,
        load_sem,
    ) = refs[32:]
    group, row, col = (lax.axis_index(name) for name in ("group", "row", "col"))
    big = group * 8 + row
    quad = col // 2
    core = lax.rem(col, 2)

    loads = {
        name: pltpu.make_async_copy(inputs[name], held[name], load_sem.at[i])
        for i, name in enumerate(NAMES)
    }
    for name in NAMES:
        loads[name].start()

    def on_col(peer):
        return {"col": peer}

    def on_quad(peer):
        return {"col": peer * 2 + core}

    def on_rows(peer):
        return {"group": peer // 8, "row": lax.rem(peer, 8)}

    barrier = pltpu.get_barrier_semaphore()

    def greet_col(d, carry):
        pl.semaphore_signal(
            barrier, inc=1, device_id=on_col(lax.rem(col + d, 16)), device_id_type=MESH
        )
        return carry

    def greet_rows(d, carry):
        pl.semaphore_signal(
            barrier, inc=1, device_id=on_rows(lax.rem(big + d, 16)), device_id_type=MESH
        )
        return carry

    lax.fori_loop(1, 16, greet_col, 0)
    lax.fori_loop(1, 16, greet_rows, 0)

    swap_in = swap_matrix(True)
    swap_out = swap_matrix(True, transposed=True)
    pair_ref = held["pair"]
    wg_ref, wo_ref = held["wg"], held["wo"]

    for name in ("pair", "mask", "wp", "wg", "wo", "gains", "bgain", "bw"):
        loads[name].wait()
    proj_weight = [held["wp"][m].T for m in range(2)]
    gain_in = [held["gains"][m, 0:1, :] for m in range(2)]
    gain_mid = [
        jnp.broadcast_to(held["gains"][m, 1:2, :], (128, 128)).T for m in range(2)
    ]
    mask = held["mask"][...].astype(F32).astype(BF16)
    picked = []
    for lo in range(4):
        t = lax.broadcasted_iota(jnp.int32, (8, 32), 0)
        i = lax.broadcasted_iota(jnp.int32, (8, 32), 1)
        pick = jnp.where(i == t * 4 + lo, 1.0, 0.0).astype(BF16)
        k = lax.broadcasted_iota(jnp.int32, (32, 128), 0)
        lane = lax.broadcasted_iota(jnp.int32, (32, 128), 1)
        place = jnp.where(lane == lo * 32 + k, 1.0, 0.0).astype(BF16)
        picked.append(mm(mm(pick, mask).astype(BF16), place))
    mask_flat = picked[0] + picked[1] + picked[2] + picked[3]

    def edges(m, state):
        for it in range(8):
            zn = normalize(state(it), gain_in[m]).astype(BF16)
            gate_s[pl.ds(it * 128, 128), :] = jax.nn.sigmoid(mm(zn, wg_ref[m]))
            proj = mm(proj_weight[m], zn, NT)
            keep = mask_flat[it : it + 1, :]
            left = keep * jax.nn.sigmoid(proj[0:128]) * proj[128:256]
            right = keep * jax.nn.sigmoid(proj[256:384]) * proj[384:512]
            flat_s[pl.ds(it, 128, stride=16), :] = left
            flat_s[pl.ds(8 + it, 128, stride=16), :] = right
        for s in range(8):
            send_a[m, s] = flat_s[pl.ds(s * 256, 256), :].astype(BF16)

    def triangle(m, during_a, during_b):
        go_a = Exchange(
            8,
            quad,
            on_quad,
            lambda p: send_a.at[m, p],
            lambda p: recv_a.at[m, p],
            ssem.at[5 * m],
            rsem.at[5 * m],
        )
        go_a.start()
        during_a()
        go_a.wait()
        for hi in range(2):
            lanes = jnp.concatenate([recv_a[m, hi * 4 + lo] for lo in range(4)], axis=1)
            moved = mm(lanes, swap_in)
            parts = [moved[:, lo * 128 : (lo + 1) * 128].reshape(32, 8, 128) for lo in range(4)]
            send_b[m, :, :, hi * 128 : (hi + 1) * 128] = jnp.concatenate(parts, axis=1).astype(BF16)
        go_b = Exchange(
            16,
            big,
            on_rows,
            lambda p: send_b.at[m, pl.ds(p * 2, 2)],
            lambda p: recv_b.at[m, p // 2, lax.rem(p, 2)],
            ssem.at[5 * m + 1],
            rsem.at[5 * m + 1],
        )
        go_b.start()
        during_b()
        go_b.wait()
        partner = on_col(quad * 2 + 1 - core)
        cross = remote(
            recv_b.at[m, :, :, 0],
            x_left.at[m],
            ssem.at[5 * m + 2, 0],
            rsem.at[5 * m + 2, 0],
            partner,
        )
        cross.start()
        if m == 0:
            cross_right = remote(
                recv_b.at[m, :, 1 - core, 1],
                x_right,
                ssem.at[5 * m + 2, 1],
                rsem.at[5 * m + 2, 1],
                partner,
            )
            cross_right.start()
            left = recv_b[m, :, :, 0].reshape(512, 256)
            right = recv_b[m, :, core, 1].reshape(256, 256)
            total = mm(left, right, NT)
            cross.wait()
            cross_right.wait()
            total += mm(x_left[m].reshape(512, 256), x_right[...].reshape(256, 256), NT)
            send_bt[m] = total.reshape(8, 2, 32, 256).astype(BF16)
        else:
            right = recv_b[m, :, :, 1].reshape(512, 256)
            own = mm(recv_b[m, :, :, 0].reshape(512, 256), right, TN)
            send_bt[m, :, core] = own.reshape(8, 32, 256).astype(BF16)
            cross.wait()
            other = mm(x_left[m].reshape(512, 256), right, TN)
            send_bt[m, :, 1 - core] = other.reshape(8, 32, 256).astype(BF16)
        back_b = Exchange(
            16,
            big,
            on_rows,
            lambda p: send_bt.at[m, p // 2, lax.rem(p, 2)],
            lambda p: recv_bt.at[m, p],
            ssem.at[5 * m + 3],
            rsem.at[5 * m + 3],
        )
        back_b.start()
        back_b.wait()
        for hi in range(2):
            block = recv_bt[m, :, :, hi * 128 : (hi + 1) * 128].astype(F32)
            lanes = jnp.concatenate(
                [block[:, lo * 8 : (lo + 1) * 8, :].reshape(128, 128) for lo in range(4)], axis=1
            ).astype(BF16)
            moved = mm(lanes, swap_out).astype(BF16)
            for lo in range(4):
                send_at[m, hi * 4 + lo] = moved[:, lo * 128 : (lo + 1) * 128]
        back_a = Exchange(
            8,
            quad,
            on_quad,
            lambda p: send_at.at[m, p],
            lambda p: recv_at.at[m, p],
            ssem.at[5 * m + 4],
            rsem.at[5 * m + 4],
        )
        back_a.start()
        back_a.wait()
        summed = recv_at[m].astype(F32).reshape(128, 8, 128)
        mean = jnp.sum(summed, axis=0, keepdims=True) * (1.0 / 128)
        mean_removed = summed - mean
        variance = jnp.sum(mean_removed * mean_removed, axis=0, keepdims=True) * (1.0 / 128)
        nrm_s[...] = (mean_removed * lax.rsqrt(variance + EPS)).reshape(1024, 128)

    def update(m, it):
        normed = (nrm_s[pl.ds(it, 128, stride=8), :] * gain_mid[m]).astype(BF16)
        return gate_s[pl.ds(it * 128, 128), :] * mm(normed, wo_ref[m], TN)

    def first_state(it):
        return pair_ref[pl.ds(it * 128, 128), :].astype(F32)

    def second_state(it):
        z = first_state(it) + update(0, it)
        z_s[pl.ds(it * 128, 128), :] = z
        return z

    def project(samples):
        weight = held["watt"][...].reshape(192, 768)
        for s in samples:
            for part in range(4):
                rows = pl.ds(s * 512 + part * 128, 128)
                value = held["tokens"][rows, :].astype(F32)
                xn_s[part * 128 : (part + 1) * 128, :] = normalize(
                    value, held["again"][...].reshape(1, 768)
                ).astype(BF16)
            proj = mm(weight, xn_s[...], NT)
            qkv_s[s] = proj[0:144].astype(BF16)
            sig_s[s] = jax.nn.sigmoid(proj[144:192])
            scores_s[s] = mm(qkv_s[s, 0:48, :], qkv_s[s, 48:96, :], TN) * (48.0**-0.5)

    def project_first():
        for name in ("tokens", "again", "watt"):
            loads[name].wait()
        project((0, 1))

    def nothing():
        pass

    edges(0, first_state)
    pl.semaphore_wait(barrier, 30)
    triangle(0, project_first, lambda: project((2, 3)))
    edges(1, second_state)
    triangle(1, nothing, nothing)
    for it in range(8):
        z = z_s[pl.ds(it * 128, 128), :] + update(1, it)
        out_ref[pl.ds(it * 128, 128), :] = z
        zn = normalize(z, held["bgain"][...]).astype(BF16)
        bias = mm(held["bw"][...], zn, NT).astype(BF16).astype(F32)
        heads_s[pl.ds(it, 16, stride=8), :] = bias
    to_head = Exchange(
        16,
        col,
        on_col,
        lambda p: heads_s.at[pl.ds(p * 8, 8)],
        lambda p: recv_h.at[p],
        ssem.at[10],
        rsem.at[10],
    )
    to_head.start()
    swap_plain = swap_matrix(False)
    to_head.wait()
    lanes = jnp.concatenate(
        [
            jnp.concatenate([recv_h[hi * 4 + lo] for lo in range(4)], axis=1)
            for hi in range(4)
        ],
        axis=0,
    ).astype(BF16)
    moved = mm(lanes, swap_plain)
    for hi in range(4):
        for lo in range(4):
            rows_s[pl.ds(hi * 32 + lo, 8, stride=4), :] = moved[
                hi * 8 : (hi + 1) * 8, lo * 128 : (lo + 1) * 128
            ]
    bias_s[big] = jnp.concatenate(
        [rows_s[hi * 32 : (hi + 1) * 32, :] for hi in range(4)], axis=1
    ).astype(BF16)
    spread = Exchange(
        16,
        big,
        on_rows,
        lambda p: bias_s.at[big],
        lambda p: bias_s.at[p],
        ssem.at[11],
        rsem.at[11],
    )

    def spread_start(d, carry):
        spread.copy(d).start()
        return carry

    to_tokens = Exchange(
        16,
        col,
        on_col,
        lambda p: send_o.at[p],
        lambda p: recv_o.at[p],
        ssem.at[12],
        rsem.at[12],
    )
    lax.fori_loop(1, 16, spread_start, 0)

    def attend(step, carry):
        part = lax.rem(big // 4 + step, 4)
        for lo in range(4):
            source = part * 4 + lo

            @pl.when(source != big)
            def _():
                spread.copy(lax.rem(big - source + 16, 16)).wait_recv()

        bias = bias_s[pl.ds(part * 4, 4)].reshape(128, 512).astype(F32)
        rows = pl.ds(pl.multiple_of(part * 128, 128), 128)
        for s in range(4):
            logits = scores_s[s, rows, :] + bias
            shifted = jnp.exp(logits - jnp.max(logits, axis=-1, keepdims=True))
            weights = shifted * (1.0 / jnp.sum(shifted, axis=-1, keepdims=True))
            mixed = mm(qkv_s[s, 96:144, :], weights.astype(BF16), NT)
            gated = mixed * sig_s[s, :, rows]
            ot_s[:, s * 128 : (s + 1) * 128] = gated.astype(BF16)
        moved = mm(ot_s[...], swap_plain).astype(BF16)
        for lo in range(4):
            target = part * 4 + lo
            send_o[target] = moved[:, lo * 128 : (lo + 1) * 128]

            @pl.when(target != col)
            def _():
                to_tokens.copy(lax.rem(target - col + 16, 16)).start()

            @pl.when(target == col)
            def _():
                to_tokens.own().start()

        return carry

    lax.fori_loop(0, 4, attend, 0)

    def spread_sent(d, carry):
        spread.copy(d).wait_send()
        return carry

    lax.fori_loop(1, 16, spread_sent, 0)
    for name in ("wout", "tgain", "wup", "wdown"):
        loads[name].wait()
    own = [
        held["tokens"][pl.ds(pl.multiple_of(s * 512 + col * 32, 32), 32), :] for s in range(4)
    ]
    own = jnp.concatenate(own, axis=0).astype(F32)
    to_tokens.wait()
    first = own + mm(recv_o[...].reshape(768, 128), held["wout"][...], TN)
    xn2 = normalize(first, held["tgain"][...].reshape(1, 768)).astype(BF16)
    total = first
    for j in range(4):
        up = mm(xn2, held["wup"][:, j * 384 : (j + 1) * 384])
        side = mm(xn2, held["wup"][:, 1536 + j * 384 : 1536 + (j + 1) * 384])
        hidden = (jax.nn.silu(up) * side).astype(BF16)
        total += mm(hidden, held["wdown"][j * 384 : (j + 1) * 384, :])
    tok_ref[...] = total


def on_device(
    pair,
    pair_mask,
    tri_proj,
    tri_gate,
    triangle_output_weight,
    tri_gains,
    pair_bias_gain,
    bias_weight,
    tokens,
    att_gain,
    att_proj,
    att_out,
    tr_gain,
    tr_up,
    tr_down,
):
    operands = (
        pair.reshape(1024, 128),
        pair_mask,
        tri_proj,
        tri_gate,
        triangle_output_weight,
        tri_gains,
        pair_bias_gain.reshape(1, 128),
        jnp.swapaxes(bias_weight, 0, 1),
        tokens.reshape(2048, 768),
        att_gain,
        jnp.swapaxes(att_proj, 1, 2),
        att_out,
        tr_gain,
        tr_up,
        tr_down,
    )
    vmem = pl.BlockSpec(memory_space=pltpu.VMEM)
    hbm = pl.BlockSpec(memory_space=pl.ANY)
    pair_out, tokens_out = pl.pallas_call(
        block_kernel,
        out_shape=(
            jax.ShapeDtypeStruct((1024, 128), F32),
            jax.ShapeDtypeStruct((128, 768), F32),
        ),
        in_specs=[hbm] * 15,
        out_specs=(vmem, vmem),
        scratch_shapes=[pltpu.VMEM(x.shape, x.dtype) for x in operands]
        + [
            pltpu.VMEM((1024, 128), F32),
            pltpu.VMEM((1024, 128), F32),
            pltpu.VMEM((2048, 128), F32),
            pltpu.VMEM((1024, 128), F32),
            pltpu.VMEM((2, 8, 256, 128), BF16),
            pltpu.VMEM((2, 8, 256, 128), BF16),
            pltpu.VMEM((2, 32, 32, 256), BF16),
            pltpu.VMEM((2, 8, 2, 2, 32, 256), BF16),
            pltpu.VMEM((2, 8, 2, 32, 256), BF16),
            pltpu.VMEM((8, 32, 256), BF16),
            pltpu.VMEM((2, 8, 2, 32, 256), BF16),
            pltpu.VMEM((2, 16, 32, 256), BF16),
            pltpu.VMEM((2, 8, 128, 128), BF16),
            pltpu.VMEM((2, 8, 128, 128), BF16),
            pltpu.VMEM((128, 128), F32),
            pltpu.VMEM((16, 8, 128), F32),
            pltpu.VMEM((128, 128), F32),
            pltpu.VMEM((16, 32, 512), BF16),
            pltpu.VMEM((512, 768), BF16),
            pltpu.VMEM((4, 144, 512), BF16),
            pltpu.VMEM((4, 48, 512), F32),
            pltpu.VMEM((4, 512, 512), F32),
            pltpu.VMEM((48, 512), BF16),
            pltpu.VMEM((16, 48, 128), BF16),
            pltpu.VMEM((16, 48, 128), BF16),
            pltpu.SemaphoreType.DMA((13, 16)),
            pltpu.SemaphoreType.DMA((13, 16)),
            pltpu.SemaphoreType.DMA((15,)),
        ],
        compiler_params=pltpu.CompilerParams(
            collective_id=0, has_side_effects=True, vmem_limit_bytes=60 * 1024 * 1024
        ),
        cost_estimate=pl.CostEstimate(
            flops=6_000_000_000, bytes_accessed=15_000_000, transcendentals=3_000_000
        ),
    )(*operands)
    return pair_out.reshape(32, 32, 128), tokens_out.reshape(4, 32, 768)


def solution(mesh):
    placed = (
        P(("group", "row"), "col", None),
        P(("group", "row"), "col"),
        P(),
        P(),
        P(),
        P(),
        P(),
        P(),
        P(("group", "row"), None, None),
        P(),
        P(None, None, "col"),
        P(),
        P(),
        P(),
        P(),
    )
    return jax.shard_map(
        on_device,
        mesh=mesh,
        in_specs=placed,
        out_specs=(P(("group", "row"), "col", None), P(("group", "row"), "col", None)),
        check_vma=False,
    )
```

```python
import jax
import jax.numpy as jnp
from jax import lax
from jax.experimental import pallas as pl
from jax.experimental.pallas import tpu as pltpu
from jax.sharding import PartitionSpec as P

EPS = 1e-05
MESH = pl.DeviceIdType.MESH
F32 = jnp.float32
BF16 = jnp.bfloat16
NT = (((1,), (1,)), ((), ()))
TN = (((0,), (0,)), ((), ()))


def normalize(value, gain):
    mean = jnp.mean(value, axis=-1, keepdims=True)
    mean_removed = value - mean
    variance = jnp.mean(mean_removed * mean_removed, axis=-1, keepdims=True)
    return mean_removed * lax.rsqrt(variance + EPS) * gain


def mm(a, b, dims=(((1,), (0,)), ((), ()))):
    return lax.dot_general(a, b, dims, preferred_element_type=F32)


def swap_matrix():
    row = lax.broadcasted_iota(jnp.int32, (512, 512), 0)
    col = lax.broadcasted_iota(jnp.int32, (512, 512), 1)
    a, b, k = row >> 7, (row >> 5) & 3, row & 31
    return jnp.where((b << 7) + (a << 5) + k == col, 1.0, 0.0).astype(BF16)


def remote(src, dst, send, recv, device):
    return pltpu.make_async_remote_copy(
        src_ref=src,
        dst_ref=dst,
        send_sem=send,
        recv_sem=recv,
        device_id=device,
        device_id_type=MESH,
    )


def loop(first, last, step):
    def body(d, carry):
        step(d)
        return carry

    lax.fori_loop(first, last, body, 0)


class Exchange:
    def __init__(self, n, me, device, src, dst, send, recv):
        self.n, self.me, self.device = n, me, device
        self.src, self.dst, self.send, self.recv = src, dst, send, recv

    def copy(self, d):
        peer = lax.rem(self.me + d, self.n)
        return remote(
            self.src(peer), self.dst(self.me), self.send.at[d], self.recv.at[d], self.device(peer)
        )

    def own(self):
        return pltpu.make_async_copy(self.src(self.me), self.dst(self.me), self.recv.at[0])


class Burst:
    def __init__(self, n, me, device, src, dst, all_dst, most_src, send, recv):
        self.n, self.me, self.device = n, me, device
        self.src, self.dst, self.all_dst, self.most_src = src, dst, all_dst, most_src
        self.send, self.recv = send, recv

    def start(self):
        def one(d):
            peer = lax.rem(self.me + d, self.n)
            remote(
                self.src(peer), self.dst(self.me), self.send, self.recv, self.device(peer)
            ).start()

        loop(1, self.n, one)
        pltpu.make_async_copy(self.src(self.me), self.dst(self.me), self.recv).start()

    def wait(self):
        pltpu.make_async_copy(self.all_dst, self.all_dst, self.recv).wait()

    def drain(self):
        pltpu.make_async_copy(self.most_src, self.most_src, self.send).wait()


NAMES = (
    "pair",
    "mask",
    "wp",
    "wg",
    "wo",
    "gains",
    "bgain",
    "bw",
    "tokens",
    "again",
    "watt",
    "wout",
    "tgain",
    "wup",
    "wdown",
)


def block_kernel(*refs):
    inputs = dict(zip(NAMES, refs[:15]))
    out_ref, tok_ref = refs[15:17]
    held = dict(zip(NAMES, refs[17:32]))
    (
        z_s,
        gate_s,
        flat_s,
        nrm_s,
        mix_s,
        wpt_s,
        gmid_s,
        mask_s,
        swap_s,
        send_a,
        recv_a,
        send_b,
        recv_b,
        x_left,
        x_right,
        send_bt,
        recv_bt,
        send_at,
        recv_at,
        heads_s,
        recv_h,
        rows_s,
        bias_s,
        xn_s,
        qkv_s,
        sig_s,
        scores_s,
        ot_s,
        send_o,
        recv_o,
        ssem,
        rsem,
        cross_ssem,
        cross_rsem,
        many_ssem,
        many_rsem,
        load_sem,
    ) = refs[32:]
    group, row, col = (lax.axis_index(name) for name in ("group", "row", "col"))
    big = group * 8 + row
    quad = col // 2
    core = lax.rem(col, 2)

    loads = {
        name: pltpu.make_async_copy(inputs[name], held[name], load_sem.at[i])
        for i, name in enumerate(NAMES)
    }
    for name in NAMES:
        loads[name].start()

    def on_col(peer):
        return {"col": peer}

    def on_quad(peer):
        return {"col": peer * 2 + core}

    def on_rows(peer):
        return {"group": peer // 8, "row": lax.rem(peer, 8)}

    barrier = pltpu.get_barrier_semaphore()

    def greet(d):
        for device in (on_col(lax.rem(col + d, 16)), on_rows(lax.rem(big + d, 16))):
            pl.semaphore_signal(barrier, inc=1, device_id=device, device_id_type=MESH)

    loop(1, 16, greet)

    swap_s[...] = swap_matrix()
    pair_ref = held["pair"]
    wg_ref, wo_ref = held["wg"], held["wo"]

    for name in ("pair", "mask", "wp", "wg", "wo", "gains", "bgain", "bw"):
        loads[name].wait()
    gain_in = [held["gains"][m, 0:1, :] for m in range(2)]
    for m in range(2):
        wpt_s[m] = held["wp"][m].T
        gmid_s[m] = jnp.broadcast_to(held["gains"][m, 1:2, :], (128, 128)).T
    mask = held["mask"][...].astype(F32).astype(BF16)
    picked = []
    for lo in range(4):
        t = lax.broadcasted_iota(jnp.int32, (8, 32), 0)
        i = lax.broadcasted_iota(jnp.int32, (8, 32), 1)
        pick = jnp.where(i == t * 4 + lo, 1.0, 0.0).astype(BF16)
        k = lax.broadcasted_iota(jnp.int32, (32, 128), 0)
        lane = lax.broadcasted_iota(jnp.int32, (32, 128), 1)
        place = jnp.where(lane == lo * 32 + k, 1.0, 0.0).astype(BF16)
        picked.append(mm(mm(pick, mask).astype(BF16), place))
    mask_s[...] = picked[0] + picked[1] + picked[2] + picked[3]

    def edges(m, half, state):
        for t in range(4):
            it = half * 4 + t
            zn = normalize(state(it), gain_in[m]).astype(BF16)
            proj = mm(wpt_s[m], zn, NT)
            keep = mask_s[it : it + 1, :]
            left = keep * jax.nn.sigmoid(proj[0:128]) * proj[128:256]
            right = keep * jax.nn.sigmoid(proj[256:384]) * proj[384:512]
            flat_s[pl.ds(t, 128, stride=8), :] = left
            flat_s[pl.ds(4 + t, 128, stride=8), :] = right
            gate_s[pl.ds(it * 128, 128), :] = jax.nn.sigmoid(mm(zn, wg_ref[m]))
        for s in range(8):
            send_a[m, half, s] = flat_s[pl.ds(s * 128, 128), :].astype(BF16)

    def burst(stage, m, half):
        sems = ssem.at[stage * 4 + m * 2 + half], rsem.at[stage * 4 + m * 2 + half]
        if stage == 0:
            return Burst(
                8,
                quad,
                on_quad,
                lambda p: send_a.at[m, half, p],
                lambda p: recv_a.at[m, half, p],
                recv_a.at[m, half],
                send_a.at[m, half, pl.ds(0, 7)],
                *sems,
            )
        if stage == 1:
            return Burst(
                16,
                big,
                on_rows,
                lambda p: send_b.at[m, half, p],
                lambda p: recv_b.at[m, half, p // 2, lax.rem(p, 2)],
                recv_b.at[m, half],
                send_b.at[m, half, pl.ds(0, 15)],
                *sems,
            )
        if stage == 2:
            return Burst(
                16,
                big,
                on_rows,
                lambda p: send_bt.at[m, half, p],
                lambda p: recv_bt.at[m, half, p],
                recv_bt.at[m, half],
                send_bt.at[m, half, pl.ds(0, 15)],
                *sems,
            )
        return Burst(
            8,
            quad,
            on_quad,
            lambda p: send_at.at[m, half, p],
            lambda p: recv_at.at[m, half, p],
            recv_at.at[m, half],
            send_at.at[m, half, pl.ds(0, 7)],
            *sems,
        )

    partner = on_col(quad * 2 + 1 - core)

    def cross_left(m, half):
        return remote(
            recv_b.at[m, half, :, :, 0],
            x_left.at[m, half],
            cross_ssem.at[m * 2 + half],
            cross_rsem.at[m * 2 + half],
            partner,
        )

    def cross_right(half):
        return remote(
            recv_b.at[0, half, :, 1 - core, 1],
            x_right.at[half],
            cross_ssem.at[4 + half],
            cross_rsem.at[4 + half],
            partner,
        )

    def to_rows(m, half):
        for hi in range(2):
            lanes = jnp.concatenate([recv_a[m, half, hi * 4 + lo] for lo in range(4)], axis=1)
            moved = mm(lanes, swap_s[...])
            for lo in range(4):
                mix_s[pl.ds(hi * 512 + lo, 128, stride=4), :] = moved[:, lo * 128 : (lo + 1) * 128]
        both = jnp.concatenate([mix_s[0:512, :], mix_s[512:1024, :]], axis=1)
        send_b[m, half] = both.astype(BF16).reshape(16, 2, 16, 256)

    def to_channels(m, half):
        for hi in range(2):
            block = recv_bt[m, half, :, :, hi * 128 : (hi + 1) * 128]
            mix_s[hi * 256 : (hi + 1) * 256, :] = block.astype(F32).reshape(256, 128)
        for hi in range(2):
            lanes = jnp.concatenate(
                [mix_s[pl.ds(hi * 256 + lo, 64, stride=4), :] for lo in range(4)], axis=1
            )
            moved = mm(lanes.astype(BF16), swap_s[...]).astype(BF16)
            for lo in range(4):
                send_at[m, half, hi * 4 + lo] = moved[:, lo * 128 : (lo + 1) * 128]

    def triangle(m, gap):
        for half in range(2):
            burst(0, m, half).wait()
            to_rows(m, half)
            burst(1, m, half).start()
        gap()
        for half in range(2):
            burst(0, m, half).drain()
        if m == 0:
            for half in range(2):
                burst(1, m, half).wait()
                cross_left(m, half).start()
                cross_right(half).start()
            right = jnp.concatenate(
                [recv_b[m, half, s, core, 1] for s in range(8) for half in range(2)], axis=0
            )
            own = [mm(recv_b[m, half, :, :, 0].reshape(256, 256), right, NT) for half in range(2)]
            for half in range(2):
                cross_left(m, half).wait_recv()
                cross_right(half).wait_recv()
            right = jnp.concatenate(
                [x_right[half, s] for s in range(8) for half in range(2)], axis=0
            )
            for half in range(2):
                total = own[half] + mm(x_left[m, half].reshape(256, 256), right, NT)
                send_bt[m, half] = total.astype(BF16).reshape(16, 16, 256)
                burst(2, m, half).start()
            for half in range(2):
                cross_right(half).wait_send()
        else:
            right, own = [], None
            for half in range(2):
                burst(1, m, half).wait()
                cross_left(m, half).start()
                right.append(recv_b[m, half, :, :, 1].reshape(256, 256))
                term = mm(recv_b[m, half, :, :, 0].reshape(256, 256), right[half], TN)
                own = term if half == 0 else own + term
            other = None
            for half in range(2):
                cross_left(m, half).wait_recv()
                term = mm(x_left[m, half].reshape(256, 256), right[half], TN)
                other = term if half == 0 else other + term
            for half in range(2):
                for s in range(8):
                    at = slice(s * 32 + half * 16, s * 32 + half * 16 + 16)
                    send_bt[m, half, s * 2 + core] = own[at].astype(BF16)
                    send_bt[m, half, s * 2 + 1 - core] = other[at].astype(BF16)
                burst(2, m, half).start()
        for half in range(2):
            burst(1, m, half).drain()
            cross_left(m, half).wait_send()
        for half in range(2):
            burst(2, m, half).wait()
            to_channels(m, half)
            burst(3, m, half).start()
        for half in range(2):
            burst(2, m, half).drain()

    def middle_norm(m, half):
        summed = recv_at[m, half].astype(F32).reshape(64, 8, 128)

        def over_channels(value):
            pairs = jnp.sum(value, axis=0)
            return (pairs + pltpu.roll(pairs, 4, 0)) * (1.0 / 128)

        mean_removed = summed - over_channels(summed)[None]
        variance = over_channels(mean_removed * mean_removed)
        nrm_s[...] = (mean_removed * lax.rsqrt(variance + EPS)[None]).reshape(512, 128)

    def update(m, it):
        normed = (nrm_s[pl.ds(it % 4, 128, stride=4), :] * gmid_s[m]).astype(BF16)
        return gate_s[pl.ds(it * 128, 128), :] * mm(normed, wo_ref[m], TN)

    def first_state(it):
        return pair_ref[pl.ds(it * 128, 128), :].astype(F32)

    def second_state(it):
        z = first_state(it) + update(0, it)
        z_s[pl.ds(it * 128, 128), :] = z
        return z

    def project(samples):
        weight = held["watt"][...].reshape(192, 768)
        for s in samples:
            for part in range(4):
                rows = pl.ds(s * 512 + part * 128, 128)
                value = held["tokens"][rows, :].astype(F32)
                xn_s[part * 128 : (part + 1) * 128, :] = normalize(
                    value, held["again"][...].reshape(1, 768)
                ).astype(BF16)
            proj = mm(weight, xn_s[...], NT)
            qkv_s[s] = proj[0:144].astype(BF16)
            sig_s[s] = jax.nn.sigmoid(proj[144:192])
            scores_s[s] = mm(qkv_s[s, 0:48, :], qkv_s[s, 48:96, :], TN) * (48.0**-0.5)

    def gap_first():
        for name in ("tokens", "again", "watt"):
            loads[name].wait()
        project((0, 1))

    edges(0, 0, first_state)
    pl.semaphore_wait(barrier, 30)
    burst(0, 0, 0).start()
    edges(0, 1, first_state)
    burst(0, 0, 1).start()
    triangle(0, gap_first)
    for half in range(2):
        burst(3, 0, half).wait()
        middle_norm(0, half)
        edges(1, half, second_state)
        burst(0, 1, half).start()
    for half in range(2):
        burst(3, 0, half).drain()
    triangle(1, lambda: project((2, 3)))
    for half in range(2):
        burst(3, 1, half).wait()
        middle_norm(1, half)
        for it in range(half * 4, half * 4 + 4):
            z = z_s[pl.ds(it * 128, 128), :] + update(1, it)
            out_ref[pl.ds(it * 128, 128), :] = z
            zn = normalize(z, held["bgain"][...]).astype(BF16)
            bias = mm(held["bw"][...], zn, NT).astype(BF16).astype(F32)
            heads_s[pl.ds(it, 16, stride=8), :] = bias
    to_head = Burst(
        16,
        col,
        on_col,
        lambda p: heads_s.at[pl.ds(p * 8, 8)],
        lambda p: recv_h.at[p],
        recv_h,
        heads_s.at[pl.ds(0, 120)],
        ssem.at[16],
        rsem.at[16],
    )
    to_head.start()
    for half in range(2):
        burst(3, 1, half).drain()
    to_head.wait()
    lanes = jnp.concatenate(
        [
            jnp.concatenate([recv_h[hi * 4 + lo] for lo in range(4)], axis=1)
            for hi in range(4)
        ],
        axis=0,
    ).astype(BF16)
    moved = mm(lanes, swap_s[...])
    for hi in range(4):
        for lo in range(4):
            rows_s[pl.ds(hi * 32 + lo, 8, stride=4), :] = moved[
                hi * 8 : (hi + 1) * 8, lo * 128 : (lo + 1) * 128
            ]
    bias_s[big] = jnp.concatenate(
        [rows_s[hi * 32 : (hi + 1) * 32, :] for hi in range(4)], axis=1
    ).astype(BF16)
    spread = Exchange(
        16,
        big,
        on_rows,
        lambda p: bias_s.at[big],
        lambda p: bias_s.at[p],
        many_ssem.at[0],
        many_rsem.at[0],
    )

    to_tokens = Exchange(
        16,
        col,
        on_col,
        lambda p: send_o.at[p],
        lambda p: recv_o.at[p],
        many_ssem.at[1],
        many_rsem.at[1],
    )
    loop(1, 16, lambda d: spread.copy(d).start())

    def attend(step, carry):
        part = lax.rem(big // 4 + step, 4)
        for lo in range(4):
            source = part * 4 + lo

            @pl.when(source != big)
            def _():
                spread.copy(lax.rem(big - source + 16, 16)).wait_recv()

        bias = bias_s[pl.ds(part * 4, 4)].reshape(128, 512).astype(F32)
        rows = pl.ds(pl.multiple_of(part * 128, 128), 128)
        for s in range(4):
            logits = scores_s[s, rows, :] + bias
            shifted = jnp.exp(logits - jnp.max(logits, axis=-1, keepdims=True))
            weights = shifted * (1.0 / jnp.sum(shifted, axis=-1, keepdims=True))
            mixed = mm(qkv_s[s, 96:144, :], weights.astype(BF16), NT)
            gated = mixed * sig_s[s, :, rows]
            ot_s[:, s * 128 : (s + 1) * 128] = gated.astype(BF16)
        moved = mm(ot_s[...], swap_s[...]).astype(BF16)
        for lo in range(4):
            target = part * 4 + lo
            send_o[target] = moved[:, lo * 128 : (lo + 1) * 128]

            @pl.when(target != col)
            def _():
                to_tokens.copy(lax.rem(target - col + 16, 16)).start()

            @pl.when(target == col)
            def _():
                to_tokens.own().start()

        return carry

    lax.fori_loop(0, 4, attend, 0)

    loop(1, 16, lambda d: spread.copy(d).wait_send())
    to_head.drain()
    for name in ("wout", "tgain", "wup", "wdown"):
        loads[name].wait()
    own = [
        held["tokens"][pl.ds(pl.multiple_of(s * 512 + col * 32, 32), 32), :] for s in range(4)
    ]
    own = jnp.concatenate(own, axis=0).astype(F32)
    to_tokens.own().wait()
    loop(1, 16, lambda d: to_tokens.copy(d).wait())
    first = own + mm(recv_o[...].reshape(768, 128), held["wout"][...], TN)
    xn2 = normalize(first, held["tgain"][...].reshape(1, 768)).astype(BF16)
    total = first
    for j in range(4):
        up = mm(xn2, held["wup"][:, j * 384 : (j + 1) * 384])
        side = mm(xn2, held["wup"][:, 1536 + j * 384 : 1536 + (j + 1) * 384])
        hidden = (jax.nn.silu(up) * side).astype(BF16)
        total += mm(hidden, held["wdown"][j * 384 : (j + 1) * 384, :])
    tok_ref[...] = total


def on_device(
    pair,
    pair_mask,
    tri_proj,
    tri_gate,
    triangle_output_weight,
    tri_gains,
    pair_bias_gain,
    bias_weight,
    tokens,
    att_gain,
    att_proj,
    att_out,
    tr_gain,
    tr_up,
    tr_down,
):
    operands = (
        pair.reshape(1024, 128),
        pair_mask,
        tri_proj,
        tri_gate,
        triangle_output_weight,
        tri_gains,
        pair_bias_gain.reshape(1, 128),
        jnp.swapaxes(bias_weight, 0, 1),
        tokens.reshape(2048, 768),
        att_gain,
        jnp.swapaxes(att_proj, 1, 2),
        att_out,
        tr_gain,
        tr_up,
        tr_down,
    )
    vmem = pl.BlockSpec(memory_space=pltpu.VMEM)
    hbm = pl.BlockSpec(memory_space=pl.ANY)
    pair_out, tokens_out = pl.pallas_call(
        block_kernel,
        out_shape=(
            jax.ShapeDtypeStruct((1024, 128), F32),
            jax.ShapeDtypeStruct((128, 768), F32),
        ),
        in_specs=[hbm] * 15,
        out_specs=(vmem, vmem),
        scratch_shapes=[pltpu.VMEM(x.shape, x.dtype) for x in operands]
        + [
            pltpu.VMEM((1024, 128), F32),
            pltpu.VMEM((1024, 128), F32),
            pltpu.VMEM((1024, 128), F32),
            pltpu.VMEM((512, 128), F32),
            pltpu.VMEM((1024, 128), F32),
            pltpu.VMEM((2, 512, 128), BF16),
            pltpu.VMEM((2, 128, 128), F32),
            pltpu.VMEM((8, 128), F32),
            pltpu.VMEM((512, 512), BF16),
            pltpu.VMEM((2, 2, 8, 128, 128), BF16),
            pltpu.VMEM((2, 2, 8, 128, 128), BF16),
            pltpu.VMEM((2, 2, 16, 2, 16, 256), BF16),
            pltpu.VMEM((2, 2, 8, 2, 2, 16, 256), BF16),
            pltpu.VMEM((2, 2, 8, 2, 16, 256), BF16),
            pltpu.VMEM((2, 8, 16, 256), BF16),
            pltpu.VMEM((2, 2, 16, 16, 256), BF16),
            pltpu.VMEM((2, 2, 16, 16, 256), BF16),
            pltpu.VMEM((2, 2, 8, 64, 128), BF16),
            pltpu.VMEM((2, 2, 8, 64, 128), BF16),
            pltpu.VMEM((128, 128), F32),
            pltpu.VMEM((16, 8, 128), F32),
            pltpu.VMEM((128, 128), F32),
            pltpu.VMEM((16, 32, 512), BF16),
            pltpu.VMEM((512, 768), BF16),
            pltpu.VMEM((4, 144, 512), BF16),
            pltpu.VMEM((4, 48, 512), F32),
            pltpu.VMEM((4, 512, 512), F32),
            pltpu.VMEM((48, 512), BF16),
            pltpu.VMEM((16, 48, 128), BF16),
            pltpu.VMEM((16, 48, 128), BF16),
            pltpu.SemaphoreType.DMA((17,)),
            pltpu.SemaphoreType.DMA((17,)),
            pltpu.SemaphoreType.DMA((6,)),
            pltpu.SemaphoreType.DMA((6,)),
            pltpu.SemaphoreType.DMA((2, 16)),
            pltpu.SemaphoreType.DMA((2, 16)),
            pltpu.SemaphoreType.DMA((15,)),
        ],
        compiler_params=pltpu.CompilerParams(
            collective_id=0, has_side_effects=True, vmem_limit_bytes=60 * 1024 * 1024
        ),
        cost_estimate=pl.CostEstimate(
            flops=6_000_000_000, bytes_accessed=15_000_000, transcendentals=3_000_000
        ),
    )(*operands)
    return pair_out.reshape(32, 32, 128), tokens_out.reshape(4, 32, 768)


def solution(mesh):
    placed = (
        P(("group", "row"), "col", None),
        P(("group", "row"), "col"),
        P(),
        P(),
        P(),
        P(),
        P(),
        P(),
        P(("group", "row"), None, None),
        P(),
        P(None, None, "col"),
        P(),
        P(),
        P(),
        P(),
    )
    return jax.shard_map(
        on_device,
        mesh=mesh,
        in_specs=placed,
        out_specs=(P(("group", "row"), "col", None), P(("group", "row"), "col", None)),
        check_vma=False,
    )
```

```python
import jax
import jax.numpy as jnp
from jax import lax
from jax.experimental import pallas as pl
from jax.experimental.pallas import tpu as pltpu
from jax.sharding import PartitionSpec as P

EPS = 1e-05
MESH = pl.DeviceIdType.MESH
F32 = jnp.float32
BF16 = jnp.bfloat16
NT = (((1,), (1,)), ((), ()))
TN = (((0,), (0,)), ((), ()))


def normalize(value, gain):
    mean = jnp.mean(value, axis=-1, keepdims=True)
    mean_removed = value - mean
    variance = jnp.mean(mean_removed * mean_removed, axis=-1, keepdims=True)
    return mean_removed * lax.rsqrt(variance + EPS) * gain


def mm(a, b, dims=(((1,), (0,)), ((), ()))):
    return lax.dot_general(a, b, dims, preferred_element_type=F32)


def swap_matrix():
    row = lax.broadcasted_iota(jnp.int32, (512, 512), 0)
    col = lax.broadcasted_iota(jnp.int32, (512, 512), 1)
    a, b, k = row >> 7, (row >> 5) & 3, row & 31
    return jnp.where((b << 7) + (a << 5) + k == col, 1.0, 0.0).astype(BF16)


def remote(src, dst, send, recv, device):
    return pltpu.make_async_remote_copy(
        src_ref=src,
        dst_ref=dst,
        send_sem=send,
        recv_sem=recv,
        device_id=device,
        device_id_type=MESH,
    )


def loop(first, last, step):
    def body(d, carry):
        step(d)
        return carry

    lax.fori_loop(first, last, body, 0)


class Exchange:
    def __init__(self, n, me, device, src, dst, send, recv):
        self.n, self.me, self.device = n, me, device
        self.src, self.dst, self.send, self.recv = src, dst, send, recv

    def copy(self, d):
        peer = lax.rem(self.me + d, self.n)
        return remote(
            self.src(peer), self.dst(self.me), self.send.at[d], self.recv.at[d], self.device(peer)
        )

    def own(self):
        return pltpu.make_async_copy(self.src(self.me), self.dst(self.me), self.recv.at[0])


def ring(at, i, n):
    step = (i + 1) // 2
    return lax.rem(at + jnp.where(lax.rem(i, 2) == 1, step, n - step), n)


class Burst:
    def __init__(self, n, at, pair, device, src, dst, all_dst, most_src, send, recv):
        self.n, self.at, self.pair, self.me, self.device = n, at, pair, pair * n + at, device
        self.src, self.dst, self.all_dst, self.most_src = src, dst, all_dst, most_src
        self.send, self.recv = send, recv

    def to(self, peer):
        remote(
            self.src(peer), self.dst(self.me), self.send, self.recv, self.device(peer)
        ).start()

    def start(self):
        other = 1 - self.pair

        def both(j):
            place = ring(self.at, self.n - 1 - j, self.n)
            self.to(other * self.n + place)
            self.to(self.pair * self.n + place)

        loop(0, self.n - 1, both)
        self.to(other * self.n + self.at)
        pltpu.make_async_copy(self.src(self.me), self.dst(self.me), self.recv).start()

    def wait(self):
        pltpu.make_async_copy(self.all_dst, self.all_dst, self.recv).wait()

    def drain(self):
        pltpu.make_async_copy(self.most_src, self.most_src, self.send).wait()


NAMES = (
    "pair",
    "mask",
    "wp",
    "wg",
    "wo",
    "gains",
    "bgain",
    "bw",
    "tokens",
    "again",
    "watt",
    "wout",
    "tgain",
    "wup",
    "wdown",
)


def block_kernel(*refs):
    inputs = dict(zip(NAMES, refs[:15]))
    out_ref, tok_ref = refs[15:17]
    held = dict(zip(NAMES, refs[17:32]))
    (
        z_s,
        gate_s,
        flat_s,
        nrm_s,
        mix_s,
        wpt_s,
        gmid_s,
        mask_s,
        swap_s,
        send_a,
        recv_a,
        send_b,
        recv_b,
        x_left,
        x_right,
        send_bt,
        recv_bt,
        send_at,
        recv_at,
        heads_s,
        recv_h,
        rows_s,
        bias_s,
        xn_s,
        qkv_s,
        sig_s,
        scores_s,
        ot_s,
        send_o,
        recv_o,
        ssem,
        rsem,
        cross_ssem,
        cross_rsem,
        many_ssem,
        many_rsem,
        load_sem,
    ) = refs[32:]
    group, row, col = (lax.axis_index(name) for name in ("group", "row", "col"))
    big = group * 8 + row
    quad = col // 2
    core = lax.rem(col, 2)

    loads = {
        name: pltpu.make_async_copy(inputs[name], held[name], load_sem.at[i])
        for i, name in enumerate(NAMES)
    }
    for name in NAMES:
        loads[name].start()

    def on_col(peer):
        return {"col": peer}

    def on_quad(peer):
        return {"col": peer * 2 + core}

    def on_rows(peer):
        return {"group": peer // 8, "row": lax.rem(peer, 8)}

    barrier = pltpu.get_barrier_semaphore()

    def greet(d):
        for device in (on_col(lax.rem(col + d, 16)), on_rows(lax.rem(big + d, 16))):
            pl.semaphore_signal(barrier, inc=1, device_id=device, device_id_type=MESH)

    loop(1, 16, greet)

    swap_s[...] = swap_matrix()
    pair_ref = held["pair"]
    wg_ref, wo_ref = held["wg"], held["wo"]

    for name in ("pair", "mask", "wp", "wg", "wo", "gains", "bgain", "bw"):
        loads[name].wait()
    gain_in = [held["gains"][m, 0:1, :] for m in range(2)]
    for m in range(2):
        wpt_s[m] = held["wp"][m].T
        gmid_s[m] = jnp.broadcast_to(held["gains"][m, 1:2, :], (128, 128)).T
    mask = held["mask"][...].astype(F32).astype(BF16)
    picked = []
    for lo in range(4):
        t = lax.broadcasted_iota(jnp.int32, (8, 32), 0)
        i = lax.broadcasted_iota(jnp.int32, (8, 32), 1)
        pick = jnp.where(i == t * 4 + lo, 1.0, 0.0).astype(BF16)
        k = lax.broadcasted_iota(jnp.int32, (32, 128), 0)
        lane = lax.broadcasted_iota(jnp.int32, (32, 128), 1)
        place = jnp.where(lane == lo * 32 + k, 1.0, 0.0).astype(BF16)
        picked.append(mm(mm(pick, mask).astype(BF16), place))
    mask_s[...] = picked[0] + picked[1] + picked[2] + picked[3]

    def edges(m, half, state):
        for t in range(4):
            it = half * 4 + t
            zn = normalize(state(it), gain_in[m]).astype(BF16)
            proj = mm(wpt_s[m], zn, NT)
            keep = mask_s[it : it + 1, :]
            left = keep * jax.nn.sigmoid(proj[0:128]) * proj[128:256]
            right = keep * jax.nn.sigmoid(proj[256:384]) * proj[384:512]
            flat_s[pl.ds(t, 128, stride=8), :] = left
            flat_s[pl.ds(4 + t, 128, stride=8), :] = right
            gate_s[pl.ds(it * 128, 128), :] = jax.nn.sigmoid(mm(zn, wg_ref[m]))
        for s in range(8):
            send_a[m, half, s] = flat_s[pl.ds(s * 128, 128), :].astype(BF16)

    def burst(stage, m, half):
        sems = ssem.at[stage * 4 + m * 2 + half], rsem.at[stage * 4 + m * 2 + half]
        if stage == 0:
            return Burst(
                4,
                lax.rem(quad, 4),
                quad // 4,
                on_quad,
                lambda p: send_a.at[m, half, p],
                lambda p: recv_a.at[m, half, p],
                recv_a.at[m, half],
                send_a.at[m, half, pl.ds(0, 7)],
                *sems,
            )
        if stage == 1:
            return Burst(
                8,
                row,
                group,
                on_rows,
                lambda p: send_b.at[m, half, p],
                lambda p: recv_b.at[m, half, p // 2, lax.rem(p, 2)],
                recv_b.at[m, half],
                send_b.at[m, half, pl.ds(0, 15)],
                *sems,
            )
        if stage == 2:
            return Burst(
                8,
                row,
                group,
                on_rows,
                lambda p: send_bt.at[m, half, p],
                lambda p: recv_bt.at[m, half, p],
                recv_bt.at[m, half],
                send_bt.at[m, half, pl.ds(0, 15)],
                *sems,
            )
        return Burst(
            4,
            lax.rem(quad, 4),
            quad // 4,
            on_quad,
            lambda p: send_at.at[m, half, p],
            lambda p: recv_at.at[m, half, p],
            recv_at.at[m, half],
            send_at.at[m, half, pl.ds(0, 7)],
            *sems,
        )

    partner = on_col(quad * 2 + 1 - core)

    def cross_left(m, half):
        return remote(
            recv_b.at[m, half, :, :, 0],
            x_left.at[m, half],
            cross_ssem.at[m * 2 + half],
            cross_rsem.at[m * 2 + half],
            partner,
        )

    def cross_right(half):
        return remote(
            recv_b.at[0, half, :, 1 - core, 1],
            x_right.at[half],
            cross_ssem.at[4 + half],
            cross_rsem.at[4 + half],
            partner,
        )

    def to_rows(m, half):
        for hi in range(2):
            lanes = jnp.concatenate([recv_a[m, half, hi * 4 + lo] for lo in range(4)], axis=1)
            moved = mm(lanes, swap_s[...])
            for lo in range(4):
                mix_s[pl.ds(hi * 512 + lo, 128, stride=4), :] = moved[:, lo * 128 : (lo + 1) * 128]
        both = jnp.concatenate([mix_s[0:512, :], mix_s[512:1024, :]], axis=1)
        send_b[m, half] = both.astype(BF16).reshape(16, 2, 16, 256)

    def to_channels(m, half):
        for hi in range(2):
            block = recv_bt[m, half, :, :, hi * 128 : (hi + 1) * 128]
            mix_s[hi * 256 : (hi + 1) * 256, :] = block.astype(F32).reshape(256, 128)
        for hi in range(2):
            lanes = jnp.concatenate(
                [mix_s[pl.ds(hi * 256 + lo, 64, stride=4), :] for lo in range(4)], axis=1
            )
            moved = mm(lanes.astype(BF16), swap_s[...]).astype(BF16)
            for lo in range(4):
                send_at[m, half, hi * 4 + lo] = moved[:, lo * 128 : (lo + 1) * 128]

    def triangle(m, gap):
        for half in range(2):
            burst(0, m, half).wait()
            to_rows(m, half)
            burst(1, m, half).start()
        gap()
        for half in range(2):
            burst(0, m, half).drain()
        if m == 0:
            for half in range(2):
                burst(1, m, half).wait()
                cross_left(m, half).start()
                cross_right(half).start()
            right = jnp.concatenate(
                [recv_b[m, half, s, core, 1] for s in range(8) for half in range(2)], axis=0
            )
            own = [mm(recv_b[m, half, :, :, 0].reshape(256, 256), right, NT) for half in range(2)]
            for half in range(2):
                cross_left(m, half).wait_recv()
                cross_right(half).wait_recv()
            right = jnp.concatenate(
                [x_right[half, s] for s in range(8) for half in range(2)], axis=0
            )
            for half in range(2):
                total = own[half] + mm(x_left[m, half].reshape(256, 256), right, NT)
                send_bt[m, half] = total.astype(BF16).reshape(16, 16, 256)
                burst(2, m, half).start()
            for half in range(2):
                cross_right(half).wait_send()
        else:
            right, own = [], None
            for half in range(2):
                burst(1, m, half).wait()
                cross_left(m, half).start()
                right.append(recv_b[m, half, :, :, 1].reshape(256, 256))
                term = mm(recv_b[m, half, :, :, 0].reshape(256, 256), right[half], TN)
                own = term if half == 0 else own + term
            other = None
            for half in range(2):
                cross_left(m, half).wait_recv()
                term = mm(x_left[m, half].reshape(256, 256), right[half], TN)
                other = term if half == 0 else other + term
            for half in range(2):
                for s in range(8):
                    at = slice(s * 32 + half * 16, s * 32 + half * 16 + 16)
                    send_bt[m, half, s * 2 + core] = own[at].astype(BF16)
                    send_bt[m, half, s * 2 + 1 - core] = other[at].astype(BF16)
                burst(2, m, half).start()
        for half in range(2):
            burst(1, m, half).drain()
            cross_left(m, half).wait_send()
        for half in range(2):
            burst(2, m, half).wait()
            to_channels(m, half)
            burst(3, m, half).start()
        for half in range(2):
            burst(2, m, half).drain()

    def middle_norm(m, half):
        summed = recv_at[m, half].astype(F32).reshape(64, 8, 128)

        def over_channels(value):
            pairs = jnp.sum(value, axis=0)
            return (pairs + pltpu.roll(pairs, 4, 0)) * (1.0 / 128)

        mean_removed = summed - over_channels(summed)[None]
        variance = over_channels(mean_removed * mean_removed)
        nrm_s[...] = (mean_removed * lax.rsqrt(variance + EPS)[None]).reshape(512, 128)

    def update(m, it):
        normed = (nrm_s[pl.ds(it % 4, 128, stride=4), :] * gmid_s[m]).astype(BF16)
        return gate_s[pl.ds(it * 128, 128), :] * mm(normed, wo_ref[m], TN)

    def first_state(it):
        return pair_ref[pl.ds(it * 128, 128), :].astype(F32)

    def second_state(it):
        z = first_state(it) + update(0, it)
        z_s[pl.ds(it * 128, 128), :] = z
        return z

    def project(samples):
        weight = held["watt"][...].reshape(192, 768)
        for s in samples:
            for part in range(4):
                rows = pl.ds(s * 512 + part * 128, 128)
                value = held["tokens"][rows, :].astype(F32)
                xn_s[part * 128 : (part + 1) * 128, :] = normalize(
                    value, held["again"][...].reshape(1, 768)
                ).astype(BF16)
            proj = mm(weight, xn_s[...], NT)
            qkv_s[s] = proj[0:144].astype(BF16)
            sig_s[s] = jax.nn.sigmoid(proj[144:192])
            scores_s[s] = mm(qkv_s[s, 0:48, :], qkv_s[s, 48:96, :], TN) * (48.0**-0.5)

    def gap_first():
        for name in ("tokens", "again", "watt"):
            loads[name].wait()
        project((0, 1))

    edges(0, 0, first_state)
    pl.semaphore_wait(barrier, 30)
    burst(0, 0, 0).start()
    edges(0, 1, first_state)
    burst(0, 0, 1).start()
    triangle(0, gap_first)
    for half in range(2):
        burst(3, 0, half).wait()
        middle_norm(0, half)
        edges(1, half, second_state)
        burst(0, 1, half).start()
    for half in range(2):
        burst(3, 0, half).drain()
    triangle(1, lambda: project((2, 3)))
    for half in range(2):
        burst(3, 1, half).wait()
        middle_norm(1, half)
        for it in range(half * 4, half * 4 + 4):
            z = z_s[pl.ds(it * 128, 128), :] + update(1, it)
            out_ref[pl.ds(it * 128, 128), :] = z
            zn = normalize(z, held["bgain"][...]).astype(BF16)
            bias = mm(held["bw"][...], zn, NT).astype(BF16).astype(F32)
            heads_s[pl.ds(it, 16, stride=8), :] = bias
    to_head = Burst(
        8,
        lax.rem(col, 8),
        col // 8,
        on_col,
        lambda p: heads_s.at[pl.ds(p * 8, 8)],
        lambda p: recv_h.at[p],
        recv_h,
        heads_s.at[pl.ds(0, 120)],
        ssem.at[16],
        rsem.at[16],
    )
    to_head.start()
    for half in range(2):
        burst(3, 1, half).drain()
    to_head.wait()
    lanes = jnp.concatenate(
        [
            jnp.concatenate([recv_h[hi * 4 + lo] for lo in range(4)], axis=1)
            for hi in range(4)
        ],
        axis=0,
    ).astype(BF16)
    moved = mm(lanes, swap_s[...])
    for hi in range(4):
        for lo in range(4):
            rows_s[pl.ds(hi * 32 + lo, 8, stride=4), :] = moved[
                hi * 8 : (hi + 1) * 8, lo * 128 : (lo + 1) * 128
            ]
    bias_s[big] = jnp.concatenate(
        [rows_s[hi * 32 : (hi + 1) * 32, :] for hi in range(4)], axis=1
    ).astype(BF16)
    def along(offset):
        return remote(
            bias_s.at[big],
            bias_s.at[big],
            many_ssem.at[0, offset],
            many_rsem.at[0, offset],
            {"row": lax.rem(row + offset, 8)},
        )

    def across(owner, z):
        return remote(
            bias_s.at[owner * 8 + z],
            bias_s.at[owner * 8 + z],
            many_ssem.at[0, 8 + z],
            many_rsem.at[0, 8 + z],
            {"group": 1 - group},
        )

    across(group, row).start()
    for offset in (4, 3, 5, 2, 6, 1, 7):
        along(offset).start()
    to_tokens = Exchange(
        16,
        col,
        on_col,
        lambda p: send_o.at[p],
        lambda p: recv_o.at[p],
        many_ssem.at[1],
        many_rsem.at[1],
    )

    def attend(step, carry):
        owner = lax.rem(group + step // 2, 2)
        side = lax.rem(row // 4 + step, 2)
        part = owner * 2 + side
        for lo in range(4):
            z = side * 4 + lo

            @pl.when(jnp.logical_and(step < 2, z != row))
            def _():
                along(lax.rem(row - z + 8, 8)).wait_recv()
                across(owner, z).start()

            @pl.when(step >= 2)
            def _():
                across(owner, z).wait_recv()

        bias = bias_s[pl.ds(part * 4, 4)].reshape(128, 512).astype(F32)
        rows = pl.ds(pl.multiple_of(part * 128, 128), 128)
        for s in range(4):
            logits = scores_s[s, rows, :] + bias
            shifted = jnp.exp(logits - jnp.max(logits, axis=-1, keepdims=True))
            weights = shifted * (1.0 / jnp.sum(shifted, axis=-1, keepdims=True))
            mixed = mm(qkv_s[s, 96:144, :], weights.astype(BF16), NT)
            gated = mixed * sig_s[s, :, rows]
            ot_s[:, s * 128 : (s + 1) * 128] = gated.astype(BF16)
        moved = mm(ot_s[...], swap_s[...]).astype(BF16)
        for lo in range(4):
            target = part * 4 + lo
            send_o[target] = moved[:, lo * 128 : (lo + 1) * 128]

            @pl.when(target != col)
            def _():
                to_tokens.copy(lax.rem(target - col + 16, 16)).start()

            @pl.when(target == col)
            def _():
                to_tokens.own().start()

        return carry

    lax.fori_loop(0, 4, attend, 0)

    loop(1, 8, lambda d: along(d).wait_send())
    loop(0, 8, lambda z: across(group, z).wait_send())
    to_head.drain()
    for name in ("wout", "tgain", "wup", "wdown"):
        loads[name].wait()
    own = [
        held["tokens"][pl.ds(pl.multiple_of(s * 512 + col * 32, 32), 32), :] for s in range(4)
    ]
    own = jnp.concatenate(own, axis=0).astype(F32)
    to_tokens.own().wait()
    loop(1, 16, lambda d: to_tokens.copy(d).wait())
    first = own + mm(recv_o[...].reshape(768, 128), held["wout"][...], TN)
    xn2 = normalize(first, held["tgain"][...].reshape(1, 768)).astype(BF16)
    total = first
    for j in range(4):
        up = mm(xn2, held["wup"][:, j * 384 : (j + 1) * 384])
        side = mm(xn2, held["wup"][:, 1536 + j * 384 : 1536 + (j + 1) * 384])
        hidden = (jax.nn.silu(up) * side).astype(BF16)
        total += mm(hidden, held["wdown"][j * 384 : (j + 1) * 384, :])
    tok_ref[...] = total


def close_kernel(pair_ref, tokens_ref, pair_out, tokens_out, sem):
    copies = []
    for i in range(4):
        rows = pl.ds(i * 256, 256)
        copies.append(pltpu.make_async_copy(pair_ref.at[rows], pair_out.at[rows], sem.at[i]))
        rows = pl.ds(i * 32, 32)
        copies.append(
            pltpu.make_async_copy(tokens_ref.at[rows], tokens_out.at[rows], sem.at[4 + i])
        )
    for copy in copies:
        copy.start()
    for copy in copies:
        copy.wait()


def on_device(
    pair,
    pair_mask,
    tri_proj,
    tri_gate,
    triangle_output_weight,
    tri_gains,
    pair_bias_gain,
    bias_weight,
    tokens,
    att_gain,
    att_proj,
    att_out,
    tr_gain,
    tr_up,
    tr_down,
):
    operands = (
        pair.reshape(1024, 128),
        pair_mask,
        tri_proj,
        tri_gate,
        triangle_output_weight,
        tri_gains,
        pair_bias_gain.reshape(1, 128),
        jnp.swapaxes(bias_weight, 0, 1),
        tokens.reshape(2048, 768),
        att_gain,
        jnp.swapaxes(att_proj, 1, 2),
        att_out,
        tr_gain,
        tr_up,
        tr_down,
    )
    vmem = pl.BlockSpec(memory_space=pltpu.VMEM)
    hbm = pl.BlockSpec(memory_space=pl.ANY)
    pair_out, tokens_out = pl.pallas_call(
        block_kernel,
        out_shape=(
            jax.ShapeDtypeStruct((1024, 128), F32),
            jax.ShapeDtypeStruct((128, 768), F32),
        ),
        in_specs=[hbm] * 15,
        out_specs=(vmem, vmem),
        scratch_shapes=[pltpu.VMEM(x.shape, x.dtype) for x in operands]
        + [
            pltpu.VMEM((1024, 128), F32),
            pltpu.VMEM((1024, 128), F32),
            pltpu.VMEM((1024, 128), F32),
            pltpu.VMEM((512, 128), F32),
            pltpu.VMEM((1024, 128), F32),
            pltpu.VMEM((2, 512, 128), BF16),
            pltpu.VMEM((2, 128, 128), F32),
            pltpu.VMEM((8, 128), F32),
            pltpu.VMEM((512, 512), BF16),
            pltpu.VMEM((2, 2, 8, 128, 128), BF16),
            pltpu.VMEM((2, 2, 8, 128, 128), BF16),
            pltpu.VMEM((2, 2, 16, 2, 16, 256), BF16),
            pltpu.VMEM((2, 2, 8, 2, 2, 16, 256), BF16),
            pltpu.VMEM((2, 2, 8, 2, 16, 256), BF16),
            pltpu.VMEM((2, 8, 16, 256), BF16),
            pltpu.VMEM((2, 2, 16, 16, 256), BF16),
            pltpu.VMEM((2, 2, 16, 16, 256), BF16),
            pltpu.VMEM((2, 2, 8, 64, 128), BF16),
            pltpu.VMEM((2, 2, 8, 64, 128), BF16),
            pltpu.VMEM((128, 128), F32),
            pltpu.VMEM((16, 8, 128), F32),
            pltpu.VMEM((128, 128), F32),
            pltpu.VMEM((16, 32, 512), BF16),
            pltpu.VMEM((512, 768), BF16),
            pltpu.VMEM((4, 144, 512), BF16),
            pltpu.VMEM((4, 48, 512), F32),
            pltpu.VMEM((4, 512, 512), F32),
            pltpu.VMEM((48, 512), BF16),
            pltpu.VMEM((16, 48, 128), BF16),
            pltpu.VMEM((16, 48, 128), BF16),
            pltpu.SemaphoreType.DMA((17,)),
            pltpu.SemaphoreType.DMA((17,)),
            pltpu.SemaphoreType.DMA((6,)),
            pltpu.SemaphoreType.DMA((6,)),
            pltpu.SemaphoreType.DMA((2, 16)),
            pltpu.SemaphoreType.DMA((2, 16)),
            pltpu.SemaphoreType.DMA((15,)),
        ],
        compiler_params=pltpu.CompilerParams(
            collective_id=0, has_side_effects=True, vmem_limit_bytes=60 * 1024 * 1024
        ),
        cost_estimate=pl.CostEstimate(
            flops=6_000_000_000, bytes_accessed=15_000_000, transcendentals=3_000_000
        ),
    )(*operands)
    pair_out, tokens_out = pl.pallas_call(
        close_kernel,
        out_shape=(
            jax.ShapeDtypeStruct((1024, 128), F32),
            jax.ShapeDtypeStruct((128, 768), F32),
        ),
        in_specs=[hbm, hbm],
        out_specs=(hbm, hbm),
        scratch_shapes=[pltpu.SemaphoreType.DMA((8,))],
    )(pair_out, tokens_out)
    return pair_out.reshape(32, 32, 128), tokens_out.reshape(4, 32, 768)


def solution(mesh):
    placed = (
        P(("group", "row"), "col", None),
        P(("group", "row"), "col"),
        P(),
        P(),
        P(),
        P(),
        P(),
        P(),
        P(("group", "row"), None, None),
        P(),
        P(None, None, "col"),
        P(),
        P(),
        P(),
        P(),
    )
    return jax.shard_map(
        on_device,
        mesh=mesh,
        in_specs=placed,
        out_specs=(P(("group", "row"), "col", None), P(("group", "row"), "col", None)),
        check_vma=False,
    )
```

```python
import jax
import jax.numpy as jnp
from jax import lax
from jax.experimental import pallas as pl
from jax.experimental.pallas import tpu as pltpu
from jax.sharding import PartitionSpec as P

EPS = 1e-05
MESH = pl.DeviceIdType.MESH
F32 = jnp.float32
BF16 = jnp.bfloat16
NT = (((1,), (1,)), ((), ()))
TN = (((0,), (0,)), ((), ()))


def normalize(value, gain):
    mean = jnp.mean(value, axis=-1, keepdims=True)
    mean_removed = value - mean
    variance = jnp.mean(mean_removed * mean_removed, axis=-1, keepdims=True)
    return mean_removed * lax.rsqrt(variance + EPS) * gain


def mm(a, b, dims=(((1,), (0,)), ((), ()))):
    return lax.dot_general(a, b, dims, preferred_element_type=F32)


def swap_matrix():
    row = lax.broadcasted_iota(jnp.int32, (512, 512), 0)
    col = lax.broadcasted_iota(jnp.int32, (512, 512), 1)
    a, b, k = row >> 7, (row >> 5) & 3, row & 31
    return jnp.where((b << 7) + (a << 5) + k == col, 1.0, 0.0).astype(BF16)


def remote(src, dst, send, recv, device):
    return pltpu.make_async_remote_copy(
        src_ref=src,
        dst_ref=dst,
        send_sem=send,
        recv_sem=recv,
        device_id=device,
        device_id_type=MESH,
    )


def loop(first, last, step):
    def body(d, carry):
        step(d)
        return carry

    lax.fori_loop(first, last, body, 0)


class Exchange:
    def __init__(self, n, me, device, src, dst, send, recv):
        self.n, self.me, self.device = n, me, device
        self.src, self.dst, self.send, self.recv = src, dst, send, recv

    def copy(self, d):
        peer = lax.rem(self.me + d, self.n)
        return remote(
            self.src(peer), self.dst(self.me), self.send.at[d], self.recv.at[d], self.device(peer)
        )

    def own(self):
        return pltpu.make_async_copy(self.src(self.me), self.dst(self.me), self.recv.at[0])


def ring(at, n):
    steps = [n // 2]
    for step in range(n // 2 - 1, 0, -1):
        steps += [step, n - step]
    return [lax.rem(at + step, n) for step in steps]


def sigmoid(value):
    return 0.5 * jnp.tanh(0.5 * value) + 0.5


class Burst:
    def __init__(self, n, places, at, pair, device, src, dst, all_dst, most_src, send, recv):
        self.n, self.places, self.at, self.pair = n, places, at, pair
        self.device = device
        self.src, self.dst, self.all_dst, self.most_src = src, dst, all_dst, most_src
        self.send, self.recv = send, recv

    def start(self):
        me, other = self.pair * self.n + self.at, 1 - self.pair
        for place in self.places + [self.at]:
            for pair in (other, self.pair):
                if place is self.at and pair is self.pair:
                    continue
                remote(
                    self.src(pair * self.n + place),
                    self.dst(me),
                    self.send,
                    self.recv,
                    self.device(pair, place),
                ).start()
        pltpu.make_async_copy(self.src(me), self.dst(me), self.recv).start()

    def wait(self):
        pltpu.make_async_copy(self.all_dst, self.all_dst, self.recv).wait()

    def drain(self):
        pltpu.make_async_copy(self.most_src, self.most_src, self.send).wait()


NAMES = (
    "pair",
    "mask",
    "wp",
    "wg",
    "wo",
    "gains",
    "bgain",
    "bw",
    "tokens",
    "again",
    "watt",
    "wout",
    "tgain",
    "wup",
    "wdown",
)


def block_kernel(*refs):
    inputs = dict(zip(NAMES, refs[:15]))
    out_ref, tok_ref = refs[15:17]
    held = dict(zip(NAMES, refs[17:32]))
    (
        z_s,
        gate_s,
        flat_s,
        nrm_s,
        mix_s,
        wpt_s,
        gmid_s,
        mask_s,
        swap_s,
        send_a,
        recv_a,
        send_b,
        recv_b,
        x_left,
        x_right,
        send_bt,
        recv_bt,
        send_at,
        recv_at,
        heads_s,
        recv_h,
        rows_s,
        bias_s,
        xn_s,
        qkv_s,
        sig_s,
        scores_s,
        ot_s,
        send_o,
        recv_o,
        ssem,
        rsem,
        cross_ssem,
        cross_rsem,
        many_ssem,
        many_rsem,
        load_sem,
    ) = refs[32:]
    group, row, col = (lax.axis_index(name) for name in ("group", "row", "col"))
    big = group * 8 + row
    quad = lax.div(col, 2)
    core = lax.rem(col, 2)

    loads = {
        name: pltpu.make_async_copy(inputs[name], held[name], load_sem.at[i])
        for i, name in enumerate(NAMES)
    }
    for name in NAMES:
        loads[name].start()

    def on_col(peer):
        return {"col": peer}

    def on_quad(pair, place):
        return {"col": pair * 8 + place * 2 + core}

    def on_rows(pair, place):
        return {"group": pair, "row": place}

    row_ring = ring(row, 8)
    quad_at, quad_pair = lax.rem(quad, 4), lax.div(quad, 4)
    quad_ring = ring(quad_at, 4)

    barrier = pltpu.get_barrier_semaphore()

    def greet(d):
        place = lax.rem(big + d, 16)
        for device in (
            on_col(lax.rem(col + d, 16)),
            on_rows(lax.div(place, 8), lax.rem(place, 8)),
        ):
            pl.semaphore_signal(barrier, inc=1, device_id=device, device_id_type=MESH)

    loop(1, 16, greet)

    swap_s[...] = swap_matrix()
    pair_ref = held["pair"]
    wg_ref, wo_ref = held["wg"], held["wo"]

    for name in ("pair", "mask", "wp", "wg", "wo", "gains", "bgain", "bw"):
        loads[name].wait()
    gain_in = [held["gains"][m, 0:1, :] for m in range(2)]
    for m in range(2):
        wpt_s[m] = held["wp"][m].T
        gmid_s[m] = jnp.broadcast_to(held["gains"][m, 1:2, :], (128, 128)).T
    mask = held["mask"][...].astype(F32).astype(BF16)
    picked = []
    for lo in range(4):
        t = lax.broadcasted_iota(jnp.int32, (8, 32), 0)
        i = lax.broadcasted_iota(jnp.int32, (8, 32), 1)
        pick = jnp.where(i == t * 4 + lo, 1.0, 0.0).astype(BF16)
        k = lax.broadcasted_iota(jnp.int32, (32, 128), 0)
        lane = lax.broadcasted_iota(jnp.int32, (32, 128), 1)
        place = jnp.where(lane == lo * 32 + k, 1.0, 0.0).astype(BF16)
        picked.append(mm(mm(pick, mask).astype(BF16), place))
    mask_s[...] = picked[0] + picked[1] + picked[2] + picked[3]

    def edges(m, half, state):
        for two in range(2):
            it = half * 4 + two * 2
            z = jnp.concatenate([state(it), state(it + 1)], axis=0)
            zn = normalize(z, gain_in[m]).astype(BF16)
            proj = mm(wpt_s[m], zn, NT)
            for t in range(2):
                part = proj[:, t * 128 : (t + 1) * 128]
                keep = mask_s[it + t : it + t + 1, :]
                left = keep * sigmoid(part[0:128]) * part[128:256]
                right = keep * sigmoid(part[256:384]) * part[384:512]
                flat_s[pl.ds(two * 2 + t, 128, stride=8), :] = left
                flat_s[pl.ds(4 + two * 2 + t, 128, stride=8), :] = right
            gate_s[pl.ds(it * 128, 256), :] = sigmoid(mm(zn, wg_ref[m]))
        for s in range(8):
            send_a[m, half, s] = flat_s[pl.ds(s * 128, 128), :].astype(BF16)

    def burst(stage, m, half):
        sems = ssem.at[stage * 4 + m * 2 + half], rsem.at[stage * 4 + m * 2 + half]
        if stage == 0:
            return Burst(
                4,
                quad_ring,
                quad_at,
                quad_pair,
                on_quad,
                lambda p: send_a.at[m, half, p],
                lambda p: recv_a.at[m, half, p],
                recv_a.at[m, half],
                send_a.at[m, half, pl.ds(0, 7)],
                *sems,
            )
        if stage == 1:
            return Burst(
                8,
                row_ring,
                row,
                group,
                on_rows,
                lambda p: send_b.at[m, half, p],
                lambda p: recv_b.at[m, half, lax.div(p, 2), lax.rem(p, 2)],
                recv_b.at[m, half],
                send_b.at[m, half, pl.ds(0, 15)],
                *sems,
            )
        if stage == 2:
            return Burst(
                8,
                row_ring,
                row,
                group,
                on_rows,
                lambda p: send_bt.at[m, half, p],
                lambda p: recv_bt.at[m, half, p],
                recv_bt.at[m, half],
                send_bt.at[m, half, pl.ds(0, 15)],
                *sems,
            )
        return Burst(
            4,
            quad_ring,
            quad_at,
            quad_pair,
            on_quad,
            lambda p: send_at.at[m, half, p],
            lambda p: recv_at.at[m, half, p],
            recv_at.at[m, half],
            send_at.at[m, half, pl.ds(0, 7)],
            *sems,
        )

    partner = on_col(quad * 2 + 1 - core)

    def cross_left(m, half):
        return remote(
            recv_b.at[m, half, :, :, 0],
            x_left.at[m, half],
            cross_ssem.at[m * 2 + half],
            cross_rsem.at[m * 2 + half],
            partner,
        )

    def cross_right(half):
        return remote(
            recv_b.at[0, half, :, 1 - core, 1],
            x_right.at[half],
            cross_ssem.at[4 + half],
            cross_rsem.at[4 + half],
            partner,
        )

    def to_rows(m, half):
        for hi in range(2):
            lanes = jnp.concatenate([recv_a[m, half, hi * 4 + lo] for lo in range(4)], axis=1)
            moved = mm(lanes, swap_s[...])
            for lo in range(4):
                mix_s[pl.ds(hi * 512 + lo, 128, stride=4), :] = moved[:, lo * 128 : (lo + 1) * 128]
        both = jnp.concatenate([mix_s[0:512, :], mix_s[512:1024, :]], axis=1)
        send_b[m, half] = both.astype(BF16).reshape(16, 2, 16, 256)

    def to_channels(m, half):
        for hi in range(2):
            block = recv_bt[m, half, :, :, hi * 128 : (hi + 1) * 128]
            mix_s[hi * 256 : (hi + 1) * 256, :] = block.astype(F32).reshape(256, 128)
        for hi in range(2):
            lanes = jnp.concatenate(
                [mix_s[pl.ds(hi * 256 + lo, 64, stride=4), :] for lo in range(4)], axis=1
            )
            moved = mm(lanes.astype(BF16), swap_s[...]).astype(BF16)
            for lo in range(4):
                send_at[m, half, hi * 4 + lo] = moved[:, lo * 128 : (lo + 1) * 128]

    def triangle(m, gap):
        for half in range(2):
            burst(0, m, half).wait()
            to_rows(m, half)
            burst(1, m, half).start()
        gap()
        for half in range(2):
            burst(0, m, half).drain()
        if m == 0:
            for half in range(2):
                burst(1, m, half).wait()
                cross_left(m, half).start()
                cross_right(half).start()
            right = jnp.concatenate(
                [recv_b[m, half, s, core, 1] for s in range(8) for half in range(2)], axis=0
            )
            own = [mm(recv_b[m, half, :, :, 0].reshape(256, 256), right, NT) for half in range(2)]
            for half in range(2):
                cross_left(m, half).wait_recv()
                cross_right(half).wait_recv()
            right = jnp.concatenate(
                [x_right[half, s] for s in range(8) for half in range(2)], axis=0
            )
            for half in range(2):
                total = own[half] + mm(x_left[m, half].reshape(256, 256), right, NT)
                send_bt[m, half] = total.astype(BF16).reshape(16, 16, 256)
                burst(2, m, half).start()
            for half in range(2):
                cross_right(half).wait_send()
        else:
            right, own = [], None
            for half in range(2):
                burst(1, m, half).wait()
                cross_left(m, half).start()
                right.append(recv_b[m, half, :, :, 1].reshape(256, 256))
                term = mm(recv_b[m, half, :, :, 0].reshape(256, 256), right[half], TN)
                own = term if half == 0 else own + term
            other = None
            for half in range(2):
                cross_left(m, half).wait_recv()
                term = mm(x_left[m, half].reshape(256, 256), right[half], TN)
                other = term if half == 0 else other + term
            for half in range(2):
                for s in range(8):
                    at = slice(s * 32 + half * 16, s * 32 + half * 16 + 16)
                    send_bt[m, half, s * 2 + core] = own[at].astype(BF16)
                    send_bt[m, half, s * 2 + 1 - core] = other[at].astype(BF16)
                burst(2, m, half).start()
        for half in range(2):
            burst(1, m, half).drain()
            cross_left(m, half).wait_send()
        for half in range(2):
            burst(2, m, half).wait()
            to_channels(m, half)
            burst(3, m, half).start()
        for half in range(2):
            burst(2, m, half).drain()

    def middle_norm(m, half):
        summed = recv_at[m, half].astype(F32).reshape(64, 8, 128)

        def over_channels(value):
            pairs = jnp.sum(value, axis=0)
            return (pairs + pltpu.roll(pairs, 4, 0)) * (1.0 / 128)

        mean_removed = summed - over_channels(summed)[None]
        variance = over_channels(mean_removed * mean_removed)
        nrm_s[...] = (mean_removed * lax.rsqrt(variance + EPS)[None]).reshape(512, 128)

    def update(m, it):
        normed = (nrm_s[pl.ds(it % 4, 128, stride=4), :] * gmid_s[m]).astype(BF16)
        return gate_s[pl.ds(it * 128, 128), :] * mm(normed, wo_ref[m], TN)

    def first_state(it):
        return pair_ref[pl.ds(it * 128, 128), :].astype(F32)

    def second_state(it):
        z = first_state(it) + update(0, it)
        z_s[pl.ds(it * 128, 128), :] = z
        return z

    def project(samples):
        weight = held["watt"][...].reshape(192, 768)
        for s in samples:
            for part in range(4):
                rows = pl.ds(s * 512 + part * 128, 128)
                value = held["tokens"][rows, :].astype(F32)
                xn_s[part * 128 : (part + 1) * 128, :] = normalize(
                    value, held["again"][...].reshape(1, 768)
                ).astype(BF16)
            proj = mm(weight, xn_s[...], NT)
            qkv_s[s] = proj[0:144].astype(BF16)
            sig_s[s] = sigmoid(proj[144:192])
            scores_s[s] = mm(qkv_s[s, 0:48, :], qkv_s[s, 48:96, :], TN) * (48.0**-0.5)

    def gap_first():
        for name in ("tokens", "again", "watt"):
            loads[name].wait()
        project((0, 1))

    edges(0, 0, first_state)
    pl.semaphore_wait(barrier, 30)
    burst(0, 0, 0).start()
    edges(0, 1, first_state)
    burst(0, 0, 1).start()
    triangle(0, gap_first)
    for half in range(2):
        burst(3, 0, half).wait()
        middle_norm(0, half)
        edges(1, half, second_state)
        burst(0, 1, half).start()
    for half in range(2):
        burst(3, 0, half).drain()
    triangle(1, lambda: project((2, 3)))
    for half in range(2):
        burst(3, 1, half).wait()
        middle_norm(1, half)
        for it in range(half * 4, half * 4 + 4):
            z = z_s[pl.ds(it * 128, 128), :] + update(1, it)
            out_ref[pl.ds(it * 128, 128), :] = z
            zn = normalize(z, held["bgain"][...]).astype(BF16)
            bias = mm(held["bw"][...], zn, NT).astype(BF16).astype(F32)
            heads_s[pl.ds(it, 16, stride=8), :] = bias
    to_head = Burst(
        8,
        ring(lax.rem(col, 8), 8),
        lax.rem(col, 8),
        lax.div(col, 8),
        lambda pair, place: on_col(pair * 8 + place),
        lambda p: heads_s.at[pl.ds(p * 8, 8)],
        lambda p: recv_h.at[p],
        recv_h,
        heads_s.at[pl.ds(0, 120)],
        ssem.at[16],
        rsem.at[16],
    )
    to_head.start()
    for half in range(2):
        burst(3, 1, half).drain()
    to_head.wait()
    lanes = jnp.concatenate(
        [
            jnp.concatenate([recv_h[hi * 4 + lo] for lo in range(4)], axis=1)
            for hi in range(4)
        ],
        axis=0,
    ).astype(BF16)
    moved = mm(lanes, swap_s[...])
    for hi in range(4):
        for lo in range(4):
            rows_s[pl.ds(hi * 32 + lo, 8, stride=4), :] = moved[
                hi * 8 : (hi + 1) * 8, lo * 128 : (lo + 1) * 128
            ]
    bias_s[big] = jnp.concatenate(
        [rows_s[hi * 32 : (hi + 1) * 32, :] for hi in range(4)], axis=1
    ).astype(BF16)
    def along(offset):
        return remote(
            bias_s.at[big],
            bias_s.at[big],
            many_ssem.at[0, offset],
            many_rsem.at[0, offset],
            {"row": lax.rem(row + offset, 8)},
        )

    def across(owner, z):
        return remote(
            bias_s.at[owner * 8 + z],
            bias_s.at[owner * 8 + z],
            many_ssem.at[0, 8 + z],
            many_rsem.at[0, 8 + z],
            {"group": 1 - group},
        )

    across(group, row).start()
    for offset in (4, 3, 5, 2, 6, 1, 7):
        along(offset).start()
    to_tokens = Exchange(
        16,
        col,
        on_col,
        lambda p: send_o.at[p],
        lambda p: recv_o.at[p],
        many_ssem.at[1],
        many_rsem.at[1],
    )

    def attend(step, carry):
        owner = lax.rem(group + step // 2, 2)
        side = lax.rem(row // 4 + step, 2)
        part = owner * 2 + side
        for lo in range(4):
            z = side * 4 + lo

            @pl.when(jnp.logical_and(step < 2, z != row))
            def _():
                along(lax.rem(row - z + 8, 8)).wait_recv()
                across(owner, z).start()

            @pl.when(step >= 2)
            def _():
                across(owner, z).wait_recv()

        bias = bias_s[pl.ds(part * 4, 4)].reshape(128, 512).astype(F32)
        rows = pl.ds(pl.multiple_of(part * 128, 128), 128)
        for s in range(4):
            logits = scores_s[s, rows, :] + bias
            shifted = jnp.exp(logits - jnp.max(logits, axis=-1, keepdims=True))
            weights = shifted * (1.0 / jnp.sum(shifted, axis=-1, keepdims=True))
            mixed = mm(qkv_s[s, 96:144, :], weights.astype(BF16), NT)
            gated = mixed * sig_s[s, :, rows]
            ot_s[:, s * 128 : (s + 1) * 128] = gated.astype(BF16)
        moved = mm(ot_s[...], swap_s[...]).astype(BF16)
        for lo in range(4):
            target = part * 4 + lo
            send_o[target] = moved[:, lo * 128 : (lo + 1) * 128]

            @pl.when(target != col)
            def _():
                to_tokens.copy(lax.rem(target - col + 16, 16)).start()

            @pl.when(target == col)
            def _():
                to_tokens.own().start()

        return carry

    lax.fori_loop(0, 4, attend, 0)

    loop(1, 8, lambda d: along(d).wait_send())
    loop(0, 8, lambda z: across(group, z).wait_send())
    to_head.drain()
    for name in ("wout", "tgain", "wup", "wdown"):
        loads[name].wait()
    own = [
        held["tokens"][pl.ds(pl.multiple_of(s * 512 + col * 32, 32), 32), :] for s in range(4)
    ]
    own = jnp.concatenate(own, axis=0).astype(F32)
    to_tokens.own().wait()
    loop(1, 16, lambda d: to_tokens.copy(d).wait())
    first = own + mm(recv_o[...].reshape(768, 128), held["wout"][...], TN)
    xn2 = normalize(first, held["tgain"][...].reshape(1, 768)).astype(BF16)
    total = first
    for j in range(4):
        up = mm(xn2, held["wup"][:, j * 384 : (j + 1) * 384])
        side = mm(xn2, held["wup"][:, 1536 + j * 384 : 1536 + (j + 1) * 384])
        hidden = (up * sigmoid(up) * side).astype(BF16)
        total += mm(hidden, held["wdown"][j * 384 : (j + 1) * 384, :])
    tok_ref[...] = total


def close_kernel(pair_ref, tokens_ref, pair_out, tokens_out, pair_s, tokens_s, in_sem, out_sem):
    copies = []
    for i in range(4):
        for n, (src, held, dst, size) in enumerate(
            ((pair_ref, pair_s, pair_out, 256), (tokens_ref, tokens_s, tokens_out, 32))
        ):
            rows = pl.ds(i * size, size)
            copies.append(
                (
                    pltpu.make_async_copy(src.at[rows], held.at[rows], in_sem.at[n, i]),
                    pltpu.make_async_copy(held.at[rows], dst.at[rows], out_sem.at[n, i]),
                )
            )
    for first, _ in copies:
        first.start()
    for first, second in copies:
        first.wait()
        second.start()
    for _, second in copies:
        second.wait()


def on_device(
    pair,
    pair_mask,
    tri_proj,
    tri_gate,
    triangle_output_weight,
    tri_gains,
    pair_bias_gain,
    bias_weight,
    tokens,
    att_gain,
    att_proj,
    att_out,
    tr_gain,
    tr_up,
    tr_down,
):
    operands = (
        pair.reshape(1024, 128),
        pair_mask,
        tri_proj,
        tri_gate,
        triangle_output_weight,
        tri_gains,
        pair_bias_gain.reshape(1, 128),
        jnp.swapaxes(bias_weight, 0, 1),
        tokens.reshape(2048, 768),
        att_gain,
        jnp.swapaxes(att_proj, 1, 2),
        att_out,
        tr_gain,
        tr_up,
        tr_down,
    )
    vmem = pl.BlockSpec(memory_space=pltpu.VMEM)
    hbm = pl.BlockSpec(memory_space=pl.ANY)
    pair_out, tokens_out = pl.pallas_call(
        block_kernel,
        out_shape=(
            jax.ShapeDtypeStruct((1024, 128), F32),
            jax.ShapeDtypeStruct((128, 768), F32),
        ),
        in_specs=[hbm] * 15,
        out_specs=(vmem, vmem),
        scratch_shapes=[pltpu.VMEM(x.shape, x.dtype) for x in operands]
        + [
            pltpu.VMEM((1024, 128), F32),
            pltpu.VMEM((1024, 128), F32),
            pltpu.VMEM((1024, 128), F32),
            pltpu.VMEM((512, 128), F32),
            pltpu.VMEM((1024, 128), F32),
            pltpu.VMEM((2, 512, 128), BF16),
            pltpu.VMEM((2, 128, 128), F32),
            pltpu.VMEM((8, 128), F32),
            pltpu.VMEM((512, 512), BF16),
            pltpu.VMEM((2, 2, 8, 128, 128), BF16),
            pltpu.VMEM((2, 2, 8, 128, 128), BF16),
            pltpu.VMEM((2, 2, 16, 2, 16, 256), BF16),
            pltpu.VMEM((2, 2, 8, 2, 2, 16, 256), BF16),
            pltpu.VMEM((2, 2, 8, 2, 16, 256), BF16),
            pltpu.VMEM((2, 8, 16, 256), BF16),
            pltpu.VMEM((2, 2, 16, 16, 256), BF16),
            pltpu.VMEM((2, 2, 16, 16, 256), BF16),
            pltpu.VMEM((2, 2, 8, 64, 128), BF16),
            pltpu.VMEM((2, 2, 8, 64, 128), BF16),
            pltpu.VMEM((128, 128), F32),
            pltpu.VMEM((16, 8, 128), F32),
            pltpu.VMEM((128, 128), F32),
            pltpu.VMEM((16, 32, 512), BF16),
            pltpu.VMEM((512, 768), BF16),
            pltpu.VMEM((4, 144, 512), BF16),
            pltpu.VMEM((4, 48, 512), F32),
            pltpu.VMEM((4, 512, 512), F32),
            pltpu.VMEM((48, 512), BF16),
            pltpu.VMEM((16, 48, 128), BF16),
            pltpu.VMEM((16, 48, 128), BF16),
            pltpu.SemaphoreType.DMA((17,)),
            pltpu.SemaphoreType.DMA((17,)),
            pltpu.SemaphoreType.DMA((6,)),
            pltpu.SemaphoreType.DMA((6,)),
            pltpu.SemaphoreType.DMA((2, 16)),
            pltpu.SemaphoreType.DMA((2, 16)),
            pltpu.SemaphoreType.DMA((15,)),
        ],
        compiler_params=pltpu.CompilerParams(
            collective_id=0, has_side_effects=True, vmem_limit_bytes=60 * 1024 * 1024
        ),
        cost_estimate=pl.CostEstimate(
            flops=6_000_000_000, bytes_accessed=15_000_000, transcendentals=3_000_000
        ),
    )(*operands)
    pair_out, tokens_out = pl.pallas_call(
        close_kernel,
        out_shape=(
            jax.ShapeDtypeStruct((1024, 128), F32),
            jax.ShapeDtypeStruct((128, 768), F32),
        ),
        in_specs=[hbm, hbm],
        out_specs=(hbm, hbm),
        scratch_shapes=[
            pltpu.VMEM((1024, 128), F32),
            pltpu.VMEM((128, 768), F32),
            pltpu.SemaphoreType.DMA((2, 4)),
            pltpu.SemaphoreType.DMA((2, 4)),
        ],
        compiler_params=pltpu.CompilerParams(vmem_limit_bytes=60 * 1024 * 1024),
    )(pair_out, tokens_out)
    return pair_out.reshape(32, 32, 128), tokens_out.reshape(4, 32, 768)


def solution(mesh):
    placed = (
        P(("group", "row"), "col", None),
        P(("group", "row"), "col"),
        P(),
        P(),
        P(),
        P(),
        P(),
        P(),
        P(("group", "row"), None, None),
        P(),
        P(None, None, "col"),
        P(),
        P(),
        P(),
        P(),
    )
    return jax.shard_map(
        on_device,
        mesh=mesh,
        in_specs=placed,
        out_specs=(P(("group", "row"), "col", None), P(("group", "row"), "col", None)),
        check_vma=False,
    )
```

```python
import jax
import jax.numpy as jnp
from jax import lax
from jax.experimental import pallas as pl
from jax.experimental.pallas import tpu as pltpu
from jax.sharding import PartitionSpec as P

EPS = 1e-05
MESH = pl.DeviceIdType.MESH
F32 = jnp.float32
BF16 = jnp.bfloat16
NT = (((1,), (1,)), ((), ()))
TN = (((0,), (0,)), ((), ()))


def normalize(value, gain):
    mean = jnp.mean(value, axis=-1, keepdims=True)
    mean_removed = value - mean
    variance = jnp.mean(mean_removed * mean_removed, axis=-1, keepdims=True)
    return mean_removed * lax.rsqrt(variance + EPS) * gain


def mm(a, b, dims=(((1,), (0,)), ((), ()))):
    return lax.dot_general(a, b, dims, preferred_element_type=F32)


def swap_matrix():
    row = lax.broadcasted_iota(jnp.int32, (512, 512), 0)
    col = lax.broadcasted_iota(jnp.int32, (512, 512), 1)
    a, b, k = row >> 7, (row >> 5) & 3, row & 31
    return jnp.where((b << 7) + (a << 5) + k == col, 1.0, 0.0).astype(BF16)


def remote(src, dst, send, recv, device):
    return pltpu.make_async_remote_copy(
        src_ref=src,
        dst_ref=dst,
        send_sem=send,
        recv_sem=recv,
        device_id=device,
        device_id_type=MESH,
    )


def loop(first, last, step):
    def body(d, carry):
        step(d)
        return carry

    lax.fori_loop(first, last, body, 0)


class Exchange:
    def __init__(self, n, me, device, src, dst, send, recv):
        self.n, self.me, self.device = n, me, device
        self.src, self.dst, self.send, self.recv = src, dst, send, recv

    def copy(self, d):
        peer = lax.rem(self.me + d, self.n)
        return remote(
            self.src(peer), self.dst(self.me), self.send.at[d], self.recv.at[d], self.device(peer)
        )

    def own(self):
        return pltpu.make_async_copy(self.src(self.me), self.dst(self.me), self.recv.at[0])


def ring(at, n):
    steps = [n // 2]
    for step in range(n // 2 - 1, 0, -1):
        steps += [step, n - step]
    return [lax.rem(at + step, n) for step in steps]


def sigmoid(value):
    return 0.5 * jnp.tanh(0.5 * value) + 0.5


class Burst:
    def __init__(self, peers, me, src, dst, all_dst, most_src, send, recv):
        self.peers, self.me = peers, me
        self.src, self.dst, self.all_dst, self.most_src = src, dst, all_dst, most_src
        self.send, self.recv = send, recv

    def start(self):
        for peer, device in self.peers:
            remote(self.src(peer), self.dst(self.me), self.send, self.recv, device).start()
        pltpu.make_async_copy(self.src(self.me), self.dst(self.me), self.recv).start()

    def wait(self):
        pltpu.make_async_copy(self.all_dst, self.all_dst, self.recv).wait()

    def drain(self):
        pltpu.make_async_copy(self.most_src, self.most_src, self.send).wait()


NAMES = (
    "pair",
    "mask",
    "wp",
    "wg",
    "wo",
    "gains",
    "bgain",
    "bw",
    "tokens",
    "again",
    "watt",
    "wout",
    "tgain",
    "wup",
    "wdown",
)


def block_kernel(*refs):
    inputs = dict(zip(NAMES, refs[:15]))
    out_ref, tok_ref = refs[15:17]
    held = dict(zip(NAMES, refs[17:32]))
    (
        z_s,
        gate_s,
        flat_s,
        nrm_s,
        mix_s,
        wpt_s,
        gmid_s,
        mask_s,
        swap_s,
        send_a,
        recv_a,
        send_b,
        recv_b,
        x_left,
        x_right,
        send_bt,
        recv_bt,
        send_at,
        recv_at,
        heads_s,
        recv_h,
        rows_s,
        bias_s,
        xn_s,
        qkv_s,
        sig_s,
        scores_s,
        ot_s,
        send_o,
        recv_o,
        ssem,
        rsem,
        cross_ssem,
        cross_rsem,
        many_ssem,
        many_rsem,
        load_sem,
    ) = refs[32:]
    group, row, col = (lax.axis_index(name) for name in ("group", "row", "col"))
    big = group * 8 + row
    quad = lax.div(col, 2)
    core = lax.rem(col, 2)

    loads = {
        name: pltpu.make_async_copy(inputs[name], held[name], load_sem.at[i])
        for i, name in enumerate(NAMES)
    }
    for name in NAMES:
        loads[name].start()

    def on_col(peer):
        return {"col": peer}

    quad_y = lax.rem(quad, 4)
    chip_x = lax.div(quad, 4) * 2 + group
    plane_me = group * 8 + quad
    xs = [lax.rem(chip_x + d, 4) for d in range(4)]
    ys = [lax.rem(quad_y + d, 4) for d in range(4)]
    plane = []
    far = ((2, 2), (2, 1), (2, 3), (1, 2), (3, 2), (1, 1), (3, 3), (1, 3), (3, 1))
    for dx, dy in far + ((2, 0), (0, 2), (1, 0), (3, 0), (0, 1), (0, 3)):
        high, low = lax.div(xs[dx], 2), lax.rem(xs[dx], 2)
        place = high * 4 + ys[dy]
        plane.append((low * 8 + place, {"group": low, "col": place * 2 + core}))
    line = [(z, {"row": z}) for z in ring(row, 8)]
    heads = [
        (pair * 8 + place, on_col(pair * 8 + place))
        for place in ring(lax.rem(col, 8), 8) + [lax.rem(col, 8)]
        for pair in (1 - lax.div(col, 8), lax.div(col, 8))
    ][:-1]

    barrier = pltpu.get_barrier_semaphore()

    def greet(device):
        pl.semaphore_signal(barrier, inc=1, device_id=device, device_id_type=MESH)

    loop(1, 16, lambda d: greet(on_col(lax.rem(col + d, 16))))
    loop(1, 8, lambda d: greet({"row": lax.rem(row + d, 8)}))
    loop(0, 8, lambda place: greet({"group": 1 - group, "col": place * 2 + core}))

    swap_s[...] = swap_matrix()
    pair_ref = held["pair"]
    wg_ref, wo_ref = held["wg"], held["wo"]

    for name in ("pair", "mask", "wp", "wg", "wo", "gains", "bgain", "bw"):
        loads[name].wait()
    gain_in = [held["gains"][m, 0:1, :] for m in range(2)]
    for m in range(2):
        wpt_s[m] = held["wp"][m].T
        gmid_s[m] = jnp.broadcast_to(held["gains"][m, 1:2, :], (128, 128)).T
    mask = held["mask"][...].astype(F32).astype(BF16)
    picked = []
    for lo in range(4):
        t = lax.broadcasted_iota(jnp.int32, (8, 32), 0)
        i = lax.broadcasted_iota(jnp.int32, (8, 32), 1)
        pick = jnp.where(i == t * 4 + lo, 1.0, 0.0).astype(BF16)
        k = lax.broadcasted_iota(jnp.int32, (32, 128), 0)
        lane = lax.broadcasted_iota(jnp.int32, (32, 128), 1)
        place = jnp.where(lane == lo * 32 + k, 1.0, 0.0).astype(BF16)
        picked.append(mm(mm(pick, mask).astype(BF16), place))
    mask_s[...] = picked[0] + picked[1] + picked[2] + picked[3]

    def edges(m, half, state):
        for two in range(2):
            it = half * 4 + two * 2
            z = jnp.concatenate([state(it), state(it + 1)], axis=0)
            zn = normalize(z, gain_in[m]).astype(BF16)
            proj = mm(wpt_s[m], zn, NT)
            for t in range(2):
                part = proj[:, t * 128 : (t + 1) * 128]
                keep = mask_s[it + t : it + t + 1, :]
                left = keep * sigmoid(part[0:128]) * part[128:256]
                right = keep * sigmoid(part[256:384]) * part[384:512]
                flat_s[pl.ds(two * 2 + t, 128, stride=8), :] = left
                flat_s[pl.ds(4 + two * 2 + t, 128, stride=8), :] = right
            gate_s[pl.ds(it * 128, 256), :] = sigmoid(mm(zn, wg_ref[m]))
        for block in range(16):
            send_a[m, half, block] = flat_s[pl.ds(block * 64, 64), :].astype(BF16)

    def burst(stage, m, half):
        sems = ssem.at[stage * 4 + m * 2 + half], rsem.at[stage * 4 + m * 2 + half]
        if stage == 0:
            return Burst(
                plane,
                plane_me,
                lambda p: send_a.at[m, half, p],
                lambda p: recv_a.at[m, half, p],
                recv_a.at[m, half],
                send_a.at[m, half, pl.ds(0, 15)],
                *sems,
            )
        if stage == 1:
            return Burst(
                line,
                row,
                lambda p: send_b.at[m, half, p],
                lambda p: recv_b.at[m, half, lax.div(p, 2), lax.rem(p, 2)],
                recv_b.at[m, half],
                send_b.at[m, half, pl.ds(0, 7)],
                *sems,
            )
        if stage == 2:
            return Burst(
                line,
                row,
                lambda p: send_bt.at[m, half, p],
                lambda p: recv_bt.at[m, half, p],
                recv_bt.at[m, half],
                send_bt.at[m, half, pl.ds(0, 7)],
                *sems,
            )
        return Burst(
            plane,
            plane_me,
            lambda p: send_at.at[m, half, p],
            lambda p: recv_at.at[m, half, p],
            recv_at.at[m, half],
            send_at.at[m, half, pl.ds(0, 15)],
            *sems,
        )

    partner = on_col(quad * 2 + 1 - core)

    def cross_left(m, half):
        return remote(
            recv_b.at[m, half, :, :, :, 0],
            x_left.at[m, half],
            cross_ssem.at[m * 2 + half],
            cross_rsem.at[m * 2 + half],
            partner,
        )

    def cross_right(half):
        return remote(
            recv_b.at[0, half, :, 1 - core, :, 1],
            x_right.at[half],
            cross_ssem.at[4 + half],
            cross_rsem.at[4 + half],
            partner,
        )

    def to_rows(m, half):
        for hi in range(2):
            lanes = jnp.concatenate(
                [
                    jnp.concatenate(
                        [recv_a[m, half, pair * 8 + hi * 4 + lo] for lo in range(4)], axis=1
                    )
                    for pair in range(2)
                ],
                axis=0,
            )
            moved = mm(lanes, swap_s[...])
            for lo in range(4):
                mix_s[pl.ds(hi * 512 + lo, 128, stride=4), :] = moved[:, lo * 128 : (lo + 1) * 128]
        both = jnp.concatenate([mix_s[0:512, :], mix_s[512:1024, :]], axis=1)
        both = both.astype(BF16).reshape(2, 8, 2, 16, 256)
        for pair in range(2):
            send_b[m, half, :, pair] = both[pair]

    def to_channels(m, half):
        for hi in range(2):
            for pair in range(2):
                block = recv_bt[m, half, :, pair, :, hi * 128 : (hi + 1) * 128]
                at = hi * 256 + pair * 128
                mix_s[at : at + 128, :] = block.astype(F32).reshape(128, 128)
        for hi in range(2):
            lanes = jnp.concatenate(
                [mix_s[pl.ds(hi * 256 + lo, 64, stride=4), :] for lo in range(4)], axis=1
            )
            moved = mm(lanes.astype(BF16), swap_s[...]).astype(BF16)
            for lo in range(4):
                part = moved[:, lo * 128 : (lo + 1) * 128]
                for pair in range(2):
                    send_at[m, half, pair * 8 + hi * 4 + lo] = part[pair * 32 : pair * 32 + 32]

    def triangle(m, gap):
        for half in range(2):
            burst(0, m, half).wait()
            to_rows(m, half)
            burst(1, m, half).start()
        gap()
        for half in range(2):
            burst(0, m, half).drain()
        if m == 0:
            for half in range(2):
                burst(1, m, half).wait()
                cross_left(m, half).start()
                cross_right(half).start()
            right = jnp.concatenate(
                [
                    recv_b[m, half, s % 4, core, s // 4, 1]
                    for s in range(8)
                    for half in range(2)
                ],
                axis=0,
            )
            own = [
                mm(recv_b[m, half, :, :, :, 0].reshape(256, 256), right, NT) for half in range(2)
            ]
            for half in range(2):
                cross_left(m, half).wait_recv()
                cross_right(half).wait_recv()
            right = jnp.concatenate(
                [x_right[half, s % 4, s // 4] for s in range(8) for half in range(2)], axis=0
            )
            for half in range(2):
                total = own[half] + mm(x_left[m, half].reshape(256, 256), right, NT)
                send_bt[m, half] = total.astype(BF16).reshape(8, 2, 16, 256)
                burst(2, m, half).start()
            for half in range(2):
                cross_right(half).wait_send()
        else:
            right, own = [], None
            for half in range(2):
                burst(1, m, half).wait()
                cross_left(m, half).start()
                right.append(recv_b[m, half, :, :, :, 1].reshape(256, 256))
                term = mm(recv_b[m, half, :, :, :, 0].reshape(256, 256), right[half], TN)
                own = term if half == 0 else own + term
            other = None
            for half in range(2):
                cross_left(m, half).wait_recv()
                term = mm(x_left[m, half].reshape(256, 256), right[half], TN)
                other = term if half == 0 else other + term
            for half in range(2):
                for s in range(8):
                    at = slice(s * 32 + half * 16, s * 32 + half * 16 + 16)
                    z = s % 4 * 2
                    send_bt[m, half, z + core, s // 4] = own[at].astype(BF16)
                    send_bt[m, half, z + 1 - core, s // 4] = other[at].astype(BF16)
                burst(2, m, half).start()
        for half in range(2):
            burst(1, m, half).drain()
            cross_left(m, half).wait_send()
        for half in range(2):
            burst(2, m, half).wait()
            to_channels(m, half)
            burst(3, m, half).start()
        for half in range(2):
            burst(2, m, half).drain()

    def middle_norm(m, half):
        summed = recv_at[m, half].astype(F32).reshape(64, 8, 128)

        def over_channels(value):
            pairs = jnp.sum(value, axis=0)
            return (pairs + pltpu.roll(pairs, 4, 0)) * (1.0 / 128)

        mean_removed = summed - over_channels(summed)[None]
        variance = over_channels(mean_removed * mean_removed)
        nrm_s[...] = (mean_removed * lax.rsqrt(variance + EPS)[None]).reshape(512, 128)

    def update(m, it):
        normed = (nrm_s[pl.ds(it % 4, 128, stride=4), :] * gmid_s[m]).astype(BF16)
        return gate_s[pl.ds(it * 128, 128), :] * mm(normed, wo_ref[m], TN)

    def first_state(it):
        return pair_ref[pl.ds(it * 128, 128), :].astype(F32)

    def second_state(it):
        z = first_state(it) + update(0, it)
        z_s[pl.ds(it * 128, 128), :] = z
        return z

    def project(samples):
        weight = held["watt"][...].reshape(192, 768)
        for s in samples:
            for part in range(4):
                rows = pl.ds(s * 512 + part * 128, 128)
                value = held["tokens"][rows, :].astype(F32)
                xn_s[part * 128 : (part + 1) * 128, :] = normalize(
                    value, held["again"][...].reshape(1, 768)
                ).astype(BF16)
            proj = mm(weight, xn_s[...], NT)
            qkv_s[s] = proj[0:144].astype(BF16)
            sig_s[s] = sigmoid(proj[144:192])
            scores_s[s] = mm(qkv_s[s, 0:48, :], qkv_s[s, 48:96, :], TN) * (48.0**-0.5)

    def gap_first():
        for name in ("tokens", "again", "watt"):
            loads[name].wait()
        project((0, 1))

    edges(0, 0, first_state)
    pl.semaphore_wait(barrier, 30)
    burst(0, 0, 0).start()
    edges(0, 1, first_state)
    burst(0, 0, 1).start()
    triangle(0, gap_first)
    for half in range(2):
        burst(3, 0, half).wait()
        middle_norm(0, half)
        edges(1, half, second_state)
        burst(0, 1, half).start()
    for half in range(2):
        burst(3, 0, half).drain()
    triangle(1, lambda: project((2, 3)))
    for half in range(2):
        burst(3, 1, half).wait()
        middle_norm(1, half)
        for it in range(half * 4, half * 4 + 4):
            z = z_s[pl.ds(it * 128, 128), :] + update(1, it)
            out_ref[pl.ds(it * 128, 128), :] = z
            zn = normalize(z, held["bgain"][...]).astype(BF16)
            bias = mm(held["bw"][...], zn, NT).astype(BF16).astype(F32)
            heads_s[pl.ds(it, 16, stride=8), :] = bias
    to_head = Burst(
        heads,
        col,
        lambda p: heads_s.at[pl.ds(p * 8, 8)],
        lambda p: recv_h.at[p],
        recv_h,
        heads_s.at[pl.ds(0, 120)],
        ssem.at[16],
        rsem.at[16],
    )
    to_head.start()
    for half in range(2):
        burst(3, 1, half).drain()
    to_head.wait()
    lanes = jnp.concatenate(
        [
            jnp.concatenate([recv_h[hi * 4 + lo] for lo in range(4)], axis=1)
            for hi in range(4)
        ],
        axis=0,
    ).astype(BF16)
    moved = mm(lanes, swap_s[...])
    for hi in range(4):
        for lo in range(4):
            rows_s[pl.ds(hi * 32 + lo, 8, stride=4), :] = moved[
                hi * 8 : (hi + 1) * 8, lo * 128 : (lo + 1) * 128
            ]
    bias_s[big] = jnp.concatenate(
        [rows_s[hi * 32 : (hi + 1) * 32, :] for hi in range(4)], axis=1
    ).astype(BF16)
    def along(offset):
        return remote(
            bias_s.at[big],
            bias_s.at[big],
            many_ssem.at[0, offset],
            many_rsem.at[0, offset],
            {"row": lax.rem(row + offset, 8)},
        )

    def across(owner, z):
        return remote(
            bias_s.at[owner * 8 + z],
            bias_s.at[owner * 8 + z],
            many_ssem.at[0, 8 + z],
            many_rsem.at[0, 8 + z],
            {"group": 1 - group},
        )

    across(group, row).start()
    for offset in (4, 3, 5, 2, 6, 1, 7):
        along(offset).start()
    to_tokens = Exchange(
        16,
        col,
        on_col,
        lambda p: send_o.at[p],
        lambda p: recv_o.at[p],
        many_ssem.at[1],
        many_rsem.at[1],
    )

    def attend(step, carry):
        owner = lax.rem(group + step // 2, 2)
        side = lax.rem(row // 4 + step, 2)
        part = owner * 2 + side
        for lo in range(4):
            z = side * 4 + lo

            @pl.when(jnp.logical_and(step < 2, z != row))
            def _():
                along(lax.rem(row - z + 8, 8)).wait_recv()
                across(owner, z).start()

            @pl.when(step >= 2)
            def _():
                across(owner, z).wait_recv()

        bias = bias_s[pl.ds(part * 4, 4)].reshape(128, 512).astype(F32)
        rows = pl.ds(pl.multiple_of(part * 128, 128), 128)
        for s in range(4):
            logits = scores_s[s, rows, :] + bias
            shifted = jnp.exp(logits - jnp.max(logits, axis=-1, keepdims=True))
            weights = shifted * (1.0 / jnp.sum(shifted, axis=-1, keepdims=True))
            mixed = mm(qkv_s[s, 96:144, :], weights.astype(BF16), NT)
            gated = mixed * sig_s[s, :, rows]
            ot_s[:, s * 128 : (s + 1) * 128] = gated.astype(BF16)
        moved = mm(ot_s[...], swap_s[...]).astype(BF16)
        for lo in range(4):
            target = part * 4 + lo
            send_o[target] = moved[:, lo * 128 : (lo + 1) * 128]

            @pl.when(target != col)
            def _():
                to_tokens.copy(lax.rem(target - col + 16, 16)).start()

            @pl.when(target == col)
            def _():
                to_tokens.own().start()

        return carry

    lax.fori_loop(0, 4, attend, 0)

    loop(1, 8, lambda d: along(d).wait_send())
    loop(0, 8, lambda z: across(group, z).wait_send())
    to_head.drain()
    for name in ("wout", "tgain", "wup", "wdown"):
        loads[name].wait()
    own = [
        held["tokens"][pl.ds(pl.multiple_of(s * 512 + col * 32, 32), 32), :] for s in range(4)
    ]
    own = jnp.concatenate(own, axis=0).astype(F32)
    to_tokens.own().wait()
    loop(1, 16, lambda d: to_tokens.copy(d).wait())
    first = own + mm(recv_o[...].reshape(768, 128), held["wout"][...], TN)
    xn2 = normalize(first, held["tgain"][...].reshape(1, 768)).astype(BF16)
    total = first
    for j in range(4):
        up = mm(xn2, held["wup"][:, j * 384 : (j + 1) * 384])
        side = mm(xn2, held["wup"][:, 1536 + j * 384 : 1536 + (j + 1) * 384])
        hidden = (up * sigmoid(up) * side).astype(BF16)
        total += mm(hidden, held["wdown"][j * 384 : (j + 1) * 384, :])
    tok_ref[...] = total


def close_kernel(pair_ref, tokens_ref, pair_out, tokens_out, pair_s, tokens_s, in_sem, out_sem):
    copies = []
    for i in range(4):
        for n, (src, held, dst, size) in enumerate(
            ((pair_ref, pair_s, pair_out, 256), (tokens_ref, tokens_s, tokens_out, 32))
        ):
            rows = pl.ds(i * size, size)
            copies.append(
                (
                    pltpu.make_async_copy(src.at[rows], held.at[rows], in_sem.at[n, i]),
                    pltpu.make_async_copy(held.at[rows], dst.at[rows], out_sem.at[n, i]),
                )
            )
    for first, _ in copies:
        first.start()
    for first, second in copies:
        first.wait()
        second.start()
    for _, second in copies:
        second.wait()


def on_device(
    pair,
    pair_mask,
    tri_proj,
    tri_gate,
    triangle_output_weight,
    tri_gains,
    pair_bias_gain,
    bias_weight,
    tokens,
    att_gain,
    att_proj,
    att_out,
    tr_gain,
    tr_up,
    tr_down,
):
    operands = (
        pair.reshape(1024, 128),
        pair_mask,
        tri_proj,
        tri_gate,
        triangle_output_weight,
        tri_gains,
        pair_bias_gain.reshape(1, 128),
        jnp.swapaxes(bias_weight, 0, 1),
        tokens.reshape(2048, 768),
        att_gain,
        jnp.swapaxes(att_proj, 1, 2),
        att_out,
        tr_gain,
        tr_up,
        tr_down,
    )
    vmem = pl.BlockSpec(memory_space=pltpu.VMEM)
    hbm = pl.BlockSpec(memory_space=pl.ANY)
    pair_out, tokens_out = pl.pallas_call(
        block_kernel,
        out_shape=(
            jax.ShapeDtypeStruct((1024, 128), F32),
            jax.ShapeDtypeStruct((128, 768), F32),
        ),
        in_specs=[hbm] * 15,
        out_specs=(vmem, vmem),
        scratch_shapes=[pltpu.VMEM(x.shape, x.dtype) for x in operands]
        + [
            pltpu.VMEM((1024, 128), F32),
            pltpu.VMEM((1024, 128), F32),
            pltpu.VMEM((1024, 128), F32),
            pltpu.VMEM((512, 128), F32),
            pltpu.VMEM((1024, 128), F32),
            pltpu.VMEM((2, 512, 128), BF16),
            pltpu.VMEM((2, 128, 128), F32),
            pltpu.VMEM((8, 128), F32),
            pltpu.VMEM((512, 512), BF16),
            pltpu.VMEM((2, 2, 16, 64, 128), BF16),
            pltpu.VMEM((2, 2, 16, 64, 128), BF16),
            pltpu.VMEM((2, 2, 8, 2, 2, 16, 256), BF16),
            pltpu.VMEM((2, 2, 4, 2, 2, 2, 16, 256), BF16),
            pltpu.VMEM((2, 2, 4, 2, 2, 16, 256), BF16),
            pltpu.VMEM((2, 4, 2, 16, 256), BF16),
            pltpu.VMEM((2, 2, 8, 2, 16, 256), BF16),
            pltpu.VMEM((2, 2, 8, 2, 16, 256), BF16),
            pltpu.VMEM((2, 2, 16, 32, 128), BF16),
            pltpu.VMEM((2, 2, 16, 32, 128), BF16),
            pltpu.VMEM((128, 128), F32),
            pltpu.VMEM((16, 8, 128), F32),
            pltpu.VMEM((128, 128), F32),
            pltpu.VMEM((16, 32, 512), BF16),
            pltpu.VMEM((512, 768), BF16),
            pltpu.VMEM((4, 144, 512), BF16),
            pltpu.VMEM((4, 48, 512), F32),
            pltpu.VMEM((4, 512, 512), F32),
            pltpu.VMEM((48, 512), BF16),
            pltpu.VMEM((16, 48, 128), BF16),
            pltpu.VMEM((16, 48, 128), BF16),
            pltpu.SemaphoreType.DMA((17,)),
            pltpu.SemaphoreType.DMA((17,)),
            pltpu.SemaphoreType.DMA((6,)),
            pltpu.SemaphoreType.DMA((6,)),
            pltpu.SemaphoreType.DMA((2, 16)),
            pltpu.SemaphoreType.DMA((2, 16)),
            pltpu.SemaphoreType.DMA((15,)),
        ],
        compiler_params=pltpu.CompilerParams(
            collective_id=0, has_side_effects=True, vmem_limit_bytes=60 * 1024 * 1024
        ),
        cost_estimate=pl.CostEstimate(
            flops=6_000_000_000, bytes_accessed=15_000_000, transcendentals=3_000_000
        ),
    )(*operands)
    pair_out, tokens_out = pl.pallas_call(
        close_kernel,
        out_shape=(
            jax.ShapeDtypeStruct((1024, 128), F32),
            jax.ShapeDtypeStruct((128, 768), F32),
        ),
        in_specs=[hbm, hbm],
        out_specs=(hbm, hbm),
        scratch_shapes=[
            pltpu.VMEM((1024, 128), F32),
            pltpu.VMEM((128, 768), F32),
            pltpu.SemaphoreType.DMA((2, 4)),
            pltpu.SemaphoreType.DMA((2, 4)),
        ],
        compiler_params=pltpu.CompilerParams(vmem_limit_bytes=60 * 1024 * 1024),
    )(pair_out, tokens_out)
    return pair_out.reshape(32, 32, 128), tokens_out.reshape(4, 32, 768)


def solution(mesh):
    placed = (
        P(("group", "row"), "col", None),
        P(("group", "row"), "col"),
        P(),
        P(),
        P(),
        P(),
        P(),
        P(),
        P(("group", "row"), None, None),
        P(),
        P(None, None, "col"),
        P(),
        P(),
        P(),
        P(),
    )
    return jax.shard_map(
        on_device,
        mesh=mesh,
        in_specs=placed,
        out_specs=(P(("group", "row"), "col", None), P(("group", "row"), "col", None)),
        check_vma=False,
    )
```

```python
import jax
import jax.numpy as jnp
from jax import lax
from jax.experimental import pallas as pl
from jax.experimental.pallas import tpu as pltpu
from jax.sharding import PartitionSpec as P

EPS = 1e-05
MESH = pl.DeviceIdType.MESH
F32 = jnp.float32
BF16 = jnp.bfloat16
NT = (((1,), (1,)), ((), ()))
TN = (((0,), (0,)), ((), ()))


def normalize(value, gain):
    mean = jnp.mean(value, axis=-1, keepdims=True)
    mean_removed = value - mean
    variance = jnp.mean(mean_removed * mean_removed, axis=-1, keepdims=True)
    return mean_removed * lax.rsqrt(variance + EPS) * gain


def mm(a, b, dims=(((1,), (0,)), ((), ()))):
    return lax.dot_general(a, b, dims, preferred_element_type=F32)


def swap_matrix():
    row = lax.broadcasted_iota(jnp.int32, (512, 512), 0)
    col = lax.broadcasted_iota(jnp.int32, (512, 512), 1)
    a, b, k = row >> 7, (row >> 5) & 3, row & 31
    return jnp.where((b << 7) + (a << 5) + k == col, 1.0, 0.0).astype(BF16)


def remote(src, dst, send, recv, device):
    return pltpu.make_async_remote_copy(
        src_ref=src,
        dst_ref=dst,
        send_sem=send,
        recv_sem=recv,
        device_id=device,
        device_id_type=MESH,
    )


def loop(first, last, step):
    def body(d, carry):
        step(d)
        return carry

    lax.fori_loop(first, last, body, 0)


class Exchange:
    def __init__(self, n, me, device, src, dst, send, recv):
        self.n, self.me, self.device = n, me, device
        self.src, self.dst, self.send, self.recv = src, dst, send, recv

    def copy(self, d):
        peer = lax.rem(self.me + d, self.n)
        return remote(
            self.src(peer), self.dst(self.me), self.send.at[d], self.recv.at[d], self.device(peer)
        )

    def own(self):
        return pltpu.make_async_copy(self.src(self.me), self.dst(self.me), self.recv.at[0])


def ring(at, n):
    steps = [n // 2]
    for step in range(n // 2 - 1, 0, -1):
        steps += [step, n - step]
    return [lax.rem(at + step, n) for step in steps]


def sigmoid(value):
    return 0.5 * jnp.tanh(0.5 * value) + 0.5


class Burst:
    def __init__(self, peers, me, src, dst, all_dst, most_src, send, recv):
        self.peers, self.me = peers, me
        self.src, self.dst, self.all_dst, self.most_src = src, dst, all_dst, most_src
        self.send, self.recv = send, recv

    def start(self):
        for peer, device in self.peers:
            remote(self.src(peer), self.dst(self.me), self.send, self.recv, device).start()
        pltpu.make_async_copy(self.src(self.me), self.dst(self.me), self.recv).start()

    def wait(self):
        pltpu.make_async_copy(self.all_dst, self.all_dst, self.recv).wait()

    def drain(self):
        pltpu.make_async_copy(self.most_src, self.most_src, self.send).wait()


NAMES = (
    "pair",
    "mask",
    "wp",
    "wg",
    "wo",
    "gains",
    "bgain",
    "bw",
    "tokens",
    "again",
    "watt",
    "wout",
    "tgain",
    "wup",
    "wdown",
)


def block_kernel(*refs):
    inputs = dict(zip(NAMES, refs[:15]))
    out_ref, tok_ref = refs[15:17]
    held = dict(zip(NAMES, refs[17:32]))
    (
        z_s,
        gate_s,
        flat_s,
        nrm_s,
        mix_s,
        wpt_s,
        gmid_s,
        mask_s,
        swap_s,
        send_a,
        recv_a,
        send_b,
        recv_b,
        x_left,
        x_right,
        send_bt,
        recv_bt,
        send_at,
        recv_at,
        heads_s,
        recv_h,
        rows_s,
        bias_s,
        xn_s,
        qkv_s,
        sig_s,
        scores_s,
        ot_s,
        send_o,
        recv_o,
        ssem,
        rsem,
        cross_ssem,
        cross_rsem,
        many_ssem,
        many_rsem,
        load_sem,
    ) = refs[32:]
    group, row, col = (lax.axis_index(name) for name in ("group", "row", "col"))
    big = group * 8 + row
    quad = lax.div(col, 2)
    core = lax.rem(col, 2)

    loads = {
        name: pltpu.make_async_copy(inputs[name], held[name], load_sem.at[i])
        for i, name in enumerate(NAMES)
    }
    early = ("pair", "wp", "mask", "gains", "wg")
    late = ("wo", "bgain", "bw", "tokens", "again", "watt", "wout", "tgain", "wup", "wdown")
    for name in early:
        loads[name].start()

    def on_col(peer):
        return {"col": peer}

    quad_y = lax.rem(quad, 4)
    chip_x = lax.div(quad, 4) * 2 + group
    plane_me = group * 8 + quad
    xs = [lax.rem(chip_x + d, 4) for d in range(4)]
    ys = [lax.rem(quad_y + d, 4) for d in range(4)]
    plane = []
    far = ((2, 2), (2, 1), (2, 3), (1, 2), (3, 2), (1, 1), (3, 3), (1, 3), (3, 1))
    for dx, dy in far + ((2, 0), (0, 2), (1, 0), (3, 0), (0, 1), (0, 3)):
        high, low = lax.div(xs[dx], 2), lax.rem(xs[dx], 2)
        place = high * 4 + ys[dy]
        plane.append((low * 8 + place, {"group": low, "col": place * 2 + core}))
    line = [(z, {"row": z}) for z in ring(row, 8)]
    heads = [
        (pair * 8 + place, on_col(pair * 8 + place))
        for place in ring(lax.rem(col, 8), 8) + [lax.rem(col, 8)]
        for pair in (1 - lax.div(col, 8), lax.div(col, 8))
    ][:-1]

    barrier = pltpu.get_barrier_semaphore()

    def greet(device):
        pl.semaphore_signal(barrier, inc=1, device_id=device, device_id_type=MESH)

    loop(1, 16, lambda d: greet(on_col(lax.rem(col + d, 16))))
    loop(1, 8, lambda d: greet({"row": lax.rem(row + d, 8)}))
    loop(0, 8, lambda place: greet({"group": 1 - group, "col": place * 2 + core}))

    swap_s[...] = swap_matrix()
    pair_ref = held["pair"]
    wg_ref, wo_ref = held["wg"], held["wo"]

    for name in early:
        loads[name].wait()
    for name in late:
        loads[name].start()
    gain_in = [held["gains"][m, 0:1, :] for m in range(2)]
    wpt_s[0] = held["wp"][0].T
    mask = held["mask"][...].astype(F32).astype(BF16)
    picked = []
    for lo in range(4):
        t = lax.broadcasted_iota(jnp.int32, (8, 32), 0)
        i = lax.broadcasted_iota(jnp.int32, (8, 32), 1)
        pick = jnp.where(i == t * 4 + lo, 1.0, 0.0).astype(BF16)
        k = lax.broadcasted_iota(jnp.int32, (32, 128), 0)
        lane = lax.broadcasted_iota(jnp.int32, (32, 128), 1)
        place = jnp.where(lane == lo * 32 + k, 1.0, 0.0).astype(BF16)
        picked.append(mm(mm(pick, mask).astype(BF16), place))
    mask_s[...] = picked[0] + picked[1] + picked[2] + picked[3]

    def edges(m, half, state):
        for two in range(2):
            it = half * 4 + two * 2
            z = jnp.concatenate([state(it), state(it + 1)], axis=0)
            zn = normalize(z, gain_in[m]).astype(BF16)
            proj = mm(wpt_s[m], zn, NT)
            for t in range(2):
                part = proj[:, t * 128 : (t + 1) * 128]
                keep = mask_s[it + t : it + t + 1, :]
                left = keep * sigmoid(part[0:128]) * part[128:256]
                right = keep * sigmoid(part[256:384]) * part[384:512]
                flat_s[pl.ds(two * 2 + t, 128, stride=8), :] = left
                flat_s[pl.ds(4 + two * 2 + t, 128, stride=8), :] = right
            gate_s[pl.ds(it * 128, 256), :] = sigmoid(mm(zn, wg_ref[m]))
        for block in range(16):
            send_a[m, half, block] = flat_s[pl.ds(block * 64, 64), :].astype(BF16)

    def burst(stage, m, half):
        sems = ssem.at[stage * 4 + m * 2 + half], rsem.at[stage * 4 + m * 2 + half]
        if stage == 0:
            return Burst(
                plane,
                plane_me,
                lambda p: send_a.at[m, half, p],
                lambda p: recv_a.at[m, half, p],
                recv_a.at[m, half],
                send_a.at[m, half, pl.ds(0, 15)],
                *sems,
            )
        if stage == 1:
            return Burst(
                line,
                row,
                lambda p: send_b.at[m, half, p],
                lambda p: recv_b.at[m, half, lax.div(p, 2), lax.rem(p, 2)],
                recv_b.at[m, half],
                send_b.at[m, half, pl.ds(0, 7)],
                *sems,
            )
        if stage == 2:
            return Burst(
                line,
                row,
                lambda p: send_bt.at[m, half, p],
                lambda p: recv_bt.at[m, half, p],
                recv_bt.at[m, half],
                send_bt.at[m, half, pl.ds(0, 7)],
                *sems,
            )
        return Burst(
            plane,
            plane_me,
            lambda p: send_at.at[m, half, p],
            lambda p: recv_at.at[m, half, p],
            recv_at.at[m, half],
            send_at.at[m, half, pl.ds(0, 15)],
            *sems,
        )

    partner = on_col(quad * 2 + 1 - core)

    def cross_left(m, half):
        return remote(
            recv_b.at[m, half, :, :, :, 0],
            x_left.at[m, half],
            cross_ssem.at[m * 2 + half],
            cross_rsem.at[m * 2 + half],
            partner,
        )

    def cross_right(half):
        return remote(
            recv_b.at[0, half, :, 1 - core, :, 1],
            x_right.at[half],
            cross_ssem.at[4 + half],
            cross_rsem.at[4 + half],
            partner,
        )

    def to_rows(m, half):
        for hi in range(2):
            lanes = jnp.concatenate(
                [
                    jnp.concatenate(
                        [recv_a[m, half, pair * 8 + hi * 4 + lo] for lo in range(4)], axis=1
                    )
                    for pair in range(2)
                ],
                axis=0,
            )
            moved = mm(lanes, swap_s[...])
            for lo in range(4):
                mix_s[pl.ds(hi * 512 + lo, 128, stride=4), :] = moved[:, lo * 128 : (lo + 1) * 128]
        both = jnp.concatenate([mix_s[0:512, :], mix_s[512:1024, :]], axis=1)
        both = both.astype(BF16).reshape(2, 8, 2, 16, 256)
        for pair in range(2):
            send_b[m, half, :, pair] = both[pair]

    def to_channels(m, half):
        for hi in range(2):
            for pair in range(2):
                block = recv_bt[m, half, :, pair, :, hi * 128 : (hi + 1) * 128]
                at = hi * 256 + pair * 128
                mix_s[at : at + 128, :] = block.astype(F32).reshape(128, 128)
        for hi in range(2):
            lanes = jnp.concatenate(
                [mix_s[pl.ds(hi * 256 + lo, 64, stride=4), :] for lo in range(4)], axis=1
            )
            moved = mm(lanes.astype(BF16), swap_s[...]).astype(BF16)
            for lo in range(4):
                part = moved[:, lo * 128 : (lo + 1) * 128]
                for pair in range(2):
                    send_at[m, half, pair * 8 + hi * 4 + lo] = part[pair * 32 : pair * 32 + 32]

    def triangle(m, gap):
        for half in range(2):
            burst(0, m, half).wait()
            to_rows(m, half)
            burst(1, m, half).start()
        gap()
        for half in range(2):
            burst(0, m, half).drain()
        if m == 0:
            for half in range(2):
                burst(1, m, half).wait()
                cross_left(m, half).start()
                cross_right(half).start()
            right = jnp.concatenate(
                [
                    recv_b[m, half, s % 4, core, s // 4, 1]
                    for s in range(8)
                    for half in range(2)
                ],
                axis=0,
            )
            own = [
                mm(recv_b[m, half, :, :, :, 0].reshape(256, 256), right, NT) for half in range(2)
            ]
            for half in range(2):
                cross_left(m, half).wait_recv()
                cross_right(half).wait_recv()
            right = jnp.concatenate(
                [x_right[half, s % 4, s // 4] for s in range(8) for half in range(2)], axis=0
            )
            for half in range(2):
                total = own[half] + mm(x_left[m, half].reshape(256, 256), right, NT)
                send_bt[m, half] = total.astype(BF16).reshape(8, 2, 16, 256)
                burst(2, m, half).start()
            for half in range(2):
                cross_right(half).wait_send()
        else:
            right, own = [], None
            for half in range(2):
                burst(1, m, half).wait()
                cross_left(m, half).start()
                right.append(recv_b[m, half, :, :, :, 1].reshape(256, 256))
                term = mm(recv_b[m, half, :, :, :, 0].reshape(256, 256), right[half], TN)
                own = term if half == 0 else own + term
            other = None
            for half in range(2):
                cross_left(m, half).wait_recv()
                term = mm(x_left[m, half].reshape(256, 256), right[half], TN)
                other = term if half == 0 else other + term
            for half in range(2):
                for s in range(8):
                    at = slice(s * 32 + half * 16, s * 32 + half * 16 + 16)
                    z = s % 4 * 2
                    send_bt[m, half, z + core, s // 4] = own[at].astype(BF16)
                    send_bt[m, half, z + 1 - core, s // 4] = other[at].astype(BF16)
                burst(2, m, half).start()
        for half in range(2):
            burst(1, m, half).drain()
            cross_left(m, half).wait_send()
        for half in range(2):
            burst(2, m, half).wait()
            to_channels(m, half)
            burst(3, m, half).start()
        for half in range(2):
            burst(2, m, half).drain()

    def middle_norm(m, half):
        summed = recv_at[m, half].astype(F32).reshape(64, 8, 128)

        def over_channels(value):
            pairs = jnp.sum(value, axis=0)
            return (pairs + pltpu.roll(pairs, 4, 0)) * (1.0 / 128)

        mean_removed = summed - over_channels(summed)[None]
        variance = over_channels(mean_removed * mean_removed)
        nrm_s[...] = (mean_removed * lax.rsqrt(variance + EPS)[None]).reshape(512, 128)

    def update(m, it):
        normed = (nrm_s[pl.ds(it % 4, 128, stride=4), :] * gmid_s[m]).astype(BF16)
        return gate_s[pl.ds(it * 128, 128), :] * mm(normed, wo_ref[m], TN)

    def first_state(it):
        return pair_ref[pl.ds(it * 128, 128), :].astype(F32)

    def second_state(it):
        z = first_state(it) + update(0, it)
        z_s[pl.ds(it * 128, 128), :] = z
        return z

    def project(samples):
        weight = held["watt"][...].reshape(192, 768)
        for s in samples:
            for part in range(4):
                rows = pl.ds(s * 512 + part * 128, 128)
                value = held["tokens"][rows, :].astype(F32)
                xn_s[part * 128 : (part + 1) * 128, :] = normalize(
                    value, held["again"][...].reshape(1, 768)
                ).astype(BF16)
            proj = mm(weight, xn_s[...], NT)
            qkv_s[s] = proj[0:144].astype(BF16)
            sig_s[s] = sigmoid(proj[144:192])
            scores_s[s] = mm(qkv_s[s, 0:48, :], qkv_s[s, 48:96, :], TN) * (48.0**-0.5)

    def gap_first():
        wpt_s[1] = held["wp"][1].T
        for m in range(2):
            gmid_s[m] = jnp.broadcast_to(held["gains"][m, 1:2, :], (128, 128)).T
        heads_s[...] = jnp.zeros_like(heads_s)
        for name in ("wo", "bgain", "bw", "tokens", "again", "watt"):
            loads[name].wait()
        project((0, 1))

    edges(0, 0, first_state)
    pl.semaphore_wait(barrier, 30)
    burst(0, 0, 0).start()
    edges(0, 1, first_state)
    burst(0, 0, 1).start()
    triangle(0, gap_first)
    for half in range(2):
        burst(3, 0, half).wait()
        middle_norm(0, half)
        edges(1, half, second_state)
        burst(0, 1, half).start()
    for half in range(2):
        burst(3, 0, half).drain()

    def to_head(half):
        return Burst(
            heads,
            col,
            lambda p: heads_s.at[half, pl.ds(p * 8, 8)],
            lambda p: recv_h.at[half, p],
            recv_h.at[half],
            heads_s.at[half, pl.ds(0, 120)],
            ssem.at[16 + half],
            rsem.at[16 + half],
        )

    triangle(1, lambda: project((2, 3)))
    for half in range(2):
        burst(3, 1, half).wait()
        middle_norm(1, half)
        for it in range(half * 4, half * 4 + 4):
            z = z_s[pl.ds(it * 128, 128), :] + update(1, it)
            out_ref[pl.ds(it * 128, 128), :] = z
            zn = normalize(z, held["bgain"][...]).astype(BF16)
            bias = mm(held["bw"][...], zn, NT).astype(BF16).astype(F32)
            heads_s[half, pl.ds(it % 4, 16, stride=8), :] = bias
        to_head(half).start()

    def along(half, offset):
        block = bias_s.at[big, pl.ds(half * 16, 16)]
        return remote(
            block,
            block,
            many_ssem.at[half, offset],
            many_rsem.at[half, offset],
            {"row": lax.rem(row + offset, 8)},
        )

    def across(half, owner, z):
        block = bias_s.at[owner * 8 + z, pl.ds(half * 16, 16)]
        return remote(
            block,
            block,
            many_ssem.at[half, 8 + z],
            many_rsem.at[half, 8 + z],
            {"group": 1 - group},
        )

    for half in range(2):
        to_head(half).wait()
        lanes = jnp.concatenate(
            [
                jnp.concatenate([recv_h[half, hi * 4 + lo] for lo in range(4)], axis=1)
                for hi in range(4)
            ],
            axis=0,
        ).astype(BF16)
        moved = mm(lanes, swap_s[...])
        for hi in range(4):
            for lo in range(4):
                rows_s[pl.ds(hi * 32 + lo, 8, stride=4), :] = moved[
                    hi * 8 : (hi + 1) * 8, lo * 128 : (lo + 1) * 128
                ]
        bias_s[big, half * 16 : (half + 1) * 16, :] = jnp.concatenate(
            [rows_s[hi * 32 : hi * 32 + 16, :] for hi in range(4)], axis=1
        ).astype(BF16)
        for offset in (4, 3, 5, 2, 6, 1, 7):
            along(half, offset).start()
        across(half, group, row).start()
    for half in range(2):
        burst(3, 1, half).drain()

    to_tokens = Exchange(
        16,
        col,
        on_col,
        lambda p: send_o.at[p],
        lambda p: recv_o.at[p],
        many_ssem.at[2],
        many_rsem.at[2],
    )

    def attend(step, carry):
        owner = lax.rem(group + step // 2, 2)
        side = lax.rem(row // 4 + step, 2)
        part = owner * 2 + side
        for lo in range(4):
            z = side * 4 + lo

            @pl.when(jnp.logical_and(step < 2, z != row))
            def _():
                for half in range(2):
                    along(half, lax.rem(row - z + 8, 8)).wait_recv()
                    across(half, owner, z).start()

            @pl.when(step >= 2)
            def _():
                for half in range(2):
                    across(half, owner, z).wait_recv()

        bias = bias_s[pl.ds(part * 4, 4)].reshape(128, 512).astype(F32)
        rows = pl.ds(pl.multiple_of(part * 128, 128), 128)
        for s in range(4):
            logits = scores_s[s, rows, :] + bias
            shifted = jnp.exp(logits - jnp.max(logits, axis=-1, keepdims=True))
            weights = shifted * (1.0 / jnp.sum(shifted, axis=-1, keepdims=True))
            mixed = mm(qkv_s[s, 96:144, :], weights.astype(BF16), NT)
            gated = mixed * sig_s[s, :, rows]
            ot_s[:, s * 128 : (s + 1) * 128] = gated.astype(BF16)
        moved = mm(ot_s[...], swap_s[...]).astype(BF16)
        for lo in range(4):
            target = part * 4 + lo
            send_o[target] = moved[:, lo * 128 : (lo + 1) * 128]

            @pl.when(target != col)
            def _():
                to_tokens.copy(lax.rem(target - col + 16, 16)).start()

            @pl.when(target == col)
            def _():
                to_tokens.own().start()

        return carry

    lax.fori_loop(0, 4, attend, 0)

    for half in range(2):
        loop(1, 8, lambda d: along(half, d).wait_send())
        loop(0, 8, lambda z: across(half, group, z).wait_send())
        to_head(half).drain()
    for name in ("wout", "tgain", "wup", "wdown"):
        loads[name].wait()
    own = [
        held["tokens"][pl.ds(pl.multiple_of(s * 512 + col * 32, 32), 32), :] for s in range(4)
    ]
    own = jnp.concatenate(own, axis=0).astype(F32)
    to_tokens.own().wait()
    loop(1, 16, lambda d: to_tokens.copy(d).wait())
    first = own + mm(recv_o[...].reshape(768, 128), held["wout"][...], TN)
    xn2 = normalize(first, held["tgain"][...].reshape(1, 768)).astype(BF16)
    total = first
    for j in range(4):
        up = mm(xn2, held["wup"][:, j * 384 : (j + 1) * 384])
        side = mm(xn2, held["wup"][:, 1536 + j * 384 : 1536 + (j + 1) * 384])
        hidden = (up * sigmoid(up) * side).astype(BF16)
        total += mm(hidden, held["wdown"][j * 384 : (j + 1) * 384, :])
    tok_ref[...] = total


def close_kernel(pair_ref, tokens_ref, pair_out, tokens_out, pair_s, tokens_s, in_sem, out_sem):
    copies = []
    for i in range(4):
        for n, (src, held, dst, size) in enumerate(
            ((pair_ref, pair_s, pair_out, 256), (tokens_ref, tokens_s, tokens_out, 32))
        ):
            rows = pl.ds(i * size, size)
            copies.append(
                (
                    pltpu.make_async_copy(src.at[rows], held.at[rows], in_sem.at[n, i]),
                    pltpu.make_async_copy(held.at[rows], dst.at[rows], out_sem.at[n, i]),
                )
            )
    for first, _ in copies:
        first.start()
    for first, second in copies:
        first.wait()
        second.start()
    for _, second in copies:
        second.wait()


def on_device(
    pair,
    pair_mask,
    tri_proj,
    tri_gate,
    triangle_output_weight,
    tri_gains,
    pair_bias_gain,
    bias_weight,
    tokens,
    att_gain,
    att_proj,
    att_out,
    tr_gain,
    tr_up,
    tr_down,
):
    operands = (
        pair.reshape(1024, 128),
        pair_mask,
        tri_proj,
        tri_gate,
        triangle_output_weight,
        tri_gains,
        pair_bias_gain.reshape(1, 128),
        jnp.swapaxes(bias_weight, 0, 1),
        tokens.reshape(2048, 768),
        att_gain,
        jnp.swapaxes(att_proj, 1, 2),
        att_out,
        tr_gain,
        tr_up,
        tr_down,
    )
    vmem = pl.BlockSpec(memory_space=pltpu.VMEM)
    hbm = pl.BlockSpec(memory_space=pl.ANY)
    pair_out, tokens_out = pl.pallas_call(
        block_kernel,
        out_shape=(
            jax.ShapeDtypeStruct((1024, 128), F32),
            jax.ShapeDtypeStruct((128, 768), F32),
        ),
        in_specs=[hbm] * 15,
        out_specs=(vmem, vmem),
        scratch_shapes=[pltpu.VMEM(x.shape, x.dtype) for x in operands]
        + [
            pltpu.VMEM((1024, 128), F32),
            pltpu.VMEM((1024, 128), F32),
            pltpu.VMEM((1024, 128), F32),
            pltpu.VMEM((512, 128), F32),
            pltpu.VMEM((1024, 128), F32),
            pltpu.VMEM((2, 512, 128), BF16),
            pltpu.VMEM((2, 128, 128), F32),
            pltpu.VMEM((8, 128), F32),
            pltpu.VMEM((512, 512), BF16),
            pltpu.VMEM((2, 2, 16, 64, 128), BF16),
            pltpu.VMEM((2, 2, 16, 64, 128), BF16),
            pltpu.VMEM((2, 2, 8, 2, 2, 16, 256), BF16),
            pltpu.VMEM((2, 2, 4, 2, 2, 2, 16, 256), BF16),
            pltpu.VMEM((2, 2, 4, 2, 2, 16, 256), BF16),
            pltpu.VMEM((2, 4, 2, 16, 256), BF16),
            pltpu.VMEM((2, 2, 8, 2, 16, 256), BF16),
            pltpu.VMEM((2, 2, 8, 2, 16, 256), BF16),
            pltpu.VMEM((2, 2, 16, 32, 128), BF16),
            pltpu.VMEM((2, 2, 16, 32, 128), BF16),
            pltpu.VMEM((2, 128, 128), F32),
            pltpu.VMEM((2, 16, 8, 128), F32),
            pltpu.VMEM((128, 128), F32),
            pltpu.VMEM((16, 32, 512), BF16),
            pltpu.VMEM((512, 768), BF16),
            pltpu.VMEM((4, 144, 512), BF16),
            pltpu.VMEM((4, 48, 512), F32),
            pltpu.VMEM((4, 512, 512), F32),
            pltpu.VMEM((48, 512), BF16),
            pltpu.VMEM((16, 48, 128), BF16),
            pltpu.VMEM((16, 48, 128), BF16),
            pltpu.SemaphoreType.DMA((18,)),
            pltpu.SemaphoreType.DMA((18,)),
            pltpu.SemaphoreType.DMA((6,)),
            pltpu.SemaphoreType.DMA((6,)),
            pltpu.SemaphoreType.DMA((3, 16)),
            pltpu.SemaphoreType.DMA((3, 16)),
            pltpu.SemaphoreType.DMA((15,)),
        ],
        compiler_params=pltpu.CompilerParams(
            collective_id=0, has_side_effects=True, vmem_limit_bytes=60 * 1024 * 1024
        ),
        cost_estimate=pl.CostEstimate(
            flops=6_000_000_000, bytes_accessed=15_000_000, transcendentals=3_000_000
        ),
    )(*operands)
    pair_out, tokens_out = pl.pallas_call(
        close_kernel,
        out_shape=(
            jax.ShapeDtypeStruct((1024, 128), F32),
            jax.ShapeDtypeStruct((128, 768), F32),
        ),
        in_specs=[hbm, hbm],
        out_specs=(hbm, hbm),
        scratch_shapes=[
            pltpu.VMEM((1024, 128), F32),
            pltpu.VMEM((128, 768), F32),
            pltpu.SemaphoreType.DMA((2, 4)),
            pltpu.SemaphoreType.DMA((2, 4)),
        ],
        compiler_params=pltpu.CompilerParams(vmem_limit_bytes=60 * 1024 * 1024),
    )(pair_out, tokens_out)
    return pair_out.reshape(32, 32, 128), tokens_out.reshape(4, 32, 768)


def solution(mesh):
    placed = (
        P(("group", "row"), "col", None),
        P(("group", "row"), "col"),
        P(),
        P(),
        P(),
        P(),
        P(),
        P(),
        P(("group", "row"), None, None),
        P(),
        P(None, None, "col"),
        P(),
        P(),
        P(),
        P(),
    )
    return jax.shard_map(
        on_device,
        mesh=mesh,
        in_specs=placed,
        out_specs=(P(("group", "row"), "col", None), P(("group", "row"), "col", None)),
        check_vma=False,
    )
```

```python
import jax
import jax.numpy as jnp
from jax import lax
from jax.experimental import pallas as pl
from jax.experimental.pallas import tpu as pltpu
from jax.sharding import PartitionSpec as P

EPS = 1e-05
MESH = pl.DeviceIdType.MESH
F32 = jnp.float32
BF16 = jnp.bfloat16
NT = (((1,), (1,)), ((), ()))
TN = (((0,), (0,)), ((), ()))


def normalize(value, gain):
    mean = jnp.mean(value, axis=-1, keepdims=True)
    mean_removed = value - mean
    variance = jnp.mean(mean_removed * mean_removed, axis=-1, keepdims=True)
    return mean_removed * lax.rsqrt(variance + EPS) * gain


def mm(a, b, dims=(((1,), (0,)), ((), ()))):
    return lax.dot_general(a, b, dims, preferred_element_type=F32)


def swap_matrix():
    row = lax.broadcasted_iota(jnp.int32, (512, 512), 0)
    col = lax.broadcasted_iota(jnp.int32, (512, 512), 1)
    a, b, k = row >> 7, (row >> 5) & 3, row & 31
    return jnp.where((b << 7) + (a << 5) + k == col, 1.0, 0.0).astype(BF16)


def remote(src, dst, send, recv, device):
    return pltpu.make_async_remote_copy(
        src_ref=src,
        dst_ref=dst,
        send_sem=send,
        recv_sem=recv,
        device_id=device,
        device_id_type=MESH,
    )


def loop(first, last, step):
    def body(d, carry):
        step(d)
        return carry

    lax.fori_loop(first, last, body, 0)


class Exchange:
    def __init__(self, n, me, device, src, dst, send, recv):
        self.n, self.me, self.device = n, me, device
        self.src, self.dst, self.send, self.recv = src, dst, send, recv

    def copy(self, d):
        peer = lax.rem(self.me + d, self.n)
        return remote(
            self.src(peer), self.dst(self.me), self.send.at[d], self.recv.at[d], self.device(peer)
        )

    def own(self):
        return pltpu.make_async_copy(self.src(self.me), self.dst(self.me), self.recv.at[0])


def ring(at, n):
    steps = [n // 2]
    for step in range(n // 2 - 1, 0, -1):
        steps += [step, n - step]
    return [lax.rem(at + step, n) for step in steps]


def sigmoid(value):
    return 0.5 * jnp.tanh(0.5 * value) + 0.5


class Burst:
    def __init__(self, peers, me, src, dst, all_dst, most_src, send, recv):
        self.peers, self.me = peers, me
        self.src, self.dst, self.all_dst, self.most_src = src, dst, all_dst, most_src
        self.send, self.recv = send, recv

    def start(self):
        for peer, device in self.peers:
            remote(self.src(peer), self.dst(self.me), self.send, self.recv, device).start()
        pltpu.make_async_copy(self.src(self.me), self.dst(self.me), self.recv).start()

    def wait(self):
        pltpu.make_async_copy(self.all_dst, self.all_dst, self.recv).wait()

    def drain(self):
        pltpu.make_async_copy(self.most_src, self.most_src, self.send).wait()


NAMES = (
    "pair",
    "mask",
    "wp",
    "wg",
    "wo",
    "gains",
    "bgain",
    "bw",
    "tokens",
    "again",
    "watt",
    "wout",
    "tgain",
    "wup",
    "wdown",
)


def block_kernel(*refs):
    inputs = dict(zip(NAMES, refs[:15]))
    out_ref, tok_ref = refs[15:17]
    held = dict(zip(NAMES, refs[17:32]))
    (
        z_s,
        gate_s,
        flat_s,
        nrm_s,
        mix_s,
        wpt_s,
        gmid_s,
        mask_s,
        swap_s,
        send_z,
        recv_z,
        send_a,
        recv_a,
        send_b,
        recv_b,
        x_left,
        x_right,
        send_bt,
        recv_bt,
        send_at,
        recv_at,
        heads_s,
        recv_h,
        rows_s,
        bias_s,
        xn_s,
        qkv_s,
        sig_s,
        scores_s,
        ot_s,
        send_o,
        recv_o,
        ssem,
        rsem,
        cross_ssem,
        cross_rsem,
        many_ssem,
        many_rsem,
        load_sem,
    ) = refs[32:]
    group, row, col = (lax.axis_index(name) for name in ("group", "row", "col"))
    big = group * 8 + row
    quad = lax.div(col, 2)
    core = lax.rem(col, 2)

    loads = {
        name: pltpu.make_async_copy(inputs[name], held[name], load_sem.at[i])
        for i, name in enumerate(NAMES)
    }
    early = ("pair", "wp", "mask", "gains", "wg")
    late = ("wo", "bgain", "bw", "tokens", "again", "watt", "wout", "tgain", "wup", "wdown")
    for name in early:
        loads[name].start()

    def on_col(peer):
        return {"col": peer}

    quad_y = lax.rem(quad, 4)
    chip_x = lax.div(quad, 4) * 2 + group
    plane_me = group * 8 + quad
    xs = [lax.rem(chip_x + d, 4) for d in range(4)]
    ys = [lax.rem(quad_y + d, 4) for d in range(4)]
    plane = []
    far = ((2, 2), (2, 1), (2, 3), (1, 2), (3, 2), (1, 1), (3, 3), (1, 3), (3, 1))
    for dx, dy in far + ((2, 0), (0, 2), (1, 0), (3, 0), (0, 1), (0, 3)):
        high, low = lax.div(xs[dx], 2), lax.rem(xs[dx], 2)
        place = high * 4 + ys[dy]
        plane.append((low * 8 + place, {"group": low, "col": place * 2 + core}))
    line = [(z, {"row": z}) for z in ring(row, 8)]
    heads = [
        (pair * 8 + place, on_col(pair * 8 + place))
        for place in ring(lax.rem(col, 8), 8) + [lax.rem(col, 8)]
        for pair in (1 - lax.div(col, 8), lax.div(col, 8))
    ][:-1]

    barrier = pltpu.get_barrier_semaphore()

    def greet(device):
        pl.semaphore_signal(barrier, inc=1, device_id=device, device_id_type=MESH)

    loop(1, 16, lambda d: greet(on_col(lax.rem(col + d, 16))))
    loop(1, 8, lambda d: greet({"row": lax.rem(row + d, 8)}))
    loop(0, 8, lambda place: greet({"group": 1 - group, "col": place * 2 + core}))

    swap_s[...] = swap_matrix()
    pair_ref = held["pair"]
    wg_ref, wo_ref = held["wg"], held["wo"]

    for name in early:
        loads[name].wait()
    for name in late:
        loads[name].start()
    gain_in = [held["gains"][m, 0:1, :] for m in range(2)]
    wpt_s[0] = held["wp"][0].T
    mask = held["mask"][...].astype(F32).astype(BF16)
    picked = []
    for lo in range(4):
        t = lax.broadcasted_iota(jnp.int32, (8, 32), 0)
        i = lax.broadcasted_iota(jnp.int32, (8, 32), 1)
        pick = jnp.where(i == t * 4 + lo, 1.0, 0.0).astype(BF16)
        k = lax.broadcasted_iota(jnp.int32, (32, 128), 0)
        lane = lax.broadcasted_iota(jnp.int32, (32, 128), 1)
        place = jnp.where(lane == lo * 32 + k, 1.0, 0.0).astype(BF16)
        picked.append(mm(mm(pick, mask).astype(BF16), place))
    mask_s[...] = picked[0] + picked[1] + picked[2] + picked[3]

    def edges(m, half, state):
        for two in range(2):
            it = half * 4 + two * 2
            z = jnp.concatenate([state(it), state(it + 1)], axis=0)
            zn = normalize(z, gain_in[m]).astype(BF16)
            proj = mm(wpt_s[m], zn, NT)
            for t in range(2):
                part = proj[:, t * 128 : (t + 1) * 128]
                keep = mask_s[it + t : it + t + 1, :]
                left = keep * sigmoid(part[0:128]) * part[128:256]
                right = keep * sigmoid(part[256:384]) * part[384:512]
                flat_s[pl.ds(two * 2 + t, 128, stride=8), :] = left
                flat_s[pl.ds(4 + two * 2 + t, 128, stride=8), :] = right
            gate_s[pl.ds(it * 128, 256), :] = sigmoid(mm(zn, wg_ref[m]))
        if half == 0:
            for z in range(8):
                rows = [flat_s[pl.ds(block * 64 + z * 8, 8), :] for block in range(16)]
                send_z[m, z] = jnp.concatenate(rows, axis=0).astype(BF16)
        else:
            for block in range(16):
                send_a[m, half, block] = flat_s[pl.ds(block * 64, 64), :].astype(BF16)

    def burst(stage, m, half):
        sems = ssem.at[stage * 4 + m * 2 + half], rsem.at[stage * 4 + m * 2 + half]
        if stage == 0:
            return Burst(
                plane,
                plane_me,
                lambda p: send_a.at[m, half, p],
                lambda p: recv_a.at[m, half, p],
                recv_a.at[m, half],
                send_a.at[m, half, pl.ds(0, 15)],
                *sems,
            )
        if stage == 1 and half == 0:
            return Burst(
                line,
                row,
                lambda p: send_z.at[m, p],
                lambda p: recv_z.at[m, p],
                recv_z.at[m],
                send_z.at[m, pl.ds(0, 7)],
                *sems,
            )
        if stage == 1:
            return Burst(
                line,
                row,
                lambda p: send_b.at[m, p],
                lambda p: recv_b.at[m, half, lax.div(p, 2), lax.rem(p, 2)],
                recv_b.at[m, half],
                send_b.at[m, pl.ds(0, 7)],
                *sems,
            )
        if stage == 2:
            return Burst(
                line,
                row,
                lambda p: send_bt.at[m, half, p],
                lambda p: recv_bt.at[m, half, p],
                recv_bt.at[m, half],
                send_bt.at[m, half, pl.ds(0, 7)],
                *sems,
            )
        return Burst(
            plane,
            plane_me,
            lambda p: send_at.at[m, half, p],
            lambda p: recv_at.at[m, half, p],
            recv_at.at[m, half],
            send_at.at[m, half, pl.ds(0, 15)],
            *sems,
        )

    partner = on_col(quad * 2 + 1 - core)

    def cross_left(m, half):
        return remote(
            recv_b.at[m, half, :, :, :, 0],
            x_left.at[m, half],
            cross_ssem.at[m * 2 + half],
            cross_rsem.at[m * 2 + half],
            partner,
        )

    def cross_right(half):
        return remote(
            recv_b.at[0, half, :, 1 - core, :, 1],
            x_right.at[half],
            cross_ssem.at[4 + half],
            cross_rsem.at[4 + half],
            partner,
        )

    def regroup(m):
        held_z = [recv_z[m, z].astype(F32) for z in range(8)]
        for block in range(16):
            rows = [held_z[z][block * 8 : (block + 1) * 8] for z in range(8)]
            send_a[m, 0, block] = jnp.concatenate(rows, axis=0).astype(BF16)

    def to_rows(m, half):
        for hi in range(2):
            lanes = jnp.concatenate(
                [
                    jnp.concatenate(
                        [recv_a[m, half, pair * 8 + hi * 4 + lo] for lo in range(4)], axis=1
                    )
                    for pair in range(2)
                ],
                axis=0,
            )
            moved = mm(lanes, swap_s[...])
            for lo in range(4):
                mix_s[pl.ds(hi * 512 + lo, 128, stride=4), :] = moved[:, lo * 128 : (lo + 1) * 128]
        both = jnp.concatenate([mix_s[0:512, :], mix_s[512:1024, :]], axis=1)
        both = both.astype(BF16).reshape(2, 8, 2, 16, 256)
        for pair in range(2):
            if half == 0:
                recv_b[m, half, :, :, pair] = both[pair].reshape(4, 2, 2, 16, 256)
            else:
                send_b[m, :, pair] = both[pair]

    def to_channels(m, half):
        for hi in range(2):
            for pair in range(2):
                block = recv_bt[m, half, :, pair, :, hi * 128 : (hi + 1) * 128]
                at = hi * 256 + pair * 128
                mix_s[at : at + 128, :] = block.astype(F32).reshape(128, 128)
        for hi in range(2):
            lanes = jnp.concatenate(
                [mix_s[pl.ds(hi * 256 + lo, 64, stride=4), :] for lo in range(4)], axis=1
            )
            moved = mm(lanes.astype(BF16), swap_s[...]).astype(BF16)
            for lo in range(4):
                part = moved[:, lo * 128 : (lo + 1) * 128]
                for pair in range(2):
                    send_at[m, half, pair * 8 + hi * 4 + lo] = part[pair * 32 : pair * 32 + 32]

    def triangle(m, gap):
        burst(0, m, 1).wait()
        to_rows(m, 1)
        burst(1, m, 1).start()
        burst(1, m, 0).wait()
        regroup(m)
        burst(0, m, 0).start()
        gap()
        burst(0, m, 1).drain()

        def arrive(half):
            if half == 0:
                burst(0, m, 0).wait()
                to_rows(m, 0)
            else:
                burst(1, m, 1).wait()

        if m == 0:
            for half in range(2):
                arrive(half)
                cross_left(m, half).start()
                cross_right(half).start()
            right = jnp.concatenate(
                [
                    recv_b[m, half, s % 4, core, s // 4, 1]
                    for s in range(8)
                    for half in range(2)
                ],
                axis=0,
            )
            own = [
                mm(recv_b[m, half, :, :, :, 0].reshape(256, 256), right, NT) for half in range(2)
            ]
            for half in range(2):
                cross_left(m, half).wait_recv()
                cross_right(half).wait_recv()
            right = jnp.concatenate(
                [x_right[half, s % 4, s // 4] for s in range(8) for half in range(2)], axis=0
            )
            for half in range(2):
                total = own[half] + mm(x_left[m, half].reshape(256, 256), right, NT)
                send_bt[m, half] = total.astype(BF16).reshape(8, 2, 16, 256)
                burst(2, m, half).start()
            for half in range(2):
                cross_right(half).wait_send()
        else:
            right, own = [], None
            for half in range(2):
                arrive(half)
                cross_left(m, half).start()
                right.append(recv_b[m, half, :, :, :, 1].reshape(256, 256))
                term = mm(recv_b[m, half, :, :, :, 0].reshape(256, 256), right[half], TN)
                own = term if half == 0 else own + term
            other = None
            for half in range(2):
                cross_left(m, half).wait_recv()
                term = mm(x_left[m, half].reshape(256, 256), right[half], TN)
                other = term if half == 0 else other + term
            for half in range(2):
                for s in range(8):
                    at = slice(s * 32 + half * 16, s * 32 + half * 16 + 16)
                    z = s % 4 * 2
                    send_bt[m, half, z + core, s // 4] = own[at].astype(BF16)
                    send_bt[m, half, z + 1 - core, s // 4] = other[at].astype(BF16)
                burst(2, m, half).start()
        burst(0, m, 0).drain()
        for half in range(2):
            burst(1, m, half).drain()
            cross_left(m, half).wait_send()
        for half in range(2):
            burst(2, m, half).wait()
            to_channels(m, half)
            burst(3, m, half).start()
        for half in range(2):
            burst(2, m, half).drain()

    def middle_norm(m, half):
        summed = recv_at[m, half].astype(F32).reshape(64, 8, 128)

        def over_channels(value):
            pairs = jnp.sum(value, axis=0)
            return (pairs + pltpu.roll(pairs, 4, 0)) * (1.0 / 128)

        mean_removed = summed - over_channels(summed)[None]
        variance = over_channels(mean_removed * mean_removed)
        nrm_s[...] = (mean_removed * lax.rsqrt(variance + EPS)[None]).reshape(512, 128)

    def update(m, it):
        normed = (nrm_s[pl.ds(it % 4, 128, stride=4), :] * gmid_s[m]).astype(BF16)
        return gate_s[pl.ds(it * 128, 128), :] * mm(normed, wo_ref[m], TN)

    def first_state(it):
        return pair_ref[pl.ds(it * 128, 128), :].astype(F32)

    def second_state(it):
        z = first_state(it) + update(0, it)
        z_s[pl.ds(it * 128, 128), :] = z
        return z

    def project(samples):
        weight = held["watt"][...].reshape(192, 768)
        for s in samples:
            for part in range(4):
                rows = pl.ds(s * 512 + part * 128, 128)
                value = held["tokens"][rows, :].astype(F32)
                xn_s[part * 128 : (part + 1) * 128, :] = normalize(
                    value, held["again"][...].reshape(1, 768)
                ).astype(BF16)
            proj = mm(weight, xn_s[...], NT)
            qkv_s[s] = proj[0:144].astype(BF16)
            sig_s[s] = sigmoid(proj[144:192])
            scores_s[s] = mm(qkv_s[s, 0:48, :], qkv_s[s, 48:96, :], TN) * (48.0**-0.5)

    def gap_first():
        wpt_s[1] = held["wp"][1].T
        for m in range(2):
            gmid_s[m] = jnp.broadcast_to(held["gains"][m, 1:2, :], (128, 128)).T
        heads_s[...] = jnp.zeros_like(heads_s)
        for name in ("wo", "bgain", "bw", "tokens", "again", "watt"):
            loads[name].wait()
        project((0, 1))

    edges(0, 0, first_state)
    pl.semaphore_wait(barrier, 30)
    burst(1, 0, 0).start()
    edges(0, 1, first_state)
    burst(0, 0, 1).start()
    triangle(0, gap_first)
    for half in range(2):
        burst(3, 0, half).wait()
        middle_norm(0, half)
        edges(1, half, second_state)
        burst(1 - half, 1, half).start()
    for half in range(2):
        burst(3, 0, half).drain()

    def to_head(half):
        return Burst(
            heads,
            col,
            lambda p: heads_s.at[half, pl.ds(p * 8, 8)],
            lambda p: recv_h.at[half, p],
            recv_h.at[half],
            heads_s.at[half, pl.ds(0, 120)],
            ssem.at[16 + half],
            rsem.at[16 + half],
        )

    triangle(1, lambda: project((2, 3)))
    for half in range(2):
        burst(3, 1, half).wait()
        middle_norm(1, half)
        for it in range(half * 4, half * 4 + 4):
            z = z_s[pl.ds(it * 128, 128), :] + update(1, it)
            out_ref[pl.ds(it * 128, 128), :] = z
            zn = normalize(z, held["bgain"][...]).astype(BF16)
            bias = mm(held["bw"][...], zn, NT).astype(BF16).astype(F32)
            heads_s[half, pl.ds(it % 4, 16, stride=8), :] = bias
        to_head(half).start()

    def along(half, offset):
        block = bias_s.at[big, pl.ds(half * 16, 16)]
        return remote(
            block,
            block,
            many_ssem.at[half, offset],
            many_rsem.at[half, offset],
            {"row": lax.rem(row + offset, 8)},
        )

    def across(half, owner, z):
        block = bias_s.at[owner * 8 + z, pl.ds(half * 16, 16)]
        return remote(
            block,
            block,
            many_ssem.at[half, 8 + z],
            many_rsem.at[half, 8 + z],
            {"group": 1 - group},
        )

    for half in range(2):
        to_head(half).wait()
        lanes = jnp.concatenate(
            [
                jnp.concatenate([recv_h[half, hi * 4 + lo] for lo in range(4)], axis=1)
                for hi in range(4)
            ],
            axis=0,
        ).astype(BF16)
        moved = mm(lanes, swap_s[...])
        for hi in range(4):
            for lo in range(4):
                rows_s[pl.ds(hi * 32 + lo, 8, stride=4), :] = moved[
                    hi * 8 : (hi + 1) * 8, lo * 128 : (lo + 1) * 128
                ]
        bias_s[big, half * 16 : (half + 1) * 16, :] = jnp.concatenate(
            [rows_s[hi * 32 : hi * 32 + 16, :] for hi in range(4)], axis=1
        ).astype(BF16)
        for offset in (4, 3, 5, 2, 6, 1, 7):
            along(half, offset).start()
        across(half, group, row).start()
    for half in range(2):
        burst(3, 1, half).drain()

    to_tokens = Exchange(
        16,
        col,
        on_col,
        lambda p: send_o.at[p],
        lambda p: recv_o.at[p],
        many_ssem.at[2],
        many_rsem.at[2],
    )

    def attend(step, carry):
        owner = lax.rem(group + step // 2, 2)
        side = lax.rem(row // 4 + step, 2)
        part = owner * 2 + side
        for lo in range(4):
            z = side * 4 + lo

            @pl.when(jnp.logical_and(step < 2, z != row))
            def _():
                for half in range(2):
                    along(half, lax.rem(row - z + 8, 8)).wait_recv()
                    across(half, owner, z).start()

            @pl.when(step >= 2)
            def _():
                for half in range(2):
                    across(half, owner, z).wait_recv()

        bias = bias_s[pl.ds(part * 4, 4)].reshape(128, 512).astype(F32)
        rows = pl.ds(pl.multiple_of(part * 128, 128), 128)
        for s in range(4):
            logits = scores_s[s, rows, :] + bias
            shifted = jnp.exp(logits - jnp.max(logits, axis=-1, keepdims=True))
            weights = shifted * (1.0 / jnp.sum(shifted, axis=-1, keepdims=True))
            mixed = mm(qkv_s[s, 96:144, :], weights.astype(BF16), NT)
            gated = mixed * sig_s[s, :, rows]
            ot_s[:, s * 128 : (s + 1) * 128] = gated.astype(BF16)
        moved = mm(ot_s[...], swap_s[...]).astype(BF16)
        for lo in range(4):
            target = part * 4 + lo
            send_o[target] = moved[:, lo * 128 : (lo + 1) * 128]

            @pl.when(target != col)
            def _():
                to_tokens.copy(lax.rem(target - col + 16, 16)).start()

            @pl.when(target == col)
            def _():
                to_tokens.own().start()

        return carry

    lax.fori_loop(0, 4, attend, 0)

    for half in range(2):
        loop(1, 8, lambda d: along(half, d).wait_send())
        loop(0, 8, lambda z: across(half, group, z).wait_send())
        to_head(half).drain()
    for name in ("wout", "tgain", "wup", "wdown"):
        loads[name].wait()
    own = [
        held["tokens"][pl.ds(pl.multiple_of(s * 512 + col * 32, 32), 32), :] for s in range(4)
    ]
    own = jnp.concatenate(own, axis=0).astype(F32)
    to_tokens.own().wait()
    loop(1, 16, lambda d: to_tokens.copy(d).wait())
    first = own + mm(recv_o[...].reshape(768, 128), held["wout"][...], TN)
    xn2 = normalize(first, held["tgain"][...].reshape(1, 768)).astype(BF16)
    total = first
    for j in range(4):
        up = mm(xn2, held["wup"][:, j * 384 : (j + 1) * 384])
        side = mm(xn2, held["wup"][:, 1536 + j * 384 : 1536 + (j + 1) * 384])
        hidden = (up * sigmoid(up) * side).astype(BF16)
        total += mm(hidden, held["wdown"][j * 384 : (j + 1) * 384, :])
    tok_ref[...] = total


def close_kernel(pair_ref, tokens_ref, pair_out, tokens_out, pair_s, tokens_s, in_sem, out_sem):
    copies = []
    for i in range(4):
        for n, (src, held, dst, size) in enumerate(
            ((pair_ref, pair_s, pair_out, 256), (tokens_ref, tokens_s, tokens_out, 32))
        ):
            rows = pl.ds(i * size, size)
            copies.append(
                (
                    pltpu.make_async_copy(src.at[rows], held.at[rows], in_sem.at[n, i]),
                    pltpu.make_async_copy(held.at[rows], dst.at[rows], out_sem.at[n, i]),
                )
            )
    for first, _ in copies:
        first.start()
    for first, second in copies:
        first.wait()
        second.start()
    for _, second in copies:
        second.wait()


def on_device(
    pair,
    pair_mask,
    tri_proj,
    tri_gate,
    triangle_output_weight,
    tri_gains,
    pair_bias_gain,
    bias_weight,
    tokens,
    att_gain,
    att_proj,
    att_out,
    tr_gain,
    tr_up,
    tr_down,
):
    operands = (
        pair.reshape(1024, 128),
        pair_mask,
        tri_proj,
        tri_gate,
        triangle_output_weight,
        tri_gains,
        pair_bias_gain.reshape(1, 128),
        jnp.swapaxes(bias_weight, 0, 1),
        tokens.reshape(2048, 768),
        att_gain,
        jnp.swapaxes(att_proj, 1, 2),
        att_out,
        tr_gain,
        tr_up,
        tr_down,
    )
    vmem = pl.BlockSpec(memory_space=pltpu.VMEM)
    hbm = pl.BlockSpec(memory_space=pl.ANY)
    pair_out, tokens_out = pl.pallas_call(
        block_kernel,
        out_shape=(
            jax.ShapeDtypeStruct((1024, 128), F32),
            jax.ShapeDtypeStruct((128, 768), F32),
        ),
        in_specs=[hbm] * 15,
        out_specs=(vmem, vmem),
        scratch_shapes=[pltpu.VMEM(x.shape, x.dtype) for x in operands]
        + [
            pltpu.VMEM((1024, 128), F32),
            pltpu.VMEM((1024, 128), F32),
            pltpu.VMEM((1024, 128), F32),
            pltpu.VMEM((512, 128), F32),
            pltpu.VMEM((1024, 128), F32),
            pltpu.VMEM((2, 512, 128), BF16),
            pltpu.VMEM((2, 128, 128), F32),
            pltpu.VMEM((8, 128), F32),
            pltpu.VMEM((512, 512), BF16),
            pltpu.VMEM((2, 8, 128, 128), BF16),
            pltpu.VMEM((2, 8, 128, 128), BF16),
            pltpu.VMEM((2, 2, 16, 64, 128), BF16),
            pltpu.VMEM((2, 2, 16, 64, 128), BF16),
            pltpu.VMEM((2, 8, 2, 2, 16, 256), BF16),
            pltpu.VMEM((2, 2, 4, 2, 2, 2, 16, 256), BF16),
            pltpu.VMEM((2, 2, 4, 2, 2, 16, 256), BF16),
            pltpu.VMEM((2, 4, 2, 16, 256), BF16),
            pltpu.VMEM((2, 2, 8, 2, 16, 256), BF16),
            pltpu.VMEM((2, 2, 8, 2, 16, 256), BF16),
            pltpu.VMEM((2, 2, 16, 32, 128), BF16),
            pltpu.VMEM((2, 2, 16, 32, 128), BF16),
            pltpu.VMEM((2, 128, 128), F32),
            pltpu.VMEM((2, 16, 8, 128), F32),
            pltpu.VMEM((128, 128), F32),
            pltpu.VMEM((16, 32, 512), BF16),
            pltpu.VMEM((512, 768), BF16),
            pltpu.VMEM((4, 144, 512), BF16),
            pltpu.VMEM((4, 48, 512), F32),
            pltpu.VMEM((4, 512, 512), F32),
            pltpu.VMEM((48, 512), BF16),
            pltpu.VMEM((16, 48, 128), BF16),
            pltpu.VMEM((16, 48, 128), BF16),
            pltpu.SemaphoreType.DMA((18,)),
            pltpu.SemaphoreType.DMA((18,)),
            pltpu.SemaphoreType.DMA((6,)),
            pltpu.SemaphoreType.DMA((6,)),
            pltpu.SemaphoreType.DMA((3, 16)),
            pltpu.SemaphoreType.DMA((3, 16)),
            pltpu.SemaphoreType.DMA((15,)),
        ],
        compiler_params=pltpu.CompilerParams(
            collective_id=0, has_side_effects=True, vmem_limit_bytes=60 * 1024 * 1024
        ),
        cost_estimate=pl.CostEstimate(
            flops=6_000_000_000, bytes_accessed=15_000_000, transcendentals=3_000_000
        ),
    )(*operands)
    pair_out, tokens_out = pl.pallas_call(
        close_kernel,
        out_shape=(
            jax.ShapeDtypeStruct((1024, 128), F32),
            jax.ShapeDtypeStruct((128, 768), F32),
        ),
        in_specs=[hbm, hbm],
        out_specs=(hbm, hbm),
        scratch_shapes=[
            pltpu.VMEM((1024, 128), F32),
            pltpu.VMEM((128, 768), F32),
            pltpu.SemaphoreType.DMA((2, 4)),
            pltpu.SemaphoreType.DMA((2, 4)),
        ],
        compiler_params=pltpu.CompilerParams(vmem_limit_bytes=60 * 1024 * 1024),
    )(pair_out, tokens_out)
    return pair_out.reshape(32, 32, 128), tokens_out.reshape(4, 32, 768)


def solution(mesh):
    placed = (
        P(("group", "row"), "col", None),
        P(("group", "row"), "col"),
        P(),
        P(),
        P(),
        P(),
        P(),
        P(),
        P(("group", "row"), None, None),
        P(),
        P(None, None, "col"),
        P(),
        P(),
        P(),
        P(),
    )
    return jax.shard_map(
        on_device,
        mesh=mesh,
        in_specs=placed,
        out_specs=(P(("group", "row"), "col", None), P(("group", "row"), "col", None)),
        check_vma=False,
    )
```

```python
import jax
import jax.numpy as jnp
from jax import lax
from jax.experimental import pallas as pl
from jax.experimental.pallas import tpu as pltpu
from jax.sharding import PartitionSpec as P

EPS = 1e-05
MESH = pl.DeviceIdType.MESH
F32 = jnp.float32
BF16 = jnp.bfloat16
NT = (((1,), (1,)), ((), ()))
TN = (((0,), (0,)), ((), ()))


def normalize(value, gain):
    mean = jnp.mean(value, axis=-1, keepdims=True)
    mean_removed = value - mean
    variance = jnp.mean(mean_removed * mean_removed, axis=-1, keepdims=True)
    return mean_removed * lax.rsqrt(variance + EPS) * gain


def mm(a, b, dims=(((1,), (0,)), ((), ()))):
    return lax.dot_general(a, b, dims, preferred_element_type=F32)


def swap_matrix():
    row = lax.broadcasted_iota(jnp.int32, (512, 512), 0)
    col = lax.broadcasted_iota(jnp.int32, (512, 512), 1)
    a, b, k = row >> 7, (row >> 5) & 3, row & 31
    return jnp.where((b << 7) + (a << 5) + k == col, 1.0, 0.0).astype(BF16)


def remote(src, dst, send, recv, device):
    return pltpu.make_async_remote_copy(
        src_ref=src,
        dst_ref=dst,
        send_sem=send,
        recv_sem=recv,
        device_id=device,
        device_id_type=MESH,
    )


def loop(first, last, step):
    def body(d, carry):
        step(d)
        return carry

    lax.fori_loop(first, last, body, 0)


class Exchange:
    def __init__(self, n, me, device, src, dst, send, recv):
        self.n, self.me, self.device = n, me, device
        self.src, self.dst, self.send, self.recv = src, dst, send, recv

    def copy(self, d):
        peer = lax.rem(self.me + d, self.n)
        return remote(
            self.src(peer), self.dst(self.me), self.send.at[d], self.recv.at[d], self.device(peer)
        )

    def own(self):
        return pltpu.make_async_copy(self.src(self.me), self.dst(self.me), self.recv.at[0])


def ring(at, n):
    steps = [n // 2]
    for step in range(n // 2 - 1, 0, -1):
        steps += [step, n - step]
    return [lax.rem(at + step, n) for step in steps]


def sigmoid(value):
    return 0.5 * jnp.tanh(0.5 * value) + 0.5


class Burst:
    def __init__(self, peers, me, src, dst, all_dst, most_src, send, recv):
        self.peers, self.me = peers, me
        self.src, self.dst, self.all_dst, self.most_src = src, dst, all_dst, most_src
        self.send, self.recv = send, recv

    def start(self):
        for peer, device in self.peers:
            remote(self.src(peer), self.dst(self.me), self.send, self.recv, device).start()
        pltpu.make_async_copy(self.src(self.me), self.dst(self.me), self.recv).start()

    def wait(self):
        pltpu.make_async_copy(self.all_dst, self.all_dst, self.recv).wait()

    def drain(self):
        pltpu.make_async_copy(self.most_src, self.most_src, self.send).wait()


NAMES = (
    "pair",
    "mask",
    "wp",
    "wg",
    "wo",
    "gains",
    "bgain",
    "bw",
    "tokens",
    "again",
    "watt",
    "wout",
    "tgain",
    "wup",
    "wdown",
)


def block_kernel(*refs):
    inputs = dict(zip(NAMES, refs[:15]))
    out_ref, tok_ref = refs[15:17]
    held = dict(zip(NAMES, refs[17:32]))
    (
        z_s,
        gate_s,
        flat_s,
        nrm_s,
        mix_s,
        wpt_s,
        gmid_s,
        wout_s,
        mask_s,
        swap_s,
        send_z,
        recv_z,
        send_a,
        recv_a,
        send_b,
        recv_b,
        x_left,
        x_right,
        send_zt,
        recv_zt,
        send_bt,
        recv_bt,
        send_at,
        recv_at,
        heads_s,
        recv_h,
        rows_s,
        bias_s,
        xn_s,
        qkv_s,
        sig_s,
        scores_s,
        ot_s,
        send_o,
        recv_o,
        ssem,
        rsem,
        cross_ssem,
        cross_rsem,
        many_ssem,
        many_rsem,
        load_sem,
    ) = refs[32:]
    group, row, col = (lax.axis_index(name) for name in ("group", "row", "col"))
    big = group * 8 + row
    quad = lax.div(col, 2)
    core = lax.rem(col, 2)

    loads = {
        name: pltpu.make_async_copy(inputs[name], held[name], load_sem.at[i])
        for i, name in enumerate(NAMES)
    }
    early = ("pair", "wp", "mask", "gains", "wg")
    late = ("wo", "bgain", "bw", "tokens", "again", "watt", "wout", "tgain", "wup", "wdown")
    for name in early:
        loads[name].start()

    def on_col(peer):
        return {"col": peer}

    quad_y = lax.rem(quad, 4)
    chip_x = lax.div(quad, 4) * 2 + group
    plane_me = group * 8 + quad
    xs = [lax.rem(chip_x + d, 4) for d in range(4)]
    ys = [lax.rem(quad_y + d, 4) for d in range(4)]
    plane = []
    far = ((2, 2), (2, 1), (2, 3), (1, 2), (3, 2), (1, 1), (3, 3), (1, 3), (3, 1))
    for dx, dy in far + ((2, 0), (0, 2), (1, 0), (3, 0), (0, 1), (0, 3)):
        high, low = lax.div(xs[dx], 2), lax.rem(xs[dx], 2)
        place = high * 4 + ys[dy]
        plane.append((low * 8 + place, {"group": low, "col": place * 2 + core}))
    line = [(z, {"row": z}) for z in ring(row, 8)]
    heads = [
        (pair * 8 + place, on_col(pair * 8 + place))
        for place in ring(lax.rem(col, 8), 8) + [lax.rem(col, 8)]
        for pair in (1 - lax.div(col, 8), lax.div(col, 8))
    ][:-1]

    barrier = pltpu.get_barrier_semaphore()

    def greet(device):
        pl.semaphore_signal(barrier, inc=1, device_id=device, device_id_type=MESH)

    loop(1, 16, lambda d: greet(on_col(lax.rem(col + d, 16))))
    loop(1, 8, lambda d: greet({"row": lax.rem(row + d, 8)}))
    loop(0, 8, lambda place: greet({"group": 1 - group, "col": place * 2 + core}))

    swap_s[...] = swap_matrix()
    pair_ref = held["pair"]
    wg_ref, wo_ref = held["wg"], held["wo"]

    for name in early:
        loads[name].wait()
    for name in late:
        loads[name].start()
    gain_in = [held["gains"][m, 0:1, :] for m in range(2)]
    wpt_s[0] = held["wp"][0].T
    mask = held["mask"][...].astype(F32).astype(BF16)
    picked = []
    for lo in range(4):
        t = lax.broadcasted_iota(jnp.int32, (8, 32), 0)
        i = lax.broadcasted_iota(jnp.int32, (8, 32), 1)
        pick = jnp.where(i == t * 4 + lo, 1.0, 0.0).astype(BF16)
        k = lax.broadcasted_iota(jnp.int32, (32, 128), 0)
        lane = lax.broadcasted_iota(jnp.int32, (32, 128), 1)
        place = jnp.where(lane == lo * 32 + k, 1.0, 0.0).astype(BF16)
        picked.append(mm(mm(pick, mask).astype(BF16), place))
    mask_s[...] = picked[0] + picked[1] + picked[2] + picked[3]

    def edges(m, half, state):
        for two in range(2):
            it = half * 4 + two * 2
            z = jnp.concatenate([state(it), state(it + 1)], axis=0)
            zn = normalize(z, gain_in[m]).astype(BF16)
            proj = mm(wpt_s[m], zn, NT)
            for t in range(2):
                part = proj[:, t * 128 : (t + 1) * 128]
                keep = mask_s[it + t : it + t + 1, :]
                left = keep * sigmoid(part[0:128]) * part[128:256]
                right = keep * sigmoid(part[256:384]) * part[384:512]
                flat_s[pl.ds(two * 2 + t, 128, stride=8), :] = left
                flat_s[pl.ds(4 + two * 2 + t, 128, stride=8), :] = right
            gate_s[pl.ds(it * 128, 256), :] = sigmoid(mm(zn, wg_ref[m]))
        if half == 0:
            for z in range(8):
                rows = [flat_s[pl.ds(block * 64 + z * 8, 8), :] for block in range(16)]
                send_z[m, z] = jnp.concatenate(rows, axis=0).astype(BF16)
        else:
            for block in range(16):
                send_a[m, half, block] = flat_s[pl.ds(block * 64, 64), :].astype(BF16)

    def burst(stage, m, half):
        sems = ssem.at[stage * 4 + m * 2 + half], rsem.at[stage * 4 + m * 2 + half]
        if stage == 0:
            return Burst(
                plane,
                plane_me,
                lambda p: send_a.at[m, half, p],
                lambda p: recv_a.at[m, half, p],
                recv_a.at[m, half],
                send_a.at[m, half, pl.ds(0, 15)],
                *sems,
            )
        if stage == 1 and half == 0:
            return Burst(
                line,
                row,
                lambda p: send_z.at[m, p],
                lambda p: recv_z.at[m, p],
                recv_z.at[m],
                send_z.at[m, pl.ds(0, 7)],
                *sems,
            )
        if stage == 1:
            return Burst(
                line,
                row,
                lambda p: send_b.at[m, p],
                lambda p: recv_b.at[m, half, lax.div(p, 2), lax.rem(p, 2)],
                recv_b.at[m, half],
                send_b.at[m, pl.ds(0, 7)],
                *sems,
            )
        if stage == 2 and half == 1:
            return Burst(
                line,
                row,
                lambda p: send_zt.at[m, p],
                lambda p: recv_zt.at[m, p],
                recv_zt.at[m],
                send_zt.at[m, pl.ds(0, 7)],
                *sems,
            )
        if stage == 2:
            return Burst(
                line,
                row,
                lambda p: send_bt.at[m, half, p],
                lambda p: recv_bt.at[m, p],
                recv_bt.at[m],
                send_bt.at[m, half, pl.ds(0, 7)],
                *sems,
            )
        return Burst(
            plane,
            plane_me,
            lambda p: send_at.at[m, half, p],
            lambda p: recv_at.at[m, half, p],
            recv_at.at[m, half],
            send_at.at[m, half, pl.ds(0, 15)],
            *sems,
        )

    partner = on_col(quad * 2 + 1 - core)

    def cross_left(m, half):
        return remote(
            recv_b.at[m, half, :, :, :, 0],
            x_left.at[m, half],
            cross_ssem.at[m * 2 + half],
            cross_rsem.at[m * 2 + half],
            partner,
        )

    def cross_right(half):
        return remote(
            recv_b.at[0, half, :, 1 - core, :, 1],
            x_right.at[half],
            cross_ssem.at[4 + half],
            cross_rsem.at[4 + half],
            partner,
        )

    def regroup(m):
        held_z = [recv_z[m, z].astype(F32) for z in range(8)]
        for block in range(16):
            rows = [held_z[z][block * 8 : (block + 1) * 8] for z in range(8)]
            send_a[m, 0, block] = jnp.concatenate(rows, axis=0).astype(BF16)

    def to_rows(m, half):
        for hi in range(2):
            lanes = jnp.concatenate(
                [
                    jnp.concatenate(
                        [recv_a[m, half, pair * 8 + hi * 4 + lo] for lo in range(4)], axis=1
                    )
                    for pair in range(2)
                ],
                axis=0,
            )
            moved = mm(lanes, swap_s[...])
            for lo in range(4):
                mix_s[pl.ds(hi * 512 + lo, 128, stride=4), :] = moved[:, lo * 128 : (lo + 1) * 128]
        both = jnp.concatenate([mix_s[0:512, :], mix_s[512:1024, :]], axis=1)
        both = both.astype(BF16).reshape(2, 8, 2, 16, 256)
        for pair in range(2):
            if half == 0:
                recv_b[m, half, :, :, pair] = both[pair].reshape(4, 2, 2, 16, 256)
            else:
                send_b[m, :, pair] = both[pair]

    def to_channels(m, half):
        for hi in range(2):
            for pair in range(2):
                if half == 0:
                    block = recv_bt[m, :, pair, :, hi * 128 : (hi + 1) * 128]
                else:
                    block = send_bt[m, half, :, pair, :, hi * 128 : (hi + 1) * 128]
                at = hi * 256 + pair * 128
                mix_s[at : at + 128, :] = block.astype(F32).reshape(128, 128)
        for hi in range(2):
            lanes = jnp.concatenate(
                [mix_s[pl.ds(hi * 256 + lo, 64, stride=4), :] for lo in range(4)], axis=1
            )
            moved = mm(lanes.astype(BF16), swap_s[...]).astype(BF16)
            for lo in range(4):
                part = moved[:, lo * 128 : (lo + 1) * 128]
                for pair in range(2):
                    send_at[m, half, pair * 8 + hi * 4 + lo] = part[pair * 32 : pair * 32 + 32]

    def regroup_back(m):
        mix_s[0:512, :] = recv_at[m, 1].astype(F32).reshape(512, 128)
        for z in range(8):
            for t in range(4):
                mix_s[pl.ds(512 + z * 64 + t, 16, stride=4), :] = mix_s[
                    pl.ds(z * 4 + t, 16, stride=32), :
                ]
            send_zt[m, z] = mix_s[pl.ds(512 + z * 64, 64), :].astype(BF16)

    def triangle(m, gap):
        burst(0, m, 1).wait()
        to_rows(m, 1)
        burst(1, m, 1).start()
        burst(1, m, 0).wait()
        regroup(m)
        burst(0, m, 0).start()
        gap()
        burst(0, m, 1).drain()

        def arrive(half):
            if half == 0:
                burst(0, m, 0).wait()
                to_rows(m, 0)
            else:
                burst(1, m, 1).wait()

        def send_back(half):
            if half == 0:
                burst(2, m, 0).start()
            else:
                to_channels(m, 1)
                burst(3, m, 1).start()

        if m == 0:
            for half in range(2):
                arrive(half)
                cross_left(m, half).start()
                cross_right(half).start()
            right = jnp.concatenate(
                [
                    recv_b[m, half, s % 4, core, s // 4, 1]
                    for s in range(8)
                    for half in range(2)
                ],
                axis=0,
            )
            own = [
                mm(recv_b[m, half, :, :, :, 0].reshape(256, 256), right, NT) for half in range(2)
            ]
            for half in range(2):
                cross_left(m, half).wait_recv()
                cross_right(half).wait_recv()
            right = jnp.concatenate(
                [x_right[half, s % 4, s // 4] for s in range(8) for half in range(2)], axis=0
            )
            for half in range(2):
                total = own[half] + mm(x_left[m, half].reshape(256, 256), right, NT)
                send_bt[m, half] = total.astype(BF16).reshape(8, 2, 16, 256)
                send_back(half)
            for half in range(2):
                cross_right(half).wait_send()
        else:
            right, own = [], None
            for half in range(2):
                arrive(half)
                cross_left(m, half).start()
                right.append(recv_b[m, half, :, :, :, 1].reshape(256, 256))
                term = mm(recv_b[m, half, :, :, :, 0].reshape(256, 256), right[half], TN)
                own = term if half == 0 else own + term
            other = None
            for half in range(2):
                cross_left(m, half).wait_recv()
                term = mm(x_left[m, half].reshape(256, 256), right[half], TN)
                other = term if half == 0 else other + term
            for half in range(2):
                for s in range(8):
                    at = slice(s * 32 + half * 16, s * 32 + half * 16 + 16)
                    z = s % 4 * 2
                    send_bt[m, half, z + core, s // 4] = own[at].astype(BF16)
                    send_bt[m, half, z + 1 - core, s // 4] = other[at].astype(BF16)
                send_back(half)
        burst(0, m, 0).drain()
        for half in range(2):
            burst(1, m, half).drain()
            cross_left(m, half).wait_send()
        burst(3, m, 1).wait()
        regroup_back(m)
        burst(2, m, 1).start()
        burst(2, m, 0).wait()
        to_channels(m, 0)
        burst(3, m, 0).start()
        burst(2, m, 0).drain()
        burst(3, m, 1).drain()

    def middle_norm(m, half):
        if half == 0:
            burst(3, m, 0).wait()
            summed = recv_at[m, 0]
        else:
            burst(2, m, 1).wait()
            summed = recv_zt[m]
        summed = summed.astype(F32).reshape(64, 8, 128)

        def over_channels(value):
            pairs = jnp.sum(value, axis=0)
            return (pairs + pltpu.roll(pairs, 4, 0)) * (1.0 / 128)

        mean_removed = summed - over_channels(summed)[None]
        variance = over_channels(mean_removed * mean_removed)
        nrm_s[...] = (mean_removed * lax.rsqrt(variance + EPS)[None]).reshape(512, 128)

    def update(m, it):
        half = it // 4
        normed = (nrm_s[pl.ds(it % 4, 128, stride=4), :] * gmid_s[half * 2 + m]).astype(BF16)
        return gate_s[pl.ds(it * 128, 128), :] * mm(normed, wout_s[half * 2 + m], TN)

    def first_state(it):
        return pair_ref[pl.ds(it * 128, 128), :].astype(F32)

    def second_state(it):
        z = first_state(it) + update(0, it)
        z_s[pl.ds(it * 128, 128), :] = z
        return z

    def project(samples):
        weight = held["watt"][...].reshape(192, 768)
        for s in samples:
            for part in range(4):
                rows = pl.ds(s * 512 + part * 128, 128)
                value = held["tokens"][rows, :].astype(F32)
                xn_s[part * 128 : (part + 1) * 128, :] = normalize(
                    value, held["again"][...].reshape(1, 768)
                ).astype(BF16)
            proj = mm(weight, xn_s[...], NT)
            qkv_s[s] = proj[0:144].astype(BF16)
            sig_s[s] = sigmoid(proj[144:192])
            scores_s[s] = mm(qkv_s[s, 0:48, :], qkv_s[s, 48:96, :], TN) * (48.0**-0.5)

    def gap_first():
        wpt_s[1] = held["wp"][1].T
        heads_s[...] = jnp.zeros_like(heads_s)
        for name in ("wo", "bgain", "bw", "tokens", "again", "watt"):
            loads[name].wait()
        for m in range(2):
            gmid_s[m] = jnp.broadcast_to(held["gains"][m, 1:2, :], (128, 128)).T
            wout_s[m] = wo_ref[m]
            mix_s[0:128, :] = gmid_s[m]
            mix_s[128:256, :] = wo_ref[m].astype(F32)
            for z in range(8):
                rows = slice(z * 16, z * 16 + 16)
                gmid_s[2 + m, rows, :] = mix_s[pl.ds(z, 16, stride=8), :]
                wout_s[2 + m, rows, :] = mix_s[pl.ds(128 + z, 16, stride=8), :].astype(BF16)
        project((0, 1))

    edges(0, 0, first_state)
    pl.semaphore_wait(barrier, 30)
    burst(1, 0, 0).start()
    edges(0, 1, first_state)
    burst(0, 0, 1).start()
    triangle(0, gap_first)
    for half in range(2):
        middle_norm(0, half)
        edges(1, half, second_state)
        burst(1 - half, 1, half).start()
    burst(3, 0, 0).drain()
    burst(2, 0, 1).drain()

    def to_head(half):
        return Burst(
            heads,
            col,
            lambda p: heads_s.at[half, pl.ds(p * 8, 8)],
            lambda p: recv_h.at[half, p],
            recv_h.at[half],
            heads_s.at[half, pl.ds(0, 120)],
            ssem.at[16 + half],
            rsem.at[16 + half],
        )

    triangle(1, lambda: project((2, 3)))
    for half in range(2):
        middle_norm(1, half)
        for it in range(half * 4, half * 4 + 4):
            z = z_s[pl.ds(it * 128, 128), :] + update(1, it)
            out_ref[pl.ds(it * 128, 128), :] = z
            zn = normalize(z, held["bgain"][...]).astype(BF16)
            bias = mm(held["bw"][...], zn, NT).astype(BF16).astype(F32)
            heads_s[half, pl.ds(it % 4, 16, stride=8), :] = bias
        to_head(half).start()

    def along(half, offset):
        block = bias_s.at[big, pl.ds(half * 16, 16)]
        return remote(
            block,
            block,
            many_ssem.at[half, offset],
            many_rsem.at[half, offset],
            {"row": lax.rem(row + offset, 8)},
        )

    def across(half, owner, z):
        block = bias_s.at[owner * 8 + z, pl.ds(half * 16, 16)]
        return remote(
            block,
            block,
            many_ssem.at[half, 8 + z],
            many_rsem.at[half, 8 + z],
            {"group": 1 - group},
        )

    for half in range(2):
        to_head(half).wait()
        lanes = jnp.concatenate(
            [
                jnp.concatenate([recv_h[half, hi * 4 + lo] for lo in range(4)], axis=1)
                for hi in range(4)
            ],
            axis=0,
        ).astype(BF16)
        moved = mm(lanes, swap_s[...])
        for hi in range(4):
            for lo in range(4):
                rows_s[pl.ds(hi * 32 + lo, 8, stride=4), :] = moved[
                    hi * 8 : (hi + 1) * 8, lo * 128 : (lo + 1) * 128
                ]
        bias_s[big, half * 16 : (half + 1) * 16, :] = jnp.concatenate(
            [rows_s[hi * 32 : hi * 32 + 16, :] for hi in range(4)], axis=1
        ).astype(BF16)
        for offset in (4, 3, 5, 2, 6, 1, 7):
            along(half, offset).start()
        across(half, group, row).start()
    burst(3, 1, 0).drain()
    burst(2, 1, 1).drain()

    to_tokens = Exchange(
        16,
        col,
        on_col,
        lambda p: send_o.at[p],
        lambda p: recv_o.at[p],
        many_ssem.at[2],
        many_rsem.at[2],
    )

    def attend(step, carry):
        owner = lax.rem(group + step // 2, 2)
        side = lax.rem(row // 4 + step, 2)
        part = owner * 2 + side
        for lo in range(4):
            z = side * 4 + lo

            @pl.when(jnp.logical_and(step < 2, z != row))
            def _():
                for half in range(2):
                    along(half, lax.rem(row - z + 8, 8)).wait_recv()
                    across(half, owner, z).start()

            @pl.when(step >= 2)
            def _():
                for half in range(2):
                    across(half, owner, z).wait_recv()

        bias = bias_s[pl.ds(part * 4, 4)].reshape(128, 512).astype(F32)
        rows = pl.ds(pl.multiple_of(part * 128, 128), 128)
        for s in range(4):
            logits = scores_s[s, rows, :] + bias
            shifted = jnp.exp(logits - jnp.max(logits, axis=-1, keepdims=True))
            weights = shifted * (1.0 / jnp.sum(shifted, axis=-1, keepdims=True))
            mixed = mm(qkv_s[s, 96:144, :], weights.astype(BF16), NT)
            gated = mixed * sig_s[s, :, rows]
            ot_s[:, s * 128 : (s + 1) * 128] = gated.astype(BF16)
        moved = mm(ot_s[...], swap_s[...]).astype(BF16)
        for lo in range(4):
            target = part * 4 + lo
            send_o[target] = moved[:, lo * 128 : (lo + 1) * 128]

            @pl.when(target != col)
            def _():
                to_tokens.copy(lax.rem(target - col + 16, 16)).start()

            @pl.when(target == col)
            def _():
                to_tokens.own().start()

        return carry

    lax.fori_loop(0, 4, attend, 0)

    for half in range(2):
        loop(1, 8, lambda d: along(half, d).wait_send())
        loop(0, 8, lambda z: across(half, group, z).wait_send())
        to_head(half).drain()
    for name in ("wout", "tgain", "wup", "wdown"):
        loads[name].wait()
    own = [
        held["tokens"][pl.ds(pl.multiple_of(s * 512 + col * 32, 32), 32), :] for s in range(4)
    ]
    own = jnp.concatenate(own, axis=0).astype(F32)
    to_tokens.own().wait()
    loop(1, 16, lambda d: to_tokens.copy(d).wait())
    first = own + mm(recv_o[...].reshape(768, 128), held["wout"][...], TN)
    xn2 = normalize(first, held["tgain"][...].reshape(1, 768)).astype(BF16)
    total = first
    for j in range(4):
        up = mm(xn2, held["wup"][:, j * 384 : (j + 1) * 384])
        side = mm(xn2, held["wup"][:, 1536 + j * 384 : 1536 + (j + 1) * 384])
        hidden = (up * sigmoid(up) * side).astype(BF16)
        total += mm(hidden, held["wdown"][j * 384 : (j + 1) * 384, :])
    tok_ref[...] = total


def close_kernel(pair_ref, tokens_ref, pair_out, tokens_out, pair_s, tokens_s, in_sem, out_sem):
    copies = []
    for i in range(4):
        for n, (src, held, dst, size) in enumerate(
            ((pair_ref, pair_s, pair_out, 256), (tokens_ref, tokens_s, tokens_out, 32))
        ):
            rows = pl.ds(i * size, size)
            copies.append(
                (
                    pltpu.make_async_copy(src.at[rows], held.at[rows], in_sem.at[n, i]),
                    pltpu.make_async_copy(held.at[rows], dst.at[rows], out_sem.at[n, i]),
                )
            )
    for first, _ in copies:
        first.start()
    for first, second in copies:
        first.wait()
        second.start()
    for _, second in copies:
        second.wait()


def on_device(
    pair,
    pair_mask,
    tri_proj,
    tri_gate,
    triangle_output_weight,
    tri_gains,
    pair_bias_gain,
    bias_weight,
    tokens,
    att_gain,
    att_proj,
    att_out,
    tr_gain,
    tr_up,
    tr_down,
):
    operands = (
        pair.reshape(1024, 128),
        pair_mask,
        tri_proj,
        tri_gate,
        triangle_output_weight,
        tri_gains,
        pair_bias_gain.reshape(1, 128),
        jnp.swapaxes(bias_weight, 0, 1),
        tokens.reshape(2048, 768),
        att_gain,
        jnp.swapaxes(att_proj, 1, 2),
        att_out,
        tr_gain,
        tr_up,
        tr_down,
    )
    vmem = pl.BlockSpec(memory_space=pltpu.VMEM)
    hbm = pl.BlockSpec(memory_space=pl.ANY)
    pair_out, tokens_out = pl.pallas_call(
        block_kernel,
        out_shape=(
            jax.ShapeDtypeStruct((1024, 128), F32),
            jax.ShapeDtypeStruct((128, 768), F32),
        ),
        in_specs=[hbm] * 15,
        out_specs=(vmem, vmem),
        scratch_shapes=[pltpu.VMEM(x.shape, x.dtype) for x in operands]
        + [
            pltpu.VMEM((1024, 128), F32),
            pltpu.VMEM((1024, 128), F32),
            pltpu.VMEM((1024, 128), F32),
            pltpu.VMEM((512, 128), F32),
            pltpu.VMEM((1024, 128), F32),
            pltpu.VMEM((2, 512, 128), BF16),
            pltpu.VMEM((4, 128, 128), F32),
            pltpu.VMEM((4, 128, 128), BF16),
            pltpu.VMEM((8, 128), F32),
            pltpu.VMEM((512, 512), BF16),
            pltpu.VMEM((2, 8, 128, 128), BF16),
            pltpu.VMEM((2, 8, 128, 128), BF16),
            pltpu.VMEM((2, 2, 16, 64, 128), BF16),
            pltpu.VMEM((2, 2, 16, 64, 128), BF16),
            pltpu.VMEM((2, 8, 2, 2, 16, 256), BF16),
            pltpu.VMEM((2, 2, 4, 2, 2, 2, 16, 256), BF16),
            pltpu.VMEM((2, 2, 4, 2, 2, 16, 256), BF16),
            pltpu.VMEM((2, 4, 2, 16, 256), BF16),
            pltpu.VMEM((2, 8, 64, 128), BF16),
            pltpu.VMEM((2, 8, 64, 128), BF16),
            pltpu.VMEM((2, 2, 8, 2, 16, 256), BF16),
            pltpu.VMEM((2, 8, 2, 16, 256), BF16),
            pltpu.VMEM((2, 2, 16, 32, 128), BF16),
            pltpu.VMEM((2, 2, 16, 32, 128), BF16),
            pltpu.VMEM((2, 128, 128), F32),
            pltpu.VMEM((2, 16, 8, 128), F32),
            pltpu.VMEM((128, 128), F32),
            pltpu.VMEM((16, 32, 512), BF16),
            pltpu.VMEM((512, 768), BF16),
            pltpu.VMEM((4, 144, 512), BF16),
            pltpu.VMEM((4, 48, 512), F32),
            pltpu.VMEM((4, 512, 512), F32),
            pltpu.VMEM((48, 512), BF16),
            pltpu.VMEM((16, 48, 128), BF16),
            pltpu.VMEM((16, 48, 128), BF16),
            pltpu.SemaphoreType.DMA((18,)),
            pltpu.SemaphoreType.DMA((18,)),
            pltpu.SemaphoreType.DMA((6,)),
            pltpu.SemaphoreType.DMA((6,)),
            pltpu.SemaphoreType.DMA((3, 16)),
            pltpu.SemaphoreType.DMA((3, 16)),
            pltpu.SemaphoreType.DMA((15,)),
        ],
        compiler_params=pltpu.CompilerParams(
            collective_id=0, has_side_effects=True, vmem_limit_bytes=60 * 1024 * 1024
        ),
        cost_estimate=pl.CostEstimate(
            flops=6_000_000_000, bytes_accessed=15_000_000, transcendentals=3_000_000
        ),
    )(*operands)
    pair_out, tokens_out = pl.pallas_call(
        close_kernel,
        out_shape=(
            jax.ShapeDtypeStruct((1024, 128), F32),
            jax.ShapeDtypeStruct((128, 768), F32),
        ),
        in_specs=[hbm, hbm],
        out_specs=(hbm, hbm),
        scratch_shapes=[
            pltpu.VMEM((1024, 128), F32),
            pltpu.VMEM((128, 768), F32),
            pltpu.SemaphoreType.DMA((2, 4)),
            pltpu.SemaphoreType.DMA((2, 4)),
        ],
        compiler_params=pltpu.CompilerParams(vmem_limit_bytes=60 * 1024 * 1024),
    )(pair_out, tokens_out)
    return pair_out.reshape(32, 32, 128), tokens_out.reshape(4, 32, 768)


def solution(mesh):
    placed = (
        P(("group", "row"), "col", None),
        P(("group", "row"), "col"),
        P(),
        P(),
        P(),
        P(),
        P(),
        P(),
        P(("group", "row"), None, None),
        P(),
        P(None, None, "col"),
        P(),
        P(),
        P(),
        P(),
    )
    return jax.shard_map(
        on_device,
        mesh=mesh,
        in_specs=placed,
        out_specs=(P(("group", "row"), "col", None), P(("group", "row"), "col", None)),
        check_vma=False,
    )
```

```python
import jax
import jax.numpy as jnp
from jax import lax
from jax.experimental import pallas as pl
from jax.experimental.pallas import tpu as pltpu
from jax.sharding import PartitionSpec as P

EPS = 1e-05
MESH = pl.DeviceIdType.MESH
F32 = jnp.float32
BF16 = jnp.bfloat16
NT = (((1,), (1,)), ((), ()))
TN = (((0,), (0,)), ((), ()))


def normalize(value, gain):
    mean = jnp.mean(value, axis=-1, keepdims=True)
    mean_removed = value - mean
    variance = jnp.mean(mean_removed * mean_removed, axis=-1, keepdims=True)
    return mean_removed * lax.rsqrt(variance + EPS) * gain


def mm(a, b, dims=(((1,), (0,)), ((), ()))):
    return lax.dot_general(a, b, dims, preferred_element_type=F32)


def swap_matrix():
    row = lax.broadcasted_iota(jnp.int32, (512, 512), 0)
    col = lax.broadcasted_iota(jnp.int32, (512, 512), 1)
    a, b, k = row >> 7, (row >> 5) & 3, row & 31
    return jnp.where((b << 7) + (a << 5) + k == col, 1.0, 0.0).astype(BF16)


def remote(src, dst, send, recv, device):
    return pltpu.make_async_remote_copy(
        src_ref=src,
        dst_ref=dst,
        send_sem=send,
        recv_sem=recv,
        device_id=device,
        device_id_type=MESH,
    )


def loop(first, last, step):
    def body(d, carry):
        step(d)
        return carry

    lax.fori_loop(first, last, body, 0)


class Exchange:
    def __init__(self, n, me, device, src, dst, send, recv):
        self.n, self.me, self.device = n, me, device
        self.src, self.dst, self.send, self.recv = src, dst, send, recv

    def copy(self, d):
        peer = lax.rem(self.me + d, self.n)
        return remote(
            self.src(peer), self.dst(self.me), self.send.at[d], self.recv.at[d], self.device(peer)
        )

    def own(self):
        return pltpu.make_async_copy(self.src(self.me), self.dst(self.me), self.recv.at[0])


def ring(at, n):
    steps = [n // 2]
    for step in range(n // 2 - 1, 0, -1):
        steps += [step, n - step]
    return [lax.rem(at + step, n) for step in steps]


def sigmoid(value):
    return 0.5 * jnp.tanh(0.5 * value) + 0.5


class Burst:
    def __init__(self, peers, me, src, dst, all_dst, most_src, send, recv, relay=None):
        self.peers, self.me, self.relay = peers, me, relay
        self.src, self.dst, self.all_dst, self.most_src = src, dst, all_dst, most_src
        self.send, self.recv = send, recv

    def start(self):
        peers = self.peers
        if self.relay is not None:
            part, held, arrived, _, _, target = self.relay
            peer, device = peers[0]
            remote(part(self.src(peer), 1), held, self.send, arrived, target).start()
            remote(
                part(self.src(peer), 0), part(self.dst(self.me), 0), self.send, self.recv, device
            ).start()
            peers = peers[1:]
        for peer, device in peers:
            remote(self.src(peer), self.dst(self.me), self.send, self.recv, device).start()
        pltpu.make_async_copy(self.src(self.me), self.dst(self.me), self.recv).start()

    def wait(self):
        pltpu.make_async_copy(self.all_dst, self.all_dst, self.recv).wait()

    def forward(self):
        part, held, arrived, left, source, target = self.relay
        pltpu.make_async_copy(held, held, arrived).wait()
        remote(held, part(self.dst(source), 1), left, self.recv, target).start()

    def drain(self):
        pltpu.make_async_copy(self.most_src, self.most_src, self.send).wait()
        if self.relay is not None:
            _, held, _, left, _, _ = self.relay
            pltpu.make_async_copy(held, held, left).wait()


NAMES = (
    "pair",
    "mask",
    "wp",
    "wg",
    "wo",
    "gains",
    "bgain",
    "bw",
    "tokens",
    "again",
    "watt",
    "wout",
    "tgain",
    "wup",
    "wdown",
)


def block_kernel(*refs):
    inputs = dict(zip(NAMES, refs[:15]))
    out_ref, tok_ref = refs[15:17]
    held = dict(zip(NAMES, refs[17:32]))
    (
        z_s,
        gate_s,
        flat_s,
        nrm_s,
        mix_s,
        wpt_s,
        gmid_s,
        wout_s,
        mask_s,
        swap_s,
        send_z,
        recv_z,
        send_a,
        recv_a,
        send_b,
        recv_b,
        x_left,
        x_right,
        send_zt,
        recv_zt,
        send_bt,
        recv_bt,
        send_at,
        recv_at,
        heads_s,
        recv_h,
        rows_s,
        bias_s,
        xn_s,
        qkv_s,
        sig_s,
        scores_s,
        ot_s,
        send_o,
        recv_o,
        ssem,
        rsem,
        cross_ssem,
        cross_rsem,
        many_ssem,
        many_rsem,
        load_sem,
        relay_1,
        relay_2,
        relay_3,
        relay_4,
        relay_ssem,
        relay_rsem,
    ) = refs[32:]
    group, row, col = (lax.axis_index(name) for name in ("group", "row", "col"))
    big = group * 8 + row
    quad = lax.div(col, 2)
    core = lax.rem(col, 2)

    loads = {
        name: pltpu.make_async_copy(inputs[name], held[name], load_sem.at[i])
        for i, name in enumerate(NAMES)
    }
    early = ("pair", "wp", "mask", "gains", "wg")
    late = ("wo", "bgain", "bw", "tokens", "again", "watt", "wout", "tgain", "wup", "wdown")
    for name in early:
        loads[name].start()

    def on_col(peer):
        return {"col": peer}

    quad_y = lax.rem(quad, 4)
    chip_x = lax.div(quad, 4) * 2 + group
    plane_me = group * 8 + quad
    xs = [lax.rem(chip_x + d, 4) for d in range(4)]
    ys = [lax.rem(quad_y + d, 4) for d in range(4)]
    plane = []
    far = ((2, 2), (2, 1), (2, 3), (1, 2), (3, 2), (1, 1), (3, 3), (1, 3), (3, 1))
    for dx, dy in far + ((2, 0), (0, 2), (1, 0), (3, 0), (0, 1), (0, 3)):
        high, low = lax.div(xs[dx], 2), lax.rem(xs[dx], 2)
        place = high * 4 + ys[dy]
        plane.append((low * 8 + place, {"group": low, "col": place * 2 + core}))
    line = [(z, {"row": z}) for z in ring(row, 8)]
    heads = [
        (pair * 8 + place, on_col(pair * 8 + place))
        for place in ring(lax.rem(col, 8), 8) + [lax.rem(col, 8)]
        for pair in (1 - lax.div(col, 8), lax.div(col, 8))
    ][:-1]

    barrier = pltpu.get_barrier_semaphore()

    def greet(device):
        pl.semaphore_signal(barrier, inc=1, device_id=device, device_id_type=MESH)

    loop(1, 16, lambda d: greet(on_col(lax.rem(col + d, 16))))
    loop(1, 8, lambda d: greet({"row": lax.rem(row + d, 8)}))
    loop(0, 8, lambda place: greet({"group": 1 - group, "col": place * 2 + core}))

    swap_s[...] = swap_matrix()
    pair_ref = held["pair"]
    wg_ref, wo_ref = held["wg"], held["wo"]

    for name in early:
        loads[name].wait()
    for name in late:
        loads[name].start()
    gain_in = [held["gains"][m, 0:1, :] for m in range(2)]
    wpt_s[0] = held["wp"][0].T
    mask = held["mask"][...].astype(F32).astype(BF16)
    picked = []
    for lo in range(4):
        t = lax.broadcasted_iota(jnp.int32, (8, 32), 0)
        i = lax.broadcasted_iota(jnp.int32, (8, 32), 1)
        pick = jnp.where(i == t * 4 + lo, 1.0, 0.0).astype(BF16)
        k = lax.broadcasted_iota(jnp.int32, (32, 128), 0)
        lane = lax.broadcasted_iota(jnp.int32, (32, 128), 1)
        place = jnp.where(lane == lo * 32 + k, 1.0, 0.0).astype(BF16)
        picked.append(mm(mm(pick, mask).astype(BF16), place))
    mask_s[...] = picked[0] + picked[1] + picked[2] + picked[3]

    def edges(m, half, state):
        for two in range(2):
            it = half * 4 + two * 2
            z = jnp.concatenate([state(it), state(it + 1)], axis=0)
            zn = normalize(z, gain_in[m]).astype(BF16)
            proj = mm(wpt_s[m], zn, NT)
            for t in range(2):
                part = proj[:, t * 128 : (t + 1) * 128]
                keep = mask_s[it + t : it + t + 1, :]
                left = keep * sigmoid(part[0:128]) * part[128:256]
                right = keep * sigmoid(part[256:384]) * part[384:512]
                flat_s[pl.ds(two * 2 + t, 128, stride=8), :] = left
                flat_s[pl.ds(4 + two * 2 + t, 128, stride=8), :] = right
            gate_s[pl.ds(it * 128, 256), :] = sigmoid(mm(zn, wg_ref[m]))
        if half == 0:
            for z in range(8):
                rows = [flat_s[pl.ds(block * 64 + z * 8, 8), :] for block in range(16)]
                send_z[m, z] = jnp.concatenate(rows, axis=0).astype(BF16)
        else:
            for block in range(16):
                send_a[m, half, block] = flat_s[pl.ds(block * 64, 64), :].astype(BF16)

    def relay(stage, m, half):
        at = (stage - 1) * 4 + m * 2 + half
        held = ((relay_1, relay_2), (relay_3, relay_4))[stage - 1][half].at[m]
        if half == stage - 1:
            size = 64 if stage == 1 else 32

            def part(ref, k):
                return ref.at[pl.ds(k * size, size)]
        else:

            def part(ref, k):
                return ref.at[k]

        source, target = lax.rem(row + 2, 8), {"row": lax.rem(row + 6, 8)}
        return part, held, relay_rsem.at[at], relay_ssem.at[at], source, target

    def burst(stage, m, half):
        sems = ssem.at[stage * 4 + m * 2 + half], rsem.at[stage * 4 + m * 2 + half]
        if stage == 0:
            return Burst(
                plane,
                plane_me,
                lambda p: send_a.at[m, half, p],
                lambda p: recv_a.at[m, half, p],
                recv_a.at[m, half],
                send_a.at[m, half, pl.ds(0, 15)],
                *sems,
            )
        if stage == 1 and half == 0:
            return Burst(
                line,
                row,
                lambda p: send_z.at[m, p],
                lambda p: recv_z.at[m, p],
                recv_z.at[m],
                send_z.at[m, pl.ds(0, 7)],
                *sems,
                relay(stage, m, half),
            )
        if stage == 1:
            return Burst(
                line,
                row,
                lambda p: send_b.at[m, p],
                lambda p: recv_b.at[m, half, lax.div(p, 2), lax.rem(p, 2)],
                recv_b.at[m, half],
                send_b.at[m, pl.ds(0, 7)],
                *sems,
                relay(stage, m, half),
            )
        if stage == 2 and half == 1:
            return Burst(
                line,
                row,
                lambda p: send_zt.at[m, p],
                lambda p: recv_zt.at[m, p],
                recv_zt.at[m],
                send_zt.at[m, pl.ds(0, 7)],
                *sems,
                relay(stage, m, half),
            )
        if stage == 2:
            return Burst(
                line,
                row,
                lambda p: send_bt.at[m, half, p],
                lambda p: recv_bt.at[m, p],
                recv_bt.at[m],
                send_bt.at[m, half, pl.ds(0, 7)],
                *sems,
                relay(stage, m, half),
            )
        return Burst(
            plane,
            plane_me,
            lambda p: send_at.at[m, half, p],
            lambda p: recv_at.at[m, half, p],
            recv_at.at[m, half],
            send_at.at[m, half, pl.ds(0, 15)],
            *sems,
        )

    partner = on_col(quad * 2 + 1 - core)

    def cross_left(m, half):
        return remote(
            recv_b.at[m, half, :, :, :, 0],
            x_left.at[m, half],
            cross_ssem.at[m * 2 + half],
            cross_rsem.at[m * 2 + half],
            partner,
        )

    def cross_right(half):
        return remote(
            recv_b.at[0, half, :, 1 - core, :, 1],
            x_right.at[half],
            cross_ssem.at[4 + half],
            cross_rsem.at[4 + half],
            partner,
        )

    def regroup(m):
        held_z = [recv_z[m, z].astype(F32) for z in range(8)]
        for block in range(16):
            rows = [held_z[z][block * 8 : (block + 1) * 8] for z in range(8)]
            send_a[m, 0, block] = jnp.concatenate(rows, axis=0).astype(BF16)

    def to_rows(m, half):
        for hi in range(2):
            lanes = jnp.concatenate(
                [
                    jnp.concatenate(
                        [recv_a[m, half, pair * 8 + hi * 4 + lo] for lo in range(4)], axis=1
                    )
                    for pair in range(2)
                ],
                axis=0,
            )
            moved = mm(lanes, swap_s[...])
            for lo in range(4):
                mix_s[pl.ds(hi * 512 + lo, 128, stride=4), :] = moved[:, lo * 128 : (lo + 1) * 128]
        both = jnp.concatenate([mix_s[0:512, :], mix_s[512:1024, :]], axis=1)
        both = both.astype(BF16).reshape(2, 8, 2, 16, 256)
        for pair in range(2):
            if half == 0:
                recv_b[m, half, :, :, pair] = both[pair].reshape(4, 2, 2, 16, 256)
            else:
                send_b[m, :, pair] = both[pair]

    def to_channels(m, half):
        for hi in range(2):
            for pair in range(2):
                if half == 0:
                    block = recv_bt[m, :, pair, :, hi * 128 : (hi + 1) * 128]
                else:
                    block = send_bt[m, half, :, pair, :, hi * 128 : (hi + 1) * 128]
                at = hi * 256 + pair * 128
                mix_s[at : at + 128, :] = block.astype(F32).reshape(128, 128)
        for hi in range(2):
            lanes = jnp.concatenate(
                [mix_s[pl.ds(hi * 256 + lo, 64, stride=4), :] for lo in range(4)], axis=1
            )
            moved = mm(lanes.astype(BF16), swap_s[...]).astype(BF16)
            for lo in range(4):
                part = moved[:, lo * 128 : (lo + 1) * 128]
                for pair in range(2):
                    send_at[m, half, pair * 8 + hi * 4 + lo] = part[pair * 32 : pair * 32 + 32]

    def regroup_back(m):
        mix_s[0:512, :] = recv_at[m, 1].astype(F32).reshape(512, 128)
        for z in range(8):
            for t in range(4):
                mix_s[pl.ds(512 + z * 64 + t, 16, stride=4), :] = mix_s[
                    pl.ds(z * 4 + t, 16, stride=32), :
                ]
            send_zt[m, z] = mix_s[pl.ds(512 + z * 64, 64), :].astype(BF16)

    def triangle(m, gap, gap_back):
        burst(1, m, 0).forward()
        burst(0, m, 1).wait()
        to_rows(m, 1)
        burst(1, m, 1).start()
        burst(1, m, 0).wait()
        regroup(m)
        burst(0, m, 0).start()
        burst(1, m, 1).forward()
        gap()
        burst(0, m, 1).drain()

        def arrive(half):
            if half == 0:
                burst(0, m, 0).wait()
                to_rows(m, 0)
            else:
                burst(1, m, 1).wait()

        def send_back(half):
            if half == 0:
                burst(2, m, 0).start()
            else:
                to_channels(m, 1)
                burst(3, m, 1).start()

        if m == 0:
            for half in range(2):
                arrive(half)
                cross_left(m, half).start()
                cross_right(half).start()
            right = jnp.concatenate(
                [
                    recv_b[m, half, s % 4, core, s // 4, 1]
                    for s in range(8)
                    for half in range(2)
                ],
                axis=0,
            )
            own = [
                mm(recv_b[m, half, :, :, :, 0].reshape(256, 256), right, NT) for half in range(2)
            ]
            for half in range(2):
                cross_left(m, half).wait_recv()
                cross_right(half).wait_recv()
            right = jnp.concatenate(
                [x_right[half, s % 4, s // 4] for s in range(8) for half in range(2)], axis=0
            )
            for half in range(2):
                total = own[half] + mm(x_left[m, half].reshape(256, 256), right, NT)
                send_bt[m, half] = total.astype(BF16).reshape(8, 2, 16, 256)
                send_back(half)
            for half in range(2):
                cross_right(half).wait_send()
        else:
            right, own = [], None
            for half in range(2):
                arrive(half)
                cross_left(m, half).start()
                right.append(recv_b[m, half, :, :, :, 1].reshape(256, 256))
                term = mm(recv_b[m, half, :, :, :, 0].reshape(256, 256), right[half], TN)
                own = term if half == 0 else own + term
            other = None
            for half in range(2):
                cross_left(m, half).wait_recv()
                term = mm(x_left[m, half].reshape(256, 256), right[half], TN)
                other = term if half == 0 else other + term
            for half in range(2):
                for s in range(8):
                    at = slice(s * 32 + half * 16, s * 32 + half * 16 + 16)
                    z = s % 4 * 2
                    send_bt[m, half, z + core, s // 4] = own[at].astype(BF16)
                    send_bt[m, half, z + 1 - core, s // 4] = other[at].astype(BF16)
                send_back(half)
        burst(0, m, 0).drain()
        for half in range(2):
            burst(1, m, half).drain()
            cross_left(m, half).wait_send()
        burst(2, m, 0).forward()
        gap_back()
        burst(3, m, 1).wait()
        regroup_back(m)
        burst(2, m, 1).start()
        burst(2, m, 0).wait()
        to_channels(m, 0)
        burst(3, m, 0).start()
        burst(2, m, 1).forward()
        burst(2, m, 0).drain()
        burst(3, m, 1).drain()

    def middle_norm(m, half):
        if half == 0:
            burst(3, m, 0).wait()
            summed = recv_at[m, 0]
        else:
            burst(2, m, 1).wait()
            summed = recv_zt[m]
        summed = summed.astype(F32).reshape(64, 8, 128)

        def over_channels(value):
            pairs = jnp.sum(value, axis=0)
            return (pairs + pltpu.roll(pairs, 4, 0)) * (1.0 / 128)

        mean_removed = summed - over_channels(summed)[None]
        variance = over_channels(mean_removed * mean_removed)
        nrm_s[...] = (mean_removed * lax.rsqrt(variance + EPS)[None]).reshape(512, 128)

    def update(m, it):
        half = it // 4
        normed = (nrm_s[pl.ds(it % 4, 128, stride=4), :] * gmid_s[half * 2 + m]).astype(BF16)
        return gate_s[pl.ds(it * 128, 128), :] * mm(normed, wout_s[half * 2 + m], TN)

    def first_state(it):
        return pair_ref[pl.ds(it * 128, 128), :].astype(F32)

    def second_state(it):
        z = first_state(it) + update(0, it)
        z_s[pl.ds(it * 128, 128), :] = z
        return z

    def project(samples):
        weight = held["watt"][...].reshape(192, 768)
        for s in samples:
            for part in range(4):
                rows = pl.ds(s * 512 + part * 128, 128)
                value = held["tokens"][rows, :].astype(F32)
                xn_s[part * 128 : (part + 1) * 128, :] = normalize(
                    value, held["again"][...].reshape(1, 768)
                ).astype(BF16)
            proj = mm(weight, xn_s[...], NT)
            qkv_s[s] = proj[0:144].astype(BF16)
            sig_s[s] = sigmoid(proj[144:192])
            scores_s[s] = mm(qkv_s[s, 0:48, :], qkv_s[s, 48:96, :], TN) * (48.0**-0.5)

    def gap_first():
        wpt_s[1] = held["wp"][1].T
        heads_s[...] = jnp.zeros_like(heads_s)
        for name in ("wo", "bgain", "bw", "tokens", "again", "watt"):
            loads[name].wait()
        for m in range(2):
            gmid_s[m] = jnp.broadcast_to(held["gains"][m, 1:2, :], (128, 128)).T
            wout_s[m] = wo_ref[m]
            mix_s[0:128, :] = gmid_s[m]
            mix_s[128:256, :] = wo_ref[m].astype(F32)
            for z in range(8):
                rows = slice(z * 16, z * 16 + 16)
                gmid_s[2 + m, rows, :] = mix_s[pl.ds(z, 16, stride=8), :]
                wout_s[2 + m, rows, :] = mix_s[pl.ds(128 + z, 16, stride=8), :].astype(BF16)
        project((0,))

    edges(0, 0, first_state)
    pl.semaphore_wait(barrier, 30)
    burst(1, 0, 0).start()
    edges(0, 1, first_state)
    burst(0, 0, 1).start()
    triangle(0, gap_first, lambda: project((1,)))
    for half in range(2):
        middle_norm(0, half)
        edges(1, half, second_state)
        burst(1 - half, 1, half).start()
    burst(3, 0, 0).drain()
    burst(2, 0, 1).drain()

    def to_head(half):
        return Burst(
            heads,
            col,
            lambda p: heads_s.at[half, pl.ds(p * 8, 8)],
            lambda p: recv_h.at[half, p],
            recv_h.at[half],
            heads_s.at[half, pl.ds(0, 120)],
            ssem.at[16 + half],
            rsem.at[16 + half],
        )

    triangle(1, lambda: project((2,)), lambda: project((3,)))
    for half in range(2):
        middle_norm(1, half)
        for it in range(half * 4, half * 4 + 4):
            z = z_s[pl.ds(it * 128, 128), :] + update(1, it)
            out_ref[pl.ds(it * 128, 128), :] = z
            zn = normalize(z, held["bgain"][...]).astype(BF16)
            bias = mm(held["bw"][...], zn, NT).astype(BF16).astype(F32)
            heads_s[half, pl.ds(it % 4, 16, stride=8), :] = bias
        to_head(half).start()

    def along(half, offset):
        block = bias_s.at[big, pl.ds(half * 16, 16)]
        return remote(
            block,
            block,
            many_ssem.at[half, offset],
            many_rsem.at[half, offset],
            {"row": lax.rem(row + offset, 8)},
        )

    def across(half, owner, z):
        block = bias_s.at[owner * 8 + z, pl.ds(half * 16, 16)]
        return remote(
            block,
            block,
            many_ssem.at[half, 8 + z],
            many_rsem.at[half, 8 + z],
            {"group": 1 - group},
        )

    for half in range(2):
        to_head(half).wait()
        lanes = jnp.concatenate(
            [
                jnp.concatenate([recv_h[half, hi * 4 + lo] for lo in range(4)], axis=1)
                for hi in range(4)
            ],
            axis=0,
        ).astype(BF16)
        moved = mm(lanes, swap_s[...])
        for hi in range(4):
            for lo in range(4):
                rows_s[pl.ds(hi * 32 + lo, 8, stride=4), :] = moved[
                    hi * 8 : (hi + 1) * 8, lo * 128 : (lo + 1) * 128
                ]
        bias_s[big, half * 16 : (half + 1) * 16, :] = jnp.concatenate(
            [rows_s[hi * 32 : hi * 32 + 16, :] for hi in range(4)], axis=1
        ).astype(BF16)
        for offset in (4, 3, 5, 2, 6, 1, 7):
            along(half, offset).start()
        across(half, group, row).start()
    burst(3, 1, 0).drain()
    burst(2, 1, 1).drain()

    to_tokens = Exchange(
        16,
        col,
        on_col,
        lambda p: send_o.at[p],
        lambda p: recv_o.at[p],
        many_ssem.at[2],
        many_rsem.at[2],
    )

    def attend(step, carry):
        owner = lax.rem(group + step // 2, 2)
        side = lax.rem(row // 4 + step, 2)
        part = owner * 2 + side
        for lo in range(4):
            z = side * 4 + lo

            @pl.when(jnp.logical_and(step < 2, z != row))
            def _():
                for half in range(2):
                    along(half, lax.rem(row - z + 8, 8)).wait_recv()
                    across(half, owner, z).start()

            @pl.when(step >= 2)
            def _():
                for half in range(2):
                    across(half, owner, z).wait_recv()

        bias = bias_s[pl.ds(part * 4, 4)].reshape(128, 512).astype(F32)
        rows = pl.ds(pl.multiple_of(part * 128, 128), 128)
        for s in range(4):
            logits = scores_s[s, rows, :] + bias
            shifted = jnp.exp(logits - jnp.max(logits, axis=-1, keepdims=True))
            weights = shifted * (1.0 / jnp.sum(shifted, axis=-1, keepdims=True))
            mixed = mm(qkv_s[s, 96:144, :], weights.astype(BF16), NT)
            gated = mixed * sig_s[s, :, rows]
            ot_s[:, s * 128 : (s + 1) * 128] = gated.astype(BF16)
        moved = mm(ot_s[...], swap_s[...]).astype(BF16)
        for lo in range(4):
            target = part * 4 + lo
            send_o[target] = moved[:, lo * 128 : (lo + 1) * 128]

            @pl.when(target != col)
            def _():
                to_tokens.copy(lax.rem(target - col + 16, 16)).start()

            @pl.when(target == col)
            def _():
                to_tokens.own().start()

        return carry

    lax.fori_loop(0, 4, attend, 0)

    for half in range(2):
        loop(1, 8, lambda d: along(half, d).wait_send())
        loop(0, 8, lambda z: across(half, group, z).wait_send())
        to_head(half).drain()
    for name in ("wout", "tgain", "wup", "wdown"):
        loads[name].wait()
    own = [
        held["tokens"][pl.ds(pl.multiple_of(s * 512 + col * 32, 32), 32), :] for s in range(4)
    ]
    own = jnp.concatenate(own, axis=0).astype(F32)
    to_tokens.own().wait()
    loop(1, 16, lambda d: to_tokens.copy(d).wait())
    first = own + mm(recv_o[...].reshape(768, 128), held["wout"][...], TN)
    xn2 = normalize(first, held["tgain"][...].reshape(1, 768)).astype(BF16)
    total = first
    for j in range(4):
        up = mm(xn2, held["wup"][:, j * 384 : (j + 1) * 384])
        side = mm(xn2, held["wup"][:, 1536 + j * 384 : 1536 + (j + 1) * 384])
        hidden = (up * sigmoid(up) * side).astype(BF16)
        total += mm(hidden, held["wdown"][j * 384 : (j + 1) * 384, :])
    tok_ref[...] = total


def close_kernel(pair_ref, tokens_ref, pair_out, tokens_out, pair_s, tokens_s, in_sem, out_sem):
    copies = []
    for i in range(4):
        for n, (src, held, dst, size) in enumerate(
            ((pair_ref, pair_s, pair_out, 256), (tokens_ref, tokens_s, tokens_out, 32))
        ):
            rows = pl.ds(i * size, size)
            copies.append(
                (
                    pltpu.make_async_copy(src.at[rows], held.at[rows], in_sem.at[n, i]),
                    pltpu.make_async_copy(held.at[rows], dst.at[rows], out_sem.at[n, i]),
                )
            )
    for first, _ in copies:
        first.start()
    for first, second in copies:
        first.wait()
        second.start()
    for _, second in copies:
        second.wait()


def on_device(
    pair,
    pair_mask,
    tri_proj,
    tri_gate,
    triangle_output_weight,
    tri_gains,
    pair_bias_gain,
    bias_weight,
    tokens,
    att_gain,
    att_proj,
    att_out,
    tr_gain,
    tr_up,
    tr_down,
):
    operands = (
        pair.reshape(1024, 128),
        pair_mask,
        tri_proj,
        tri_gate,
        triangle_output_weight,
        tri_gains,
        pair_bias_gain.reshape(1, 128),
        jnp.swapaxes(bias_weight, 0, 1),
        tokens.reshape(2048, 768),
        att_gain,
        jnp.swapaxes(att_proj, 1, 2),
        att_out,
        tr_gain,
        tr_up,
        tr_down,
    )
    vmem = pl.BlockSpec(memory_space=pltpu.VMEM)
    hbm = pl.BlockSpec(memory_space=pl.ANY)
    pair_out, tokens_out = pl.pallas_call(
        block_kernel,
        out_shape=(
            jax.ShapeDtypeStruct((1024, 128), F32),
            jax.ShapeDtypeStruct((128, 768), F32),
        ),
        in_specs=[hbm] * 15,
        out_specs=(vmem, vmem),
        scratch_shapes=[pltpu.VMEM(x.shape, x.dtype) for x in operands]
        + [
            pltpu.VMEM((1024, 128), F32),
            pltpu.VMEM((1024, 128), F32),
            pltpu.VMEM((1024, 128), F32),
            pltpu.VMEM((512, 128), F32),
            pltpu.VMEM((1024, 128), F32),
            pltpu.VMEM((2, 512, 128), BF16),
            pltpu.VMEM((4, 128, 128), F32),
            pltpu.VMEM((4, 128, 128), BF16),
            pltpu.VMEM((8, 128), F32),
            pltpu.VMEM((512, 512), BF16),
            pltpu.VMEM((2, 8, 128, 128), BF16),
            pltpu.VMEM((2, 8, 128, 128), BF16),
            pltpu.VMEM((2, 2, 16, 64, 128), BF16),
            pltpu.VMEM((2, 2, 16, 64, 128), BF16),
            pltpu.VMEM((2, 8, 2, 2, 16, 256), BF16),
            pltpu.VMEM((2, 2, 4, 2, 2, 2, 16, 256), BF16),
            pltpu.VMEM((2, 2, 4, 2, 2, 16, 256), BF16),
            pltpu.VMEM((2, 4, 2, 16, 256), BF16),
            pltpu.VMEM((2, 8, 64, 128), BF16),
            pltpu.VMEM((2, 8, 64, 128), BF16),
            pltpu.VMEM((2, 2, 8, 2, 16, 256), BF16),
            pltpu.VMEM((2, 8, 2, 16, 256), BF16),
            pltpu.VMEM((2, 2, 16, 32, 128), BF16),
            pltpu.VMEM((2, 2, 16, 32, 128), BF16),
            pltpu.VMEM((2, 128, 128), F32),
            pltpu.VMEM((2, 16, 8, 128), F32),
            pltpu.VMEM((128, 128), F32),
            pltpu.VMEM((16, 32, 512), BF16),
            pltpu.VMEM((512, 768), BF16),
            pltpu.VMEM((4, 144, 512), BF16),
            pltpu.VMEM((4, 48, 512), F32),
            pltpu.VMEM((4, 512, 512), F32),
            pltpu.VMEM((48, 512), BF16),
            pltpu.VMEM((16, 48, 128), BF16),
            pltpu.VMEM((16, 48, 128), BF16),
            pltpu.SemaphoreType.DMA((18,)),
            pltpu.SemaphoreType.DMA((18,)),
            pltpu.SemaphoreType.DMA((6,)),
            pltpu.SemaphoreType.DMA((6,)),
            pltpu.SemaphoreType.DMA((3, 16)),
            pltpu.SemaphoreType.DMA((3, 16)),
            pltpu.SemaphoreType.DMA((15,)),
            pltpu.VMEM((2, 64, 128), BF16),
            pltpu.VMEM((2, 2, 16, 256), BF16),
            pltpu.VMEM((2, 16, 256), BF16),
            pltpu.VMEM((2, 32, 128), BF16),
            pltpu.SemaphoreType.DMA((8,)),
            pltpu.SemaphoreType.DMA((8,)),
        ],
        compiler_params=pltpu.CompilerParams(
            collective_id=0, has_side_effects=True, vmem_limit_bytes=60 * 1024 * 1024
        ),
        cost_estimate=pl.CostEstimate(
            flops=6_000_000_000, bytes_accessed=15_000_000, transcendentals=3_000_000
        ),
    )(*operands)
    pair_out, tokens_out = pl.pallas_call(
        close_kernel,
        out_shape=(
            jax.ShapeDtypeStruct((1024, 128), F32),
            jax.ShapeDtypeStruct((128, 768), F32),
        ),
        in_specs=[hbm, hbm],
        out_specs=(hbm, hbm),
        scratch_shapes=[
            pltpu.VMEM((1024, 128), F32),
            pltpu.VMEM((128, 768), F32),
            pltpu.SemaphoreType.DMA((2, 4)),
            pltpu.SemaphoreType.DMA((2, 4)),
        ],
        compiler_params=pltpu.CompilerParams(vmem_limit_bytes=60 * 1024 * 1024),
    )(pair_out, tokens_out)
    return pair_out.reshape(32, 32, 128), tokens_out.reshape(4, 32, 768)


def solution(mesh):
    placed = (
        P(("group", "row"), "col", None),
        P(("group", "row"), "col"),
        P(),
        P(),
        P(),
        P(),
        P(),
        P(),
        P(("group", "row"), None, None),
        P(),
        P(None, None, "col"),
        P(),
        P(),
        P(),
        P(),
    )
    return jax.shard_map(
        on_device,
        mesh=mesh,
        in_specs=placed,
        out_specs=(P(("group", "row"), "col", None), P(("group", "row"), "col", None)),
        check_vma=False,
    )
```

```python
import jax
import jax.numpy as jnp
from jax import lax
from jax.experimental import pallas as pl
from jax.experimental.pallas import tpu as pltpu
from jax.sharding import PartitionSpec as P

EPS = 1e-05
MESH = pl.DeviceIdType.MESH
F32 = jnp.float32
BF16 = jnp.bfloat16
NT = (((1,), (1,)), ((), ()))
TN = (((0,), (0,)), ((), ()))


def normalize(value, gain):
    mean = jnp.mean(value, axis=-1, keepdims=True)
    mean_removed = value - mean
    variance = jnp.mean(mean_removed * mean_removed, axis=-1, keepdims=True)
    return mean_removed * lax.rsqrt(variance + EPS) * gain


def mm(a, b, dims=(((1,), (0,)), ((), ()))):
    return lax.dot_general(a, b, dims, preferred_element_type=F32)


def swap_matrix():
    row = lax.broadcasted_iota(jnp.int32, (512, 512), 0)
    col = lax.broadcasted_iota(jnp.int32, (512, 512), 1)
    a, b, k = row >> 7, (row >> 5) & 3, row & 31
    return jnp.where((b << 7) + (a << 5) + k == col, 1.0, 0.0).astype(BF16)


def remote(src, dst, send, recv, device):
    return pltpu.make_async_remote_copy(
        src_ref=src,
        dst_ref=dst,
        send_sem=send,
        recv_sem=recv,
        device_id=device,
        device_id_type=MESH,
    )


def loop(first, last, step):
    def body(d, carry):
        step(d)
        return carry

    lax.fori_loop(first, last, body, 0)


class Exchange:
    def __init__(self, n, me, device, src, dst, send, recv):
        self.n, self.me, self.device = n, me, device
        self.src, self.dst, self.send, self.recv = src, dst, send, recv

    def copy(self, d):
        peer = lax.rem(self.me + d, self.n)
        return remote(
            self.src(peer), self.dst(self.me), self.send.at[d], self.recv.at[d], self.device(peer)
        )

    def own(self):
        return pltpu.make_async_copy(self.src(self.me), self.dst(self.me), self.recv.at[0])


def ring(at, n):
    steps = [n // 2]
    for step in range(n // 2 - 1, 0, -1):
        steps += [step, n - step]
    return [lax.rem(at + step, n) for step in steps]


def sigmoid(value):
    return 0.5 * jnp.tanh(0.5 * value) + 0.5


class Burst:
    def __init__(self, peers, me, src, dst, all_dst, most_src, send, recv):
        self.peers, self.me = peers, me
        self.src, self.dst, self.all_dst, self.most_src = src, dst, all_dst, most_src
        self.send, self.recv = send, recv

    def start(self):
        for peer, device in self.peers:
            remote(self.src(peer), self.dst(self.me), self.send, self.recv, device).start()
        pltpu.make_async_copy(self.src(self.me), self.dst(self.me), self.recv).start()

    def wait(self):
        pltpu.make_async_copy(self.all_dst, self.all_dst, self.recv).wait()

    def drain(self):
        pltpu.make_async_copy(self.most_src, self.most_src, self.send).wait()


NAMES = (
    "pair",
    "mask",
    "wp",
    "wg",
    "wo",
    "gains",
    "bgain",
    "bw",
    "tokens",
    "again",
    "watt",
    "wout",
    "tgain",
    "wup",
    "wdown",
)


def block_kernel(*refs):
    inputs = dict(zip(NAMES, refs[:15]))
    out_ref, tok_ref = refs[15:17]
    held = dict(zip(NAMES, refs[17:32]))
    (
        z_s,
        gate_s,
        flat_s,
        nrm_s,
        mix_s,
        wpt_s,
        gmid_s,
        wout_s,
        mask_s,
        swap_s,
        send_z,
        recv_z,
        send_a,
        recv_a,
        send_b,
        recv_b,
        x_left,
        x_right,
        send_zt,
        recv_zt,
        send_bt,
        recv_bt,
        send_at,
        recv_at,
        heads_s,
        recv_h,
        rows_s,
        bias_s,
        xn_s,
        qkv_s,
        sig_s,
        scores_s,
        ot_s,
        send_o,
        recv_o,
        ssem,
        rsem,
        cross_ssem,
        cross_rsem,
        many_ssem,
        many_rsem,
        load_sem,
        out_sem,
    ) = refs[32:]
    group, row, col = (lax.axis_index(name) for name in ("group", "row", "col"))
    big = group * 8 + row
    quad = lax.div(col, 2)
    core = lax.rem(col, 2)

    loads = {
        name: pltpu.make_async_copy(inputs[name], held[name], load_sem.at[i])
        for i, name in enumerate(NAMES)
    }
    early = ("pair", "wp", "mask", "gains", "wg")
    late = ("wo", "bgain", "bw", "tokens", "again", "watt", "wout", "tgain", "wup", "wdown")
    for name in early:
        loads[name].start()

    def on_col(peer):
        return {"col": peer}

    quad_y = lax.rem(quad, 4)
    chip_x = lax.div(quad, 4) * 2 + group
    plane_me = group * 8 + quad
    xs = [lax.rem(chip_x + d, 4) for d in range(4)]
    ys = [lax.rem(quad_y + d, 4) for d in range(4)]
    plane = []
    far = ((2, 2), (2, 1), (2, 3), (1, 2), (3, 2), (1, 1), (3, 3), (1, 3), (3, 1))
    for dx, dy in far + ((2, 0), (0, 2), (1, 0), (3, 0), (0, 1), (0, 3)):
        high, low = lax.div(xs[dx], 2), lax.rem(xs[dx], 2)
        place = high * 4 + ys[dy]
        plane.append((low * 8 + place, {"group": low, "col": place * 2 + core}))
    line = [(z, {"row": z}) for z in ring(row, 8)]
    heads = [
        (pair * 8 + place, on_col(pair * 8 + place))
        for place in ring(lax.rem(col, 8), 8) + [lax.rem(col, 8)]
        for pair in (1 - lax.div(col, 8), lax.div(col, 8))
    ][:-1]

    barrier = pltpu.get_barrier_semaphore()

    def greet(device):
        pl.semaphore_signal(barrier, inc=1, device_id=device, device_id_type=MESH)

    loop(1, 16, lambda d: greet(on_col(lax.rem(col + d, 16))))
    loop(1, 8, lambda d: greet({"row": lax.rem(row + d, 8)}))
    loop(0, 8, lambda place: greet({"group": 1 - group, "col": place * 2 + core}))

    swap_s[...] = swap_matrix()
    pair_ref = held["pair"]
    wg_ref, wo_ref = held["wg"], held["wo"]

    for name in early:
        loads[name].wait()
    for name in late:
        loads[name].start()
    gain_in = [held["gains"][m, 0:1, :] for m in range(2)]
    wpt_s[0] = held["wp"][0].T
    mask = held["mask"][...].astype(F32).astype(BF16)
    picked = []
    for lo in range(4):
        t = lax.broadcasted_iota(jnp.int32, (8, 32), 0)
        i = lax.broadcasted_iota(jnp.int32, (8, 32), 1)
        pick = jnp.where(i == t * 4 + lo, 1.0, 0.0).astype(BF16)
        k = lax.broadcasted_iota(jnp.int32, (32, 128), 0)
        lane = lax.broadcasted_iota(jnp.int32, (32, 128), 1)
        place = jnp.where(lane == lo * 32 + k, 1.0, 0.0).astype(BF16)
        picked.append(mm(mm(pick, mask).astype(BF16), place))
    mask_s[...] = picked[0] + picked[1] + picked[2] + picked[3]

    def edges(m, half, state):
        for two in range(2):
            it = half * 4 + two * 2
            z = jnp.concatenate([state(it), state(it + 1)], axis=0)
            zn = normalize(z, gain_in[m]).astype(BF16)
            proj = mm(wpt_s[m], zn, NT)
            for t in range(2):
                part = proj[:, t * 128 : (t + 1) * 128]
                keep = mask_s[it + t : it + t + 1, :]
                left = keep * sigmoid(part[0:128]) * part[128:256]
                right = keep * sigmoid(part[256:384]) * part[384:512]
                flat_s[pl.ds(two * 2 + t, 128, stride=8), :] = left
                flat_s[pl.ds(4 + two * 2 + t, 128, stride=8), :] = right
            gate_s[pl.ds(it * 128, 256), :] = sigmoid(mm(zn, wg_ref[m]))
        if half == 0:
            for z in range(8):
                rows = [flat_s[pl.ds(block * 64 + z * 8, 8), :] for block in range(16)]
                send_z[m, z] = jnp.concatenate(rows, axis=0).astype(BF16)
        else:
            for block in range(16):
                send_a[m, half, block] = flat_s[pl.ds(block * 64, 64), :].astype(BF16)

    def burst(stage, m, half):
        sems = ssem.at[stage * 4 + m * 2 + half], rsem.at[stage * 4 + m * 2 + half]
        if stage == 0:
            return Burst(
                plane,
                plane_me,
                lambda p: send_a.at[m, half, p],
                lambda p: recv_a.at[m, half, p],
                recv_a.at[m, half],
                send_a.at[m, half, pl.ds(0, 15)],
                *sems,
            )
        if stage == 1 and half == 0:
            return Burst(
                line,
                row,
                lambda p: send_z.at[m, p],
                lambda p: recv_z.at[m, p],
                recv_z.at[m],
                send_z.at[m, pl.ds(0, 7)],
                *sems,
            )
        if stage == 1:
            return Burst(
                line,
                row,
                lambda p: send_b.at[m, p],
                lambda p: recv_b.at[m, half, lax.div(p, 2), lax.rem(p, 2)],
                recv_b.at[m, half],
                send_b.at[m, pl.ds(0, 7)],
                *sems,
            )
        if stage == 2 and half == 1:
            return Burst(
                line,
                row,
                lambda p: send_zt.at[m, p],
                lambda p: recv_zt.at[m, p],
                recv_zt.at[m],
                send_zt.at[m, pl.ds(0, 7)],
                *sems,
            )
        if stage == 2:
            return Burst(
                line,
                row,
                lambda p: send_bt.at[m, half, p],
                lambda p: recv_bt.at[m, p],
                recv_bt.at[m],
                send_bt.at[m, half, pl.ds(0, 7)],
                *sems,
            )
        return Burst(
            plane,
            plane_me,
            lambda p: send_at.at[m, half, p],
            lambda p: recv_at.at[m, half, p],
            recv_at.at[m, half],
            send_at.at[m, half, pl.ds(0, 15)],
            *sems,
        )

    partner = on_col(quad * 2 + 1 - core)

    def cross_left(m, half):
        return remote(
            recv_b.at[m, half, :, :, :, 0],
            x_left.at[m, half],
            cross_ssem.at[m * 2 + half],
            cross_rsem.at[m * 2 + half],
            partner,
        )

    def cross_right(half):
        return remote(
            recv_b.at[0, half, :, 1 - core, :, 1],
            x_right.at[half],
            cross_ssem.at[4 + half],
            cross_rsem.at[4 + half],
            partner,
        )

    def regroup(m):
        held_z = [recv_z[m, z].astype(F32) for z in range(8)]
        for block in range(16):
            rows = [held_z[z][block * 8 : (block + 1) * 8] for z in range(8)]
            send_a[m, 0, block] = jnp.concatenate(rows, axis=0).astype(BF16)

    def to_rows(m, half):
        for hi in range(2):
            lanes = jnp.concatenate(
                [
                    jnp.concatenate(
                        [recv_a[m, half, pair * 8 + hi * 4 + lo] for lo in range(4)], axis=1
                    )
                    for pair in range(2)
                ],
                axis=0,
            )
            moved = mm(lanes, swap_s[...])
            for lo in range(4):
                mix_s[pl.ds(hi * 512 + lo, 128, stride=4), :] = moved[:, lo * 128 : (lo + 1) * 128]
        both = jnp.concatenate([mix_s[0:512, :], mix_s[512:1024, :]], axis=1)
        both = both.astype(BF16).reshape(2, 8, 2, 16, 256)
        for pair in range(2):
            if half == 0:
                recv_b[m, half, :, :, pair] = both[pair].reshape(4, 2, 2, 16, 256)
            else:
                send_b[m, :, pair] = both[pair]

    def to_channels(m, half):
        for hi in range(2):
            for pair in range(2):
                if half == 0:
                    block = recv_bt[m, :, pair, :, hi * 128 : (hi + 1) * 128]
                else:
                    block = send_bt[m, half, :, pair, :, hi * 128 : (hi + 1) * 128]
                at = hi * 256 + pair * 128
                mix_s[at : at + 128, :] = block.astype(F32).reshape(128, 128)
        for hi in range(2):
            lanes = jnp.concatenate(
                [mix_s[pl.ds(hi * 256 + lo, 64, stride=4), :] for lo in range(4)], axis=1
            )
            moved = mm(lanes.astype(BF16), swap_s[...]).astype(BF16)
            for lo in range(4):
                part = moved[:, lo * 128 : (lo + 1) * 128]
                for pair in range(2):
                    send_at[m, half, pair * 8 + hi * 4 + lo] = part[pair * 32 : pair * 32 + 32]

    def regroup_back(m):
        mix_s[0:512, :] = recv_at[m, 1].astype(F32).reshape(512, 128)
        for z in range(8):
            for t in range(4):
                mix_s[pl.ds(512 + z * 64 + t, 16, stride=4), :] = mix_s[
                    pl.ds(z * 4 + t, 16, stride=32), :
                ]
            send_zt[m, z] = mix_s[pl.ds(512 + z * 64, 64), :].astype(BF16)

    def triangle(m, gap):
        burst(0, m, 1).wait()
        to_rows(m, 1)
        burst(1, m, 1).start()
        burst(1, m, 0).wait()
        regroup(m)
        burst(0, m, 0).start()
        gap()
        burst(0, m, 1).drain()

        def arrive(half):
            if half == 0:
                burst(0, m, 0).wait()
                to_rows(m, 0)
            else:
                burst(1, m, 1).wait()

        def send_back(half):
            if half == 0:
                burst(2, m, 0).start()
            else:
                to_channels(m, 1)
                burst(3, m, 1).start()

        if m == 0:
            for half in range(2):
                arrive(half)
                cross_right(half).start()
                cross_left(m, half).start()
            right = jnp.concatenate(
                [
                    recv_b[m, half, s % 4, core, s // 4, 1]
                    for s in range(8)
                    for half in range(2)
                ],
                axis=0,
            )
            own = [
                mm(recv_b[m, half, :, :, :, 0].reshape(256, 256), right, NT) for half in range(2)
            ]
            for half in range(2):
                cross_right(half).wait_recv()
            right = jnp.concatenate(
                [x_right[half, s % 4, s // 4] for s in range(8) for half in range(2)], axis=0
            )
            for half in range(2):
                cross_left(m, half).wait_recv()
                total = own[half] + mm(x_left[m, half].reshape(256, 256), right, NT)
                send_bt[m, half] = total.astype(BF16).reshape(8, 2, 16, 256)
                send_back(half)
            for half in range(2):
                cross_right(half).wait_send()
        else:
            right, own = [], None
            for half in range(2):
                arrive(half)
                cross_left(m, half).start()
                right.append(recv_b[m, half, :, :, :, 1].reshape(256, 256))
                term = mm(recv_b[m, half, :, :, :, 0].reshape(256, 256), right[half], TN)
                own = term if half == 0 else own + term
            other = None
            for half in range(2):
                cross_left(m, half).wait_recv()
                term = mm(x_left[m, half].reshape(256, 256), right[half], TN)
                other = term if half == 0 else other + term
            for half in range(2):
                for s in range(8):
                    at = slice(s * 32 + half * 16, s * 32 + half * 16 + 16)
                    z = s % 4 * 2
                    send_bt[m, half, z + core, s // 4] = own[at].astype(BF16)
                    send_bt[m, half, z + 1 - core, s // 4] = other[at].astype(BF16)
                send_back(half)
        burst(0, m, 0).drain()
        for half in range(2):
            burst(1, m, half).drain()
            cross_left(m, half).wait_send()
        burst(3, m, 1).wait()
        regroup_back(m)
        burst(2, m, 1).start()
        burst(2, m, 0).wait()
        to_channels(m, 0)
        burst(3, m, 0).start()
        burst(2, m, 0).drain()
        burst(3, m, 1).drain()

    def middle_norm(m, half):
        if half == 0:
            burst(3, m, 0).wait()
            summed = recv_at[m, 0]
        else:
            burst(2, m, 1).wait()
            summed = recv_zt[m]
        summed = summed.astype(F32).reshape(64, 8, 128)

        def over_channels(value):
            pairs = jnp.sum(value, axis=0)
            return (pairs + pltpu.roll(pairs, 4, 0)) * (1.0 / 128)

        mean_removed = summed - over_channels(summed)[None]
        variance = over_channels(mean_removed * mean_removed)
        nrm_s[...] = (mean_removed * lax.rsqrt(variance + EPS)[None]).reshape(512, 128)

    def update(m, it):
        half = it // 4
        normed = (nrm_s[pl.ds(it % 4, 128, stride=4), :] * gmid_s[half * 2 + m]).astype(BF16)
        return gate_s[pl.ds(it * 128, 128), :] * mm(normed, wout_s[half * 2 + m], TN)

    def first_state(it):
        return pair_ref[pl.ds(it * 128, 128), :].astype(F32)

    def second_state(it):
        z = first_state(it) + update(0, it)
        z_s[pl.ds(it * 128, 128), :] = z
        return z

    def project(samples):
        weight = held["watt"][...].reshape(192, 768)
        for s in samples:
            for part in range(4):
                rows = pl.ds(s * 512 + part * 128, 128)
                value = held["tokens"][rows, :].astype(F32)
                xn_s[part * 128 : (part + 1) * 128, :] = normalize(
                    value, held["again"][...].reshape(1, 768)
                ).astype(BF16)
            proj = mm(weight, xn_s[...], NT)
            qkv_s[s] = proj[0:144].astype(BF16)
            sig_s[s] = sigmoid(proj[144:192])
            scores_s[s] = mm(qkv_s[s, 0:48, :], qkv_s[s, 48:96, :], TN) * (48.0**-0.5)

    def gap_first():
        wpt_s[1] = held["wp"][1].T
        heads_s[...] = jnp.zeros_like(heads_s)
        for name in ("wo", "bgain", "bw", "tokens", "again", "watt"):
            loads[name].wait()
        for m in range(2):
            gmid_s[m] = jnp.broadcast_to(held["gains"][m, 1:2, :], (128, 128)).T
            wout_s[m] = wo_ref[m]
            mix_s[0:128, :] = gmid_s[m]
            mix_s[128:256, :] = wo_ref[m].astype(F32)
            for z in range(8):
                rows = slice(z * 16, z * 16 + 16)
                gmid_s[2 + m, rows, :] = mix_s[pl.ds(z, 16, stride=8), :]
                wout_s[2 + m, rows, :] = mix_s[pl.ds(128 + z, 16, stride=8), :].astype(BF16)
        project((0, 1))

    edges(0, 0, first_state)
    pl.semaphore_wait(barrier, 30)
    burst(1, 0, 0).start()
    edges(0, 1, first_state)
    burst(0, 0, 1).start()
    triangle(0, gap_first)
    for half in range(2):
        middle_norm(0, half)
        edges(1, half, second_state)
        burst(1 - half, 1, half).start()
    burst(3, 0, 0).drain()
    burst(2, 0, 1).drain()

    def write_pair(half):
        rows = pl.ds(half * 512, 512)
        return pltpu.make_async_copy(z_s.at[rows], out_ref.at[rows], out_sem.at[half])

    def to_head(half):
        return Burst(
            heads,
            col,
            lambda p: heads_s.at[half, pl.ds(p * 8, 8)],
            lambda p: recv_h.at[half, p],
            recv_h.at[half],
            heads_s.at[half, pl.ds(0, 120)],
            ssem.at[16 + half],
            rsem.at[16 + half],
        )

    triangle(1, lambda: project((2, 3)))
    for half in range(2):
        middle_norm(1, half)
        for it in range(half * 4, half * 4 + 4):
            z = z_s[pl.ds(it * 128, 128), :] + update(1, it)
            z_s[pl.ds(it * 128, 128), :] = z
            zn = normalize(z, held["bgain"][...]).astype(BF16)
            bias = mm(held["bw"][...], zn, NT).astype(BF16).astype(F32)
            heads_s[half, pl.ds(it % 4, 16, stride=8), :] = bias
        to_head(half).start()
        write_pair(half).start()

    def along(half, offset):
        block = bias_s.at[big, pl.ds(half * 16, 16)]
        return remote(
            block,
            block,
            many_ssem.at[half, offset],
            many_rsem.at[half, offset],
            {"row": lax.rem(row + offset, 8)},
        )

    def across(half, owner, z):
        block = bias_s.at[owner * 8 + z, pl.ds(half * 16, 16)]
        return remote(
            block,
            block,
            many_ssem.at[half, 8 + z],
            many_rsem.at[half, 8 + z],
            {"group": 1 - group},
        )

    for half in range(2):
        to_head(half).wait()
        lanes = jnp.concatenate(
            [
                jnp.concatenate([recv_h[half, hi * 4 + lo] for lo in range(4)], axis=1)
                for hi in range(4)
            ],
            axis=0,
        ).astype(BF16)
        moved = mm(lanes, swap_s[...])
        for hi in range(4):
            for lo in range(4):
                rows_s[pl.ds(hi * 32 + lo, 8, stride=4), :] = moved[
                    hi * 8 : (hi + 1) * 8, lo * 128 : (lo + 1) * 128
                ]
        bias_s[big, half * 16 : (half + 1) * 16, :] = jnp.concatenate(
            [rows_s[hi * 32 : hi * 32 + 16, :] for hi in range(4)], axis=1
        ).astype(BF16)
        for offset in (4, 3, 5, 2, 6, 1, 7):
            along(half, offset).start()
        across(half, group, row).start()
    burst(3, 1, 0).drain()
    burst(2, 1, 1).drain()

    to_tokens = Exchange(
        16,
        col,
        on_col,
        lambda p: send_o.at[p],
        lambda p: recv_o.at[p],
        many_ssem.at[2],
        many_rsem.at[2],
    )

    def attend(step, carry):
        owner = lax.rem(group + step // 2, 2)
        side = lax.rem(row // 4 + step, 2)
        part = owner * 2 + side
        for lo in range(4):
            z = side * 4 + lo

            @pl.when(jnp.logical_and(step < 2, z != row))
            def _():
                for half in range(2):
                    along(half, lax.rem(row - z + 8, 8)).wait_recv()
                    across(half, owner, z).start()

            @pl.when(step >= 2)
            def _():
                for half in range(2):
                    across(half, owner, z).wait_recv()

        bias = bias_s[pl.ds(part * 4, 4)].reshape(128, 512).astype(F32)
        rows = pl.ds(pl.multiple_of(part * 128, 128), 128)
        for s in range(4):
            logits = scores_s[s, rows, :] + bias
            shifted = jnp.exp(logits - jnp.max(logits, axis=-1, keepdims=True))
            weights = shifted * (1.0 / jnp.sum(shifted, axis=-1, keepdims=True))
            mixed = mm(qkv_s[s, 96:144, :], weights.astype(BF16), NT)
            gated = mixed * sig_s[s, :, rows]
            ot_s[:, s * 128 : (s + 1) * 128] = gated.astype(BF16)
        moved = mm(ot_s[...], swap_s[...]).astype(BF16)
        for lo in range(4):
            target = part * 4 + lo
            send_o[target] = moved[:, lo * 128 : (lo + 1) * 128]

            @pl.when(target != col)
            def _():
                to_tokens.copy(lax.rem(target - col + 16, 16)).start()

            @pl.when(target == col)
            def _():
                to_tokens.own().start()

        return carry

    lax.fori_loop(0, 4, attend, 0)

    for half in range(2):
        loop(1, 8, lambda d: along(half, d).wait_send())
        loop(0, 8, lambda z: across(half, group, z).wait_send())
        to_head(half).drain()
    for name in ("wout", "tgain", "wup", "wdown"):
        loads[name].wait()
    own = [
        held["tokens"][pl.ds(pl.multiple_of(s * 512 + col * 32, 32), 32), :] for s in range(4)
    ]
    own = jnp.concatenate(own, axis=0).astype(F32)
    to_tokens.own().wait()
    loop(1, 16, lambda d: to_tokens.copy(d).wait())
    first = own + mm(recv_o[...].reshape(768, 128), held["wout"][...], TN)
    xn2 = normalize(first, held["tgain"][...].reshape(1, 768)).astype(BF16)
    total = first
    for j in range(3):
        up = mm(xn2, held["wup"][:, j * 512 : (j + 1) * 512])
        side = mm(xn2, held["wup"][:, 1536 + j * 512 : 1536 + (j + 1) * 512])
        hidden = (up * sigmoid(up) * side).astype(BF16)
        total += mm(hidden, held["wdown"][j * 512 : (j + 1) * 512, :])
    tok_ref[...] = total
    for half in range(2):
        write_pair(half).wait()


def close_kernel(pair_ref, tokens_ref, pair_out, tokens_out, pair_s, tokens_s, in_sem, out_sem):
    copies = []
    for i in range(4):
        for n, (src, held, dst, size) in enumerate(
            ((pair_ref, pair_s, pair_out, 256), (tokens_ref, tokens_s, tokens_out, 32))
        ):
            rows = pl.ds(i * size, size)
            copies.append(
                (
                    pltpu.make_async_copy(src.at[rows], held.at[rows], in_sem.at[n, i]),
                    pltpu.make_async_copy(held.at[rows], dst.at[rows], out_sem.at[n, i]),
                )
            )
    for first, _ in copies:
        first.start()
    for first, second in copies:
        first.wait()
        second.start()
    for _, second in copies:
        second.wait()


def on_device(
    pair,
    pair_mask,
    tri_proj,
    tri_gate,
    triangle_output_weight,
    tri_gains,
    pair_bias_gain,
    bias_weight,
    tokens,
    att_gain,
    att_proj,
    att_out,
    tr_gain,
    tr_up,
    tr_down,
):
    operands = (
        pair.reshape(1024, 128),
        pair_mask,
        tri_proj,
        tri_gate,
        triangle_output_weight,
        tri_gains,
        pair_bias_gain.reshape(1, 128),
        jnp.swapaxes(bias_weight, 0, 1),
        tokens.reshape(2048, 768),
        att_gain,
        jnp.swapaxes(att_proj, 1, 2),
        att_out,
        tr_gain,
        tr_up,
        tr_down,
    )
    vmem = pl.BlockSpec(memory_space=pltpu.VMEM)
    hbm = pl.BlockSpec(memory_space=pl.ANY)
    pair_out, tokens_out = pl.pallas_call(
        block_kernel,
        out_shape=(
            jax.ShapeDtypeStruct((1024, 128), F32),
            jax.ShapeDtypeStruct((128, 768), F32),
        ),
        in_specs=[hbm] * 15,
        out_specs=(hbm, vmem),
        scratch_shapes=[pltpu.VMEM(x.shape, x.dtype) for x in operands]
        + [
            pltpu.VMEM((1024, 128), F32),
            pltpu.VMEM((1024, 128), F32),
            pltpu.VMEM((1024, 128), F32),
            pltpu.VMEM((512, 128), F32),
            pltpu.VMEM((1024, 128), F32),
            pltpu.VMEM((2, 512, 128), BF16),
            pltpu.VMEM((4, 128, 128), F32),
            pltpu.VMEM((4, 128, 128), BF16),
            pltpu.VMEM((8, 128), F32),
            pltpu.VMEM((512, 512), BF16),
            pltpu.VMEM((2, 8, 128, 128), BF16),
            pltpu.VMEM((2, 8, 128, 128), BF16),
            pltpu.VMEM((2, 2, 16, 64, 128), BF16),
            pltpu.VMEM((2, 2, 16, 64, 128), BF16),
            pltpu.VMEM((2, 8, 2, 2, 16, 256), BF16),
            pltpu.VMEM((2, 2, 4, 2, 2, 2, 16, 256), BF16),
            pltpu.VMEM((2, 2, 4, 2, 2, 16, 256), BF16),
            pltpu.VMEM((2, 4, 2, 16, 256), BF16),
            pltpu.VMEM((2, 8, 64, 128), BF16),
            pltpu.VMEM((2, 8, 64, 128), BF16),
            pltpu.VMEM((2, 2, 8, 2, 16, 256), BF16),
            pltpu.VMEM((2, 8, 2, 16, 256), BF16),
            pltpu.VMEM((2, 2, 16, 32, 128), BF16),
            pltpu.VMEM((2, 2, 16, 32, 128), BF16),
            pltpu.VMEM((2, 128, 128), F32),
            pltpu.VMEM((2, 16, 8, 128), F32),
            pltpu.VMEM((128, 128), F32),
            pltpu.VMEM((16, 32, 512), BF16),
            pltpu.VMEM((512, 768), BF16),
            pltpu.VMEM((4, 144, 512), BF16),
            pltpu.VMEM((4, 48, 512), F32),
            pltpu.VMEM((4, 512, 512), F32),
            pltpu.VMEM((48, 512), BF16),
            pltpu.VMEM((16, 48, 128), BF16),
            pltpu.VMEM((16, 48, 128), BF16),
            pltpu.SemaphoreType.DMA((18,)),
            pltpu.SemaphoreType.DMA((18,)),
            pltpu.SemaphoreType.DMA((6,)),
            pltpu.SemaphoreType.DMA((6,)),
            pltpu.SemaphoreType.DMA((3, 16)),
            pltpu.SemaphoreType.DMA((3, 16)),
            pltpu.SemaphoreType.DMA((15,)),
            pltpu.SemaphoreType.DMA((2,)),
        ],
        compiler_params=pltpu.CompilerParams(
            collective_id=0, has_side_effects=True, vmem_limit_bytes=60 * 1024 * 1024
        ),
        cost_estimate=pl.CostEstimate(
            flops=6_000_000_000, bytes_accessed=15_000_000, transcendentals=3_000_000
        ),
    )(*operands)
    pair_out, tokens_out = pl.pallas_call(
        close_kernel,
        out_shape=(
            jax.ShapeDtypeStruct((1024, 128), F32),
            jax.ShapeDtypeStruct((128, 768), F32),
        ),
        in_specs=[hbm, hbm],
        out_specs=(hbm, hbm),
        scratch_shapes=[
            pltpu.VMEM((1024, 128), F32),
            pltpu.VMEM((128, 768), F32),
            pltpu.SemaphoreType.DMA((2, 4)),
            pltpu.SemaphoreType.DMA((2, 4)),
        ],
        compiler_params=pltpu.CompilerParams(vmem_limit_bytes=60 * 1024 * 1024),
    )(pair_out, tokens_out)
    return pair_out.reshape(32, 32, 128), tokens_out.reshape(4, 32, 768)


def solution(mesh):
    placed = (
        P(("group", "row"), "col", None),
        P(("group", "row"), "col"),
        P(),
        P(),
        P(),
        P(),
        P(),
        P(),
        P(("group", "row"), None, None),
        P(),
        P(None, None, "col"),
        P(),
        P(),
        P(),
        P(),
    )
    return jax.shard_map(
        on_device,
        mesh=mesh,
        in_specs=placed,
        out_specs=(P(("group", "row"), "col", None), P(("group", "row"), "col", None)),
        check_vma=False,
    )
```
